32 devices in a mesh: ctx: 4 (over y, x), fsdp: 8 (over z, core).
Axes of the slice: x: 2, y: 2, z: 4, core: 2. Of those that a mesh axis runs over, the one named last changes fastest.
Arguments:
- tokens: bfloat16 [8, 2048, 1152], P('fsdp', 'ctx'), may hold values from -6 to 6
- table: int32 [4, 2], replicated, may hold values from 0 to 7, as said below
- norm1_gain: bfloat16 [1152], P('fsdp'), may hold values from 0.5 to 1.5
- w_query: bfloat16 [1152, 1152], P('fsdp'), may hold values from -0.1875 to 0.1875
- w_key: bfloat16 [1152, 384], P('fsdp'), may hold values from -0.1875 to 0.1875
- w_value: bfloat16 [1152, 384], P('fsdp'), may hold values from -0.1875 to 0.1875
- w_out: bfloat16 [1152, 1152], P('fsdp'), may hold values from -6 to 6
- norm2_gain: bfloat16 [1152], P('fsdp'), may hold values from 0.5 to 1.5
- w_gate: bfloat16 [1152, 3072], P('fsdp'), may hold values from -0.1875 to 0.1875
- w_up: bfloat16 [1152, 3072], P('fsdp'), may hold values from -0.1875 to 0.1875
- w_down: bfloat16 [3072, 1152], P('fsdp'), may hold values from -0.109375 to 0.109375
- cotangent: bfloat16 [8, 2048, 1152], P('fsdp', 'ctx'), may hold values from -6 to 6
Outputs:
- output: bfloat16 [8, 2048, 1152], P('fsdp', 'ctx')
- grad_tokens: bfloat16 [8, 2048, 1152], P('fsdp', 'ctx')
- grad_norm1: float32 [1152], P('fsdp')
- grad_query: float32 [1152, 1152], P('fsdp')
- grad_key: float32 [1152, 384], P('fsdp')
- grad_value: float32 [1152, 384], P('fsdp')
- grad_out: float32 [1152, 1152], P('fsdp')
- grad_norm2: float32 [1152], P('fsdp')
- grad_gate: float32 [1152, 3072], P('fsdp')
- grad_up: float32 [1152, 3072], P('fsdp')
- grad_down: float32 [3072, 1152], P('fsdp')
The draws below stay inside these ranges and needn't reach their ends.
Inputs may be any that keep to these rules, and one draw needn't show every extreme that they name: `table`: row c lists the 2 blocks of context device c; every block 0 to 7 stands once, and each row is made of consecutive pairs b, 7 - b.
All inputs are finite; a program needn't handle non-finite values.
Results may differ from the reference program's by a relative error of at most 0.022.
Values may be sent and summed in bfloat16 or wider, within the bound.
No kernel may reach another device: no remote copies, remote signals or barrier semaphores. Data moves between devices by JAX's collectives and lax.ppermute only.
A program may use at most 320 MiB of HBM per device.

```python
import math
import jax
import jax.numpy as jnp
from jax import lax

D = 1152
H = 18
KVH = 6
HD = 64
FF = 3072
BLK = 256
BLK_DEV = 2
NBLK = 8
SEQ = 2048
SEQS = 8


def draw_table(key, part):
    key = jax.random.fold_in(key, 11)
    pair_key, flip_key = jax.random.split(key)
    devices = NBLK // BLK_DEV
    pair_order = jax.random.permutation(pair_key, NBLK // 2).reshape(devices, BLK_DEV // 2)
    flip_bits = jax.random.randint(flip_key, (devices, BLK_DEV // 2), 0, 2)
    lead_block = jnp.where(flip_bits == 1, NBLK - 1 - pair_order, pair_order)
    second = NBLK - 1 - lead_block
    return jnp.stack([lead_block, second], axis=-1).reshape(devices, BLK_DEV).astype(jnp.int32)


def levels(rng, dims, shards, least, high):
    loudness, own = 1.0, jax.random.fold_in(rng, 6)
    for position, parts in shards:
        heights = jnp.exp(jax.random.uniform(jax.random.fold_in(own, position), (parts,), jnp.float32, least / len(shards), high / len(shards)))
        loudness = loudness * jnp.repeat(heights, dims[position] // parts).reshape([-1 if axis == position else 1 for axis in range(len(dims))])
    return loudness


def gaussian(rng, dims, spread, reach, pieces=(), kind=jnp.bfloat16):
    values = spread * jax.random.normal(rng, dims, jnp.float32)
    if pieces:
        values = values * levels(rng, dims, pieces, -0.22, 0.18)
    return jnp.clip(values, -reach, reach).astype(kind)


def setup_inputs(seed: int = 0) -> dict:
    splits = jax.random.split(jax.random.key(seed), 13)
    return {
        "tokens": gaussian(splits[0], (SEQS, SEQ, D), 1.0, 6.0, ((0, 8), (1, 4))),
        "table": draw_table(jax.random.fold_in(splits[12], 71), 0),
        "norm1_gain": jnp.clip(1.0 + 0.1 * jax.random.normal(splits[2], (D,), jnp.float32), 0.5, 1.5).astype(jnp.bfloat16),
        "w_query": gaussian(splits[3], (D, H * HD), D ** -0.5, 0.1875, ((0, 8),)),
        "w_key": gaussian(splits[4], (D, KVH * HD), D ** -0.5, 0.1875, ((0, 8),)),
        "w_value": gaussian(splits[5], (D, KVH * HD), D ** -0.5, 0.1875, ((0, 8),)),
        "w_out": gaussian(splits[6], (H * HD, D), (max(1, H * HD // 1024)) ** -0.5, 6.0, ((0, 8),)),
        "norm2_gain": jnp.clip(1.0 + 0.1 * jax.random.normal(splits[7], (D,), jnp.float32), 0.5, 1.5).astype(jnp.bfloat16),
        "w_gate": gaussian(splits[8], (D, FF), D ** -0.5, 0.1875, ((0, 8),)),
        "w_up": gaussian(splits[9], (D, FF), D ** -0.5, 0.1875, ((0, 8),)),
        "w_down": gaussian(splits[10], (FF, D), FF ** -0.5, 0.109375, ((0, 8),)),
        "cotangent": gaussian(splits[11], (SEQS, SEQ, D), 1.0, 6.0, ((0, 8), (1, 4))),
    }


EPS = 1e-05

@jax.custom_vjp
def low(v):
    return lax.optimization_barrier(v.astype(jnp.bfloat16)).astype(jnp.float32)

@jax.custom_vjp
def low_back(v):
    return v

def low_keep(v):
    return (low(v), None)

def low_pass(kept, grad):
    return (grad,)

def back_keep(v):
    return (v, None)

def back_low(kept, grad):
    return (low(grad),)
low.defvjp(low_keep, low_pass)
low_back.defvjp(back_keep, back_low)

def matmul(left, right):
    return jnp.dot(left, right, precision=lax.Precision.HIGHEST, preferred_element_type=jnp.float32)

def rms_scale(values, gain):
    return values * lax.rsqrt(lax.optimization_barrier(jnp.mean(values * values, -1, keepdims=True)) + EPS) * gain

def rotate(values, places, count):
    split = HD // 2
    shaped = values.reshape(values.shape[0], count, HD)
    frequency = 10000.0 ** (-(jnp.arange(split, dtype=jnp.float32) * 2.0 / HD))
    angles = places.astype(jnp.float32)[:, None] * frequency
    cosine = jnp.cos(angles)[:, None, :]
    sine = jnp.sin(angles)[:, None, :]
    first_half = shaped[..., :split]
    second_half = shaped[..., split:]
    turned = jnp.concatenate([first_half * cosine - second_half * sine, second_half * cosine + first_half * sine], -1)
    return turned.reshape(values.shape[0], count * HD)

def attend(query_rot, key_rot, values, block_ids):
    ratio = H // KVH
    rows = math.gcd(SEQ, 512)
    key_heads = jnp.repeat(key_rot.reshape(SEQ, KVH, HD), ratio, axis=1)
    value_heads = jnp.repeat(values.reshape(SEQ, KVH, HD), ratio, axis=1)
    scale = HD ** (-0.5)

    def one_block(inputs):
        query_block, query_ids = inputs
        raw = jnp.einsum('qhd,khd->hqk', query_block, key_heads, precision=lax.Precision.HIGHEST) * scale
        scores = low_back(raw)
        visible = block_ids[None, :] <= query_ids[:, None]
        masked = jnp.where(visible[None], scores, -1e+30)
        top = lax.optimization_barrier(jnp.max(masked, -1, keepdims=True))
        expo = jnp.exp(masked - top)
        probs = expo / lax.optimization_barrier(jnp.sum(expo, -1, keepdims=True))
        probs_low = low(probs)
        mixed = jnp.einsum('hqk,khd->qhd', probs_low, value_heads, precision=lax.Precision.HIGHEST)
        return low(low_back(mixed)).reshape(rows, H * HD)
    blocks = lax.map(jax.checkpoint(one_block), (query_rot.reshape(SEQ // rows, rows, H, HD), block_ids.reshape(SEQ // rows, rows)))
    return blocks.reshape(SEQ, H * HD)

def layer_fwd(x, gain_one, w_q, w_k, w_v, w_o, gain_two, w_g, w_u, w_d, places, block_ids):
    a = low(rms_scale(x, gain_one))
    q = low_back(matmul(a, w_q))
    k = low_back(matmul(a, w_k))
    v = low(low_back(matmul(a, w_v)))
    query_rot = low(rotate(q, places, H))
    key_rot = low(rotate(k, places, KVH))
    head_out = attend(query_rot, key_rot, v, block_ids)
    resid = x + low_back(matmul(head_out, w_o))
    b = low(rms_scale(resid, gain_two))
    gate_pre = low_back(matmul(b, w_g))
    up_pre = low_back(matmul(b, w_u))
    hidden = low(jax.nn.sigmoid(gate_pre) * gate_pre * up_pre)
    return resid + low_back(matmul(hidden, w_d))

def reference(tokens, table, norm1_gain, w_query, w_key, w_value, w_out, norm2_gain, w_gate, w_up, w_down, cotangent):
    offsets = jnp.arange(BLK, dtype=jnp.int32)
    places = (table[:, :, None] * BLK + offsets[None, None, :]).reshape(SEQ).astype(jnp.int32)
    block_ids = jnp.repeat(table.reshape(-1), BLK).astype(jnp.int32)
    weights = tuple((w.astype(jnp.float32) for w in (norm1_gain, w_query, w_key, w_value, w_out, norm2_gain, w_gate, w_up, w_down)))

    def per_sequence(totals, inputs):
        x_seq, cot_seq = inputs
        result, pull = jax.vjp(lambda x, *ws: layer_fwd(x, *ws, places, block_ids), x_seq.astype(jnp.float32), *weights)
        gradients = pull(cot_seq.astype(jnp.float32))
        updated = tuple((t + g for t, g in zip(totals, gradients[1:])))
        return (updated, (result.astype(jnp.bfloat16), gradients[0].astype(jnp.bfloat16)))
    start = tuple((jnp.zeros(w.shape, jnp.float32) for w in weights))
    totals, (outputs, grad_x) = lax.scan(per_sequence, start, (tokens, cotangent))
    return (outputs, grad_x, totals[0], totals[1], totals[2], totals[3], totals[4], totals[5], totals[6], totals[7], totals[8])
```

```python
import functools

import jax
import jax.numpy as jnp
from jax import lax
from jax.experimental import pallas as pl
from jax.experimental.pallas import tpu as pltpu
from jax.sharding import PartitionSpec as P

H = 18
KVH = 6
HD = 64
BLK = 256


EPS = 1e-05


def dot_first(left, right):
    return lax.dot_general(
        left, right, (((0,), (0,)), ((), ())), preferred_element_type=jnp.float32
    )


def dot_last(left, right):
    return lax.dot_general(
        left, right, (((1,), (1,)), ((), ())), preferred_element_type=jnp.float32
    )


def rotate(values, places, count, sign):
    split = HD // 2
    shaped = values.reshape(values.shape[0], count, HD)
    frequency = 10000.0 ** (-(jnp.arange(split, dtype=jnp.float32) * 2.0 / HD))
    angles = places.astype(jnp.float32)[:, None] * frequency
    cosine = jnp.cos(angles)[:, None, :]
    sine = jnp.sin(angles)[:, None, :] * sign
    first_half = shaped[..., :split]
    second_half = shaped[..., split:]
    turned = jnp.concatenate(
        [first_half * cosine - second_half * sine, second_half * cosine + first_half * sine], -1
    )
    return turned.reshape(values.shape[0], count * HD)


def norm_back(values, scale_inv, gain, grad_in):
    weighted = gain.astype(jnp.float32) * grad_in
    gain_grad = jnp.sum(grad_in * values * scale_inv, 0)
    grad_out = scale_inv * weighted - values * scale_inv**3 * jnp.mean(
        weighted * values, -1, keepdims=True
    )
    return (gain_grad, grad_out)


def to_groups(values, rows):
    ratio = H // KVH
    return values.reshape(rows, KVH, ratio, HD).transpose(1, 2, 0, 3).reshape(KVH, ratio * rows, HD)


def from_groups(values, rows):
    ratio = H // KVH
    return values.reshape(KVH, ratio, rows, HD).transpose(2, 0, 1, 3).reshape(rows, H * HD)


def plain_body(
    tokens,
    table,
    norm1_gain,
    w_query,
    w_key,
    w_value,
    w_out,
    norm2_gain,
    w_gate,
    w_up,
    w_down,
    cotangent,
):
    ratio = H // KVH
    scale = HD ** (-0.5)
    x = tokens[0].astype(jnp.float32)
    rows = x.shape[0]
    offsets = jnp.arange(BLK, dtype=jnp.int32)
    own_blocks = lax.dynamic_index_in_dim(table, lax.axis_index("ctx"), 0, keepdims=False)
    own_places = (own_blocks[:, None] * BLK + offsets[None, :]).reshape(-1)
    own_ids = jnp.tile(jnp.repeat(own_blocks, BLK), ratio)
    all_ids = jnp.repeat(table.reshape(-1), BLK)
    visible = all_ids[None, :] <= own_ids[:, None]
    forward_set = (
        lax.all_gather(norm1_gain, "fsdp", axis=0, tiled=True),
        lax.all_gather(w_query, "fsdp", axis=0, tiled=True),
        lax.all_gather(w_key, "fsdp", axis=0, tiled=True),
        lax.all_gather(w_value, "fsdp", axis=0, tiled=True),
        lax.all_gather(w_out, "fsdp", axis=0, tiled=True),
        lax.all_gather(norm2_gain, "fsdp", axis=0, tiled=True),
        lax.all_gather(w_gate, "fsdp", axis=0, tiled=True),
        lax.all_gather(w_up, "fsdp", axis=0, tiled=True),
        lax.all_gather(w_down, "fsdp", axis=0, tiled=True),
    )
    gain_one, w_q, w_k, w_v, w_o, gain_two, w_g, w_u, w_d = forward_set
    scale_one = lax.rsqrt(jnp.mean(x * x, -1, keepdims=True) + EPS)
    a = (x * scale_one * gain_one.astype(jnp.float32)).astype(jnp.bfloat16)
    q = jnp.dot(a, w_q, preferred_element_type=jnp.float32)
    k = jnp.dot(a, w_k, preferred_element_type=jnp.float32)
    v = jnp.dot(a, w_v, preferred_element_type=jnp.float32).astype(jnp.bfloat16)
    query_rot = rotate(q, own_places, H, 1.0).astype(jnp.bfloat16)
    key_rot = rotate(k, own_places, KVH, 1.0).astype(jnp.bfloat16)
    key_all, value_all = (
        lax.all_gather(key_rot, "ctx", axis=0, tiled=True),
        lax.all_gather(v, "ctx", axis=0, tiled=True),
    )
    length = key_all.shape[0]
    query_groups = to_groups(query_rot, rows)
    key_groups = key_all.reshape(length, KVH, HD).transpose(1, 0, 2)
    value_groups = value_all.reshape(length, KVH, HD).transpose(1, 0, 2)

    def group_fwd(inputs):
        query_one, key_one, value_one = inputs
        scores = dot_last(query_one, key_one) * scale
        masked = jnp.where(visible, scores, -1e30)
        top = jnp.max(masked, -1, keepdims=True)
        expo = jnp.exp(masked - top)
        total = jnp.sum(expo, -1, keepdims=True)
        probs = (expo / total).astype(jnp.bfloat16)
        mixed = jnp.dot(probs, value_one, preferred_element_type=jnp.float32)
        return (mixed.astype(jnp.bfloat16), (top + jnp.log(total))[:, 0])

    mixed_groups, log_sums = lax.map(group_fwd, (query_groups, key_groups, value_groups))
    head_out = from_groups(mixed_groups, rows)
    resid = x + jnp.dot(head_out, w_o, preferred_element_type=jnp.float32)
    scale_two = lax.rsqrt(jnp.mean(resid * resid, -1, keepdims=True) + EPS)
    b = (resid * scale_two * gain_two.astype(jnp.float32)).astype(jnp.bfloat16)
    gate_pre = jnp.dot(b, w_g, preferred_element_type=jnp.float32)
    up_pre = jnp.dot(b, w_u, preferred_element_type=jnp.float32)
    sig_gate = jax.nn.sigmoid(gate_pre)
    silu_gate = gate_pre * sig_gate
    hidden = (silu_gate * up_pre).astype(jnp.bfloat16)
    result = (resid + jnp.dot(hidden, w_d, preferred_element_type=jnp.float32)).astype(jnp.bfloat16)
    backward_set = (
        lax.all_gather(norm1_gain, "fsdp", axis=0, tiled=True),
        lax.all_gather(w_query, "fsdp", axis=0, tiled=True),
        lax.all_gather(w_key, "fsdp", axis=0, tiled=True),
        lax.all_gather(w_value, "fsdp", axis=0, tiled=True),
        lax.all_gather(w_out, "fsdp", axis=0, tiled=True),
        lax.all_gather(norm2_gain, "fsdp", axis=0, tiled=True),
        lax.all_gather(w_gate, "fsdp", axis=0, tiled=True),
        lax.all_gather(w_up, "fsdp", axis=0, tiled=True),
        lax.all_gather(w_down, "fsdp", axis=0, tiled=True),
    )
    gain_one_b, w_q_b, w_k_b, w_v_b, w_o_b, gain_two_b, w_g_b, w_u_b, w_d_b = backward_set
    dy = cotangent[0].astype(jnp.float32)
    dy_low = dy.astype(jnp.bfloat16)
    grad_d = dot_first(hidden, dy_low)
    dhidden = dot_last(dy_low, w_d_b)
    dgate = (dhidden * up_pre * sig_gate * (1.0 + gate_pre * (1.0 - sig_gate))).astype(jnp.bfloat16)
    dup_low = (dhidden * silu_gate).astype(jnp.bfloat16)
    grad_g = dot_first(b, dgate)
    grad_u = dot_first(b, dup_low)
    grad_b = dot_last(dgate, w_g_b) + dot_last(dup_low, w_u_b)
    grad_gain_two, norm_part = norm_back(resid, scale_two, gain_two_b, grad_b)
    grad_resid = dy + norm_part
    resid_low = grad_resid.astype(jnp.bfloat16)
    grad_o = dot_first(head_out, resid_low)
    dheads = dot_last(resid_low, w_o_b).astype(jnp.bfloat16)
    dhead_groups = to_groups(dheads, rows)

    def group_bwd(inputs):
        query_one, key_one, value_one, dout_one, lse_one = inputs
        scores = dot_last(query_one, key_one) * scale
        probs = jnp.exp(jnp.where(visible, scores, -1e30) - lse_one[:, None])
        probs_low = probs.astype(jnp.bfloat16)
        dprobs = dot_last(dout_one, value_one)
        inner = jnp.sum(probs * dprobs, -1, keepdims=True)
        dscores = (probs * (dprobs - inner)).astype(jnp.bfloat16)
        dquery = jnp.dot(dscores, key_one, preferred_element_type=jnp.float32) * scale
        dkey = dot_first(dscores, query_one) * scale
        dvalue = dot_first(probs_low, dout_one)
        return (dquery, dkey, dvalue)

    dquery_groups, dkey_groups, dvalue_groups = lax.map(
        group_bwd, (query_groups, key_groups, value_groups, dhead_groups, log_sums)
    )
    dquery_rot = from_groups(dquery_groups, rows)
    dkey_all = dkey_groups.transpose(1, 0, 2).reshape(length, KVH * HD)
    dvalue_all = dvalue_groups.transpose(1, 0, 2).reshape(length, KVH * HD)
    own_kv = lax.psum_scatter(
        jnp.concatenate([dkey_all, dvalue_all], 1).astype(jnp.bfloat16),
        "ctx",
        scatter_dimension=0,
        tiled=True,
    ).astype(jnp.float32)
    dq = rotate(dquery_rot, own_places, H, -1.0).astype(jnp.bfloat16)
    dk = rotate(own_kv[:, : KVH * HD], own_places, KVH, -1.0).astype(jnp.bfloat16)
    dv_low = own_kv[:, KVH * HD :].astype(jnp.bfloat16)
    grad_q = dot_first(a, dq)
    grad_k = dot_first(a, dk)
    grad_v = dot_first(a, dv_low)
    grad_a = dot_last(dq, w_q_b) + dot_last(dk, w_k_b) + dot_last(dv_low, w_v_b)
    grad_gain_one, input_part = norm_back(x, scale_one, gain_one_b, grad_a)
    grad_x = (grad_resid + input_part).astype(jnp.bfloat16)
    grad_terms = (
        grad_gain_one,
        grad_q,
        grad_k,
        grad_v,
        grad_o,
        grad_gain_two,
        grad_g,
        grad_u,
        grad_d,
    )
    shares = (
        lax.psum_scatter(
            grad_terms[0].astype(jnp.bfloat16), "fsdp", scatter_dimension=0, tiled=True
        ).astype(jnp.float32),
        lax.psum_scatter(
            grad_terms[1].astype(jnp.bfloat16), "fsdp", scatter_dimension=0, tiled=True
        ).astype(jnp.float32),
        lax.psum_scatter(
            grad_terms[2].astype(jnp.bfloat16), "fsdp", scatter_dimension=0, tiled=True
        ).astype(jnp.float32),
        lax.psum_scatter(
            grad_terms[3].astype(jnp.bfloat16), "fsdp", scatter_dimension=0, tiled=True
        ).astype(jnp.float32),
        lax.psum_scatter(
            grad_terms[4].astype(jnp.bfloat16), "fsdp", scatter_dimension=0, tiled=True
        ).astype(jnp.float32),
        lax.psum_scatter(
            grad_terms[5].astype(jnp.bfloat16), "fsdp", scatter_dimension=0, tiled=True
        ).astype(jnp.float32),
        lax.psum_scatter(
            grad_terms[6].astype(jnp.bfloat16), "fsdp", scatter_dimension=0, tiled=True
        ).astype(jnp.float32),
        lax.psum_scatter(
            grad_terms[7].astype(jnp.bfloat16), "fsdp", scatter_dimension=0, tiled=True
        ).astype(jnp.float32),
        lax.psum_scatter(
            grad_terms[8].astype(jnp.bfloat16), "fsdp", scatter_dimension=0, tiled=True
        ).astype(jnp.float32),
    )
    summed = (
        lax.psum(shares[0].astype(jnp.bfloat16), "ctx").astype(jnp.float32),
        lax.psum(shares[1].astype(jnp.bfloat16), "ctx").astype(jnp.float32),
        lax.psum(shares[2].astype(jnp.bfloat16), "ctx").astype(jnp.float32),
        lax.psum(shares[3].astype(jnp.bfloat16), "ctx").astype(jnp.float32),
        lax.psum(shares[4].astype(jnp.bfloat16), "ctx").astype(jnp.float32),
        lax.psum(shares[5].astype(jnp.bfloat16), "ctx").astype(jnp.float32),
        lax.psum(shares[6].astype(jnp.bfloat16), "ctx").astype(jnp.float32),
        lax.psum(shares[7].astype(jnp.bfloat16), "ctx").astype(jnp.float32),
        lax.psum(shares[8].astype(jnp.bfloat16), "ctx").astype(jnp.float32),
    )
    return (
        result[None],
        grad_x[None],
        summed[0],
        summed[1],
        summed[2],
        summed[3],
        summed[4],
        summed[5],
        summed[6],
        summed[7],
        summed[8],
    )


RATIO = H // KVH
PAIR = 2 * RATIO * HD
WIDE = 2 * HD
NT = (((1,), (1,)), ((), ()))
TN = (((0,), (0,)), ((), ()))
NN = (((1,), (0,)), ((), ()))
VMEM = pl.BlockSpec(memory_space=pltpu.VMEM)
HBM = pl.BlockSpec(memory_space=pl.ANY)
ROOM = pltpu.CompilerParams(vmem_limit_bytes=60 * 2**20)


def mm(left, right, dims):
    return lax.dot_general(left, right, dims, preferred_element_type=jnp.float32)


def cost(flops, nbytes, exps=0):
    return pl.CostEstimate(flops=int(flops), bytes_accessed=int(nbytes), transcendentals=int(exps))


def turn(values, cosine, sine):
    lane = lax.broadcasted_iota(jnp.int32, values.shape, 1)
    first = lax.rem(lane, HD) < HD // 2
    partner = jnp.where(first, pltpu.roll(values, WIDE - HD // 2, 1), pltpu.roll(values, HD // 2, 1))
    return values * cosine + partner * sine


def kv_kernel(x_ref, w_ref, cos_ref, sin_ref, a_ref, at_ref, kv_ref, gain_ref):
    width = kv_ref.shape[1]
    gains = jnp.transpose(w_ref[:, width : width + WIDE].astype(jnp.float32))[0:8]
    gain_ref[...] = gains
    x = x_ref[...].astype(jnp.float32)
    inv = lax.rsqrt(jnp.mean(x * x, -1, keepdims=True) + EPS)
    a = (x * inv * gains[0:1]).astype(jnp.bfloat16)
    a_ref[...] = a
    at_ref[...] = jnp.transpose(a)
    kv = mm(a, w_ref[:, 0:width], NN)
    for at in range(0, width, WIDE):
        part = kv[:, at : at + WIDE]
        if at < width // 2:
            part = turn(part, cos_ref[...], sin_ref[...])
        kv_ref[:, at : at + WIDE] = part.astype(jnp.bfloat16)


def kv_project(x, w_kvg, cosine, sine):
    rows, model = x.shape
    width = 2 * KVH * HD
    return pl.pallas_call(
        kv_kernel,
        in_specs=[VMEM] * 4,
        out_specs=[VMEM] * 4,
        out_shape=[
            jax.ShapeDtypeStruct((rows, model), jnp.bfloat16),
            jax.ShapeDtypeStruct((model, rows), jnp.bfloat16),
            jax.ShapeDtypeStruct((rows, width), jnp.bfloat16),
            jax.ShapeDtypeStruct((8, model), jnp.float32),
        ],
        compiler_params=ROOM,
        cost_estimate=cost(2 * rows * model * width, 2 * (3 * rows * model + model * width + rows * width)),
        name="kv_project",
    )(x, w_kvg, cosine, sine)


def q_kernel(a_ref, w_ref, cos_ref, sin_ref, q_ref):
    q = mm(a_ref[...], w_ref[...], NN)
    for at in range(0, q.shape[1], WIDE):
        q_ref[:, at : at + WIDE] = turn(q[:, at : at + WIDE], cos_ref[...], sin_ref[...]).astype(jnp.bfloat16)


def q_project(a, w_q, cosine, sine):
    rows, model = a.shape
    return pl.pallas_call(
        q_kernel,
        in_specs=[VMEM] * 4,
        out_specs=VMEM,
        out_shape=jax.ShapeDtypeStruct((rows, H * HD), jnp.bfloat16),
        compiler_params=ROOM,
        cost_estimate=cost(2 * rows * model * H * HD, 2 * (2 * rows * model + model * H * HD)),
        name="q_project",
    )(a, w_q, cosine, sine)


def pick_heads(ref, row, group, factor):
    own = lax.broadcasted_iota(jnp.int32, (BLK, WIDE), 1) // HD == group
    out = []
    for n in range(group * RATIO, (group + 1) * RATIO):
        piece = ref[pl.ds(row, BLK), pl.ds(n // 2 * WIDE, WIDE)].astype(jnp.float32) * factor
        if n % 2 != group:
            piece = pltpu.roll(piece, HD, 1)
        out.append(jnp.where(own, piece, 0.0).astype(jnp.bfloat16))
    return jnp.concatenate(out, 0)


def join_heads(groups):
    lane = lax.broadcasted_iota(jnp.int32, (BLK, WIDE), 1)
    parts = []
    for n in range(2 * RATIO):
        group, i = divmod(n, RATIO)
        piece = groups[group][i * BLK : (i + 1) * BLK, :]
        parts.append(piece if n % 2 == group else pltpu.roll(piece, HD, 1))
    return [jnp.where(lane < HD, parts[2 * b], parts[2 * b + 1]) for b in range(RATIO)]


def steps_of(pairs, most):
    return max(u for u in range(1, most + 1) if pairs % u == 0)


def attend_kernel(own_ref, slot_ref, q_ref, k_ref, v_ref, o_ref, lse_ref, s_scr, v_scr, q_scr, m_scr, a_scr):
    rows = RATIO * BLK
    length = v_ref.shape[0]
    pairs = length // BLK + 1
    lane = lax.broadcasted_iota(jnp.int32, (length, WIDE), 1)
    first = own_ref[0] + 1

    def place(t):
        j = jnp.where(t >= first, 1, 0)
        return j, pl.multiple_of(slot_ref[t - j * first] * BLK, BLK)

    outs = [[], []]
    for group in range(2):
        v_scr[...] = jnp.where(lane // HD == group, v_ref[...].astype(jnp.float32), 1.0).astype(jnp.bfloat16)
        for j in range(2):
            q_scr[j] = pick_heads(q_ref, j * BLK, group, HD**-0.5)
        m_scr[...] = jnp.full(m_scr.shape, -jnp.inf, jnp.float32)
        a_scr[...] = jnp.zeros(a_scr.shape, jnp.float32)

        def scores(t, carry):
            j, at = place(t)
            s = mm(q_scr[j], k_ref[pl.ds(at, BLK), :], NT)
            s_scr[t] = s
            m_scr[j] = jnp.maximum(m_scr[j], jnp.maximum(s[:, 0:WIDE], s[:, WIDE : 2 * WIDE]))
            return carry

        lax.fori_loop(0, pairs, scores, 0, unroll=steps_of(pairs, 9))
        for j in range(2):
            m_scr[j] = jnp.broadcast_to(jnp.max(m_scr[j], 1, keepdims=True), (rows, WIDE))

        def mix(t, carry):
            j, at = place(t)
            top = m_scr[j]
            p = jnp.exp(s_scr[t] - jnp.concatenate([top, top], 1)).astype(jnp.bfloat16)
            a_scr[j] += mm(p, v_scr[pl.ds(at, BLK), :], NN)
            return carry

        lax.fori_loop(0, pairs, mix, 0, unroll=steps_of(pairs, 9))
        own = lax.broadcasted_iota(jnp.int32, (rows, WIDE), 1) // HD == group
        for j in range(2):
            acc = a_scr[j]
            total = jnp.where(own, pltpu.roll(acc, HD, 1), acc)
            outs[j].append(acc / total)
            lse_ref[group, j] = jnp.transpose(m_scr[j] + jnp.log(total))[0:1]
    for j in range(2):
        for b, part in enumerate(join_heads(outs[j])):
            o_ref[pl.ds(j * BLK, BLK), pl.ds(b * WIDE, WIDE)] = part.astype(jnp.bfloat16)


def attend(own, slots, q, kv):
    rows, length = q.shape[0], kv.shape[0]
    nblk = length // BLK
    work = rows * length * H * (nblk + 1) // (2 * nblk)
    wide = pl.BlockSpec((rows, PAIR), lambda p, *_: (0, p))
    return pl.pallas_call(
        attend_kernel,
        grid_spec=pltpu.PrefetchScalarGridSpec(
            num_scalar_prefetch=2,
            grid=(KVH // 2,),
            in_specs=[
                wide,
                pl.BlockSpec((length, WIDE), lambda p, *_: (0, p)),
                pl.BlockSpec((length, WIDE), lambda p, *_: (0, p + KVH // 2)),
            ],
            out_specs=[wide, pl.BlockSpec((2, 2, 1, RATIO * BLK), lambda p, *_: (p, 0, 0, 0))],
            scratch_shapes=[
                pltpu.VMEM((nblk + 1, RATIO * BLK, BLK), jnp.float32),
                pltpu.VMEM((length, WIDE), jnp.bfloat16),
                pltpu.VMEM((2, RATIO * BLK, WIDE), jnp.bfloat16),
                pltpu.VMEM((2, RATIO * BLK, WIDE), jnp.float32),
                pltpu.VMEM((2, RATIO * BLK, WIDE), jnp.float32),
            ],
        ),
        out_shape=[
            jax.ShapeDtypeStruct((rows, H * HD), jnp.bfloat16),
            jax.ShapeDtypeStruct((KVH, 2, 1, RATIO * BLK), jnp.float32),
        ],
        compiler_params=ROOM,
        cost_estimate=cost(4 * 8 * work * HD, 4 * rows * H * HD + 2 * kv.size, work),
        name="attend",
    )(own, slots, q, kv, kv)


def attend_back_kernel(
    own_ref, slot_ref, q_ref, k_ref, v_ref, do_ref, o_ref, lse_ref, cos_ref, sin_ref,
    dq_ref, dks_ref, dkk_ref, dvs_ref, dvk_ref, dk_scr, dv_scr, q_scr, do_scr, st_scr, a_scr,
):
    rows = RATIO * BLK
    length = v_ref.shape[0]
    pairs = length // BLK + 1
    dk_scr[...] = jnp.zeros_like(dk_scr)
    dv_scr[...] = jnp.zeros_like(dv_scr)
    first = own_ref[0] + 1
    outs = [[], []]
    for group in range(2):
        for j in range(2):
            q_scr[j] = pick_heads(q_ref, j * BLK, group, HD**-0.5)
            grads = pick_heads(do_ref, j * BLK, group, 1.0)
            do_scr[j] = grads
            mixed = pick_heads(o_ref, j * BLK, group, 1.0)
            inner = jnp.sum(grads.astype(jnp.float32) * mixed.astype(jnp.float32), 1, keepdims=True)
            st_scr[j, 0:1] = jnp.transpose(jnp.broadcast_to(inner, (rows, WIDE)))[0:1]
            st_scr[j, 1:2] = lse_ref[group, j]
        a_scr[...] = jnp.zeros_like(a_scr)

        def step(t, carry):
            j = jnp.where(t >= first, 1, 0)
            at = pl.multiple_of(slot_ref[t - j * first] * BLK, BLK)
            keys = k_ref[pl.ds(at, BLK), :]
            qs, grads = q_scr[j], do_scr[j]
            p = jnp.exp(mm(keys, qs, NT) - st_scr[j, 1:2])
            dp = mm(v_ref[pl.ds(at, BLK), :], grads, NT)
            ds = (p * (dp - st_scr[j, 0:1])).astype(jnp.bfloat16)
            dv_scr[pl.ds(at, BLK), :] += mm(p.astype(jnp.bfloat16), grads, NN)
            dk_scr[pl.ds(at, BLK), :] += mm(ds, qs, NN)
            a_scr[j] += mm(ds, keys, TN)
            return carry

        lax.fori_loop(0, pairs, step, 0, unroll=steps_of(pairs, 3))
        for j in range(2):
            outs[j].append(a_scr[j] * HD**-0.5)
    for j in range(2):
        span = pl.ds(j * BLK, BLK)
        for b, part in enumerate(join_heads(outs[j])):
            dq_ref[span, pl.ds(b * WIDE, WIDE)] = turn(part, cos_ref[span, :], -sin_ref[span, :]).astype(jnp.bfloat16)
    own_rows = length // 4
    for ref, scr, order in (
        (dks_ref, dk_scr, (1, 3)),
        (dkk_ref, dk_scr, (0, 2)),
        (dvs_ref, dv_scr, (2, 3)),
        (dvk_ref, dv_scr, (0, 1)),
    ):
        for n, r in enumerate(order):
            ref[n] = scr[pl.ds(r * own_rows, own_rows), :].astype(jnp.bfloat16)


def attend_back(own, slots, q, kv, grads, mixed, lse, cosine, sine):
    rows, length = q.shape[0], kv.shape[0]
    nblk = length // BLK
    work = rows * length * H * (nblk + 1) // (2 * nblk)
    wide = pl.BlockSpec((rows, PAIR), lambda p, *_: (0, p))
    whole = pl.BlockSpec((rows, WIDE), lambda p, *_: (0, 0))
    half = pl.BlockSpec((2, length // 4, WIDE), lambda p, *_: (0, 0, p))
    half_shape = jax.ShapeDtypeStruct((2, length // 4, KVH * HD), jnp.bfloat16)
    return pl.pallas_call(
        attend_back_kernel,
        grid_spec=pltpu.PrefetchScalarGridSpec(
            num_scalar_prefetch=2,
            grid=(KVH // 2,),
            in_specs=[
                wide,
                pl.BlockSpec((length, WIDE), lambda p, *_: (0, p)),
                pl.BlockSpec((length, WIDE), lambda p, *_: (0, p + KVH // 2)),
                wide,
                wide,
                pl.BlockSpec((2, 2, 1, RATIO * BLK), lambda p, *_: (p, 0, 0, 0)),
                whole,
                whole,
            ],
            out_specs=[wide, half, half, half, half],
            scratch_shapes=[
                pltpu.VMEM((length, WIDE), jnp.float32),
                pltpu.VMEM((length, WIDE), jnp.float32),
                pltpu.VMEM((2, RATIO * BLK, WIDE), jnp.bfloat16),
                pltpu.VMEM((2, RATIO * BLK, WIDE), jnp.bfloat16),
                pltpu.VMEM((2, 8, RATIO * BLK), jnp.float32),
                pltpu.VMEM((2, RATIO * BLK, WIDE), jnp.float32),
            ],
        ),
        out_shape=[jax.ShapeDtypeStruct((rows, H * HD), jnp.bfloat16)] + [half_shape] * 4,
        compiler_params=ROOM,
        cost_estimate=cost(10 * 8 * work * HD, 8 * rows * H * HD + 4 * kv.size, work),
        name="attend_back",
    )(own, slots, q, kv, kv, grads, mixed, lse, cosine, sine)


def middle_kernel(
    core_ref, ho_ref, x_ref, dy_ref, wo_ref, gain_ref, gu0_ref, gu1_ref, d0_ref, d1_ref,
    out_ref, hot_ref, bt_ref, ht_ref, dg_ref, du_ref, dr_ref, low_ref, dh_ref, gg_ref,
    gu_scr, d_scr, r_scr, b_scr, acc_scr, db_scr, h_scr, sem,
):
    r = pl.program_id(0)
    count = pl.num_programs(0)
    core = core_ref[0]
    lines, cut = gu0_ref.shape[1], gu0_ref.shape[3]
    cut_d = d0_ref.shape[2]

    def copies(at, slot):
        out = []
        for n, (gu, d) in enumerate(((gu0_ref, d0_ref), (gu1_ref, d1_ref))):
            other = core if n == 0 else 1 - core
            for z in range(lines):
                shard = 2 * z + other
                i = 2 * (n * lines + z)
                out.append(
                    pltpu.make_async_copy(
                        gu.at[at, z],
                        gu_scr.at[slot, :, pl.ds(pl.multiple_of(shard * cut, 16), cut), :],
                        sem.at[slot, i],
                    )
                )
                out.append(
                    pltpu.make_async_copy(
                        d.at[at, z],
                        d_scr.at[slot, pl.ds(pl.multiple_of(shard * cut_d, 16), cut_d), :],
                        sem.at[slot, i + 1],
                    )
                )
        return out

    slot = lax.rem(r, 2)

    @pl.when(r == 0)
    def _():
        for c in copies(0, 0):
            c.start()
        resid = x_ref[...].astype(jnp.float32) + mm(ho_ref[...], wo_ref[...], NN)
        r_scr[...] = resid
        inv = lax.rsqrt(jnp.mean(resid * resid, -1, keepdims=True) + EPS)
        b = (resid * inv * gain_ref[1:2]).astype(jnp.bfloat16)
        b_scr[...] = b
        bt_ref[...] = jnp.transpose(b)
        hot_ref[...] = jnp.transpose(ho_ref[...])

    for c in copies(r, slot):
        c.wait()

    @pl.when(r + 1 < count)
    def _():
        for c in copies(r + 1, 1 - slot):
            c.start()

    width = dg_ref.shape[2]
    for at in range(0, width, 256):
        span = slice(at, at + 256)
        gate = mm(b_scr[...], gu_scr[slot, 0, :, span], NN)
        up = mm(b_scr[...], gu_scr[slot, 1, :, span], NN)
        dhid = mm(dy_ref[...], d_scr[slot, span, :], NT)
        sig = jax.nn.sigmoid(gate)
        silu = gate * sig
        hidden = (silu * up).astype(jnp.bfloat16)
        h_scr[:, span] = hidden
        ht_ref[0, span, :] = jnp.transpose(hidden)
        dg_ref[0, :, span] = (dhid * up * sig * (1.0 + gate * (1.0 - sig))).astype(jnp.bfloat16)
        du_ref[0, :, span] = (dhid * silu).astype(jnp.bfloat16)
    model = acc_scr.shape[1]
    for at in range(0, model, 384):
        span = slice(at, at + 384)
        acc = mm(h_scr[...], d_scr[slot, :, span], NN)
        db = mm(dg_ref[0], gu_scr[slot, 0, span, :], NT) + mm(du_ref[0], gu_scr[slot, 1, span, :], NT)

        @pl.when(r == 0)
        def _():
            acc_scr[:, span] = acc
            db_scr[:, span] = db

        @pl.when(r > 0)
        def _():
            acc_scr[:, span] += acc
            db_scr[:, span] += db

    @pl.when(r == count - 1)
    def _():
        resid = r_scr[...]
        out_ref[...] = (resid + acc_scr[...]).astype(jnp.bfloat16)
        inv = lax.rsqrt(jnp.mean(resid * resid, -1, keepdims=True) + EPS)
        db = db_scr[...]
        gg_ref[...] = jnp.sum(db * resid * inv, 0, keepdims=True)
        weighted = gain_ref[1:2] * db
        dr = (
            dy_ref[...].astype(jnp.float32)
            + inv * weighted
            - resid * (inv * inv * inv) * jnp.mean(weighted * resid, -1, keepdims=True)
        )
        dr_ref[...] = dr
        low = dr.astype(jnp.bfloat16)
        low_ref[...] = low
        dh_ref[...] = mm(low, wo_ref[...], NT).astype(jnp.bfloat16)


def middle(core, ho, x, dy, w_o, gains, gu, d):
    rows, model = x.shape
    count, lines, _, cut, width = gu[0].shape
    cut_d = d[0].shape[2]
    once = pl.Buffered(1)
    whole = lambda shape: pl.BlockSpec(shape, lambda r, *_: (0,) * len(shape), pipeline_mode=once)
    act = pl.BlockSpec((1, rows, width), lambda r, *_: (r, 0, 0))
    low = jnp.bfloat16
    return pl.pallas_call(
        middle_kernel,
        grid_spec=pltpu.PrefetchScalarGridSpec(
            num_scalar_prefetch=1,
            grid=(count,),
            in_specs=[
                whole((rows, H * HD)), whole((rows, model)), whole((rows, model)), whole((H * HD, model)), whole((8, model)),
                HBM, HBM, HBM, HBM,
            ],
            out_specs=[
                whole((rows, model)), whole((H * HD, rows)), whole((model, rows)),
                pl.BlockSpec((1, width, rows), lambda r, *_: (r, 0, 0)), act, act,
                whole((rows, model)), whole((rows, model)), whole((rows, H * HD)), whole((1, model)),
            ],
            scratch_shapes=[
                pltpu.VMEM((2, 2, 2 * lines * cut, width), low),
                pltpu.VMEM((2, width, model), low),
                pltpu.VMEM((rows, model), jnp.float32),
                pltpu.VMEM((rows, model), low),
                pltpu.VMEM((rows, model), jnp.float32),
                pltpu.VMEM((rows, model), jnp.float32),
                pltpu.VMEM((rows, width), low),
                pltpu.SemaphoreType.DMA((2, 4 * lines)),
            ],
        ),
        out_shape=[
            jax.ShapeDtypeStruct((rows, model), low),
            jax.ShapeDtypeStruct((H * HD, rows), low),
            jax.ShapeDtypeStruct((model, rows), low),
            jax.ShapeDtypeStruct((count, width, rows), low),
            jax.ShapeDtypeStruct((count, rows, width), low),
            jax.ShapeDtypeStruct((count, rows, width), low),
            jax.ShapeDtypeStruct((rows, model), jnp.float32),
            jax.ShapeDtypeStruct((rows, model), low),
            jax.ShapeDtypeStruct((rows, H * HD), low),
            jax.ShapeDtypeStruct((1, model), jnp.float32),
        ],
        compiler_params=ROOM,
        cost_estimate=cost(12 * rows * model * width * count + 4 * rows * model * model, 2 * 16 * rows * model + 6 * count * width * model, rows * width * count),
        name="middle",
    )(core, ho, x, dy, w_o, gains, gu[0], gu[1], d[0], d[1])


def last_kernel(x_ref, gain_ref, dr_ref, dq_ref, dk_ref, dv_ref, wq_ref, wkv_ref, cos_ref, sin_ref, gx_ref, act_ref, gg_ref):
    half = KVH * HD
    model = x_ref.shape[1]
    act_ref[:, 0 : H * HD] = dq_ref[...]
    for at in range(0, half, WIDE):
        turned = turn(dk_ref[:, at : at + WIDE], cos_ref[...], -sin_ref[...])
        act_ref[:, H * HD + at : H * HD + at + WIDE] = turned.astype(jnp.bfloat16)
    act_ref[:, H * HD + half : H * HD + 2 * half] = dv_ref[...].astype(jnp.bfloat16)
    act_ref[:, H * HD + 2 * half :] = jnp.zeros((x_ref.shape[0], act_ref.shape[1] - H * HD - 2 * half), jnp.bfloat16)
    da = mm(dq_ref[...], wq_ref[...], NT)
    da += mm(act_ref[:, H * HD : H * HD + 2 * half], wkv_ref[:, 0 : 2 * half], NT)
    x = x_ref[...].astype(jnp.float32)
    inv = lax.rsqrt(jnp.mean(x * x, -1, keepdims=True) + EPS)
    gg_ref[...] = jnp.sum(da * x * inv, 0, keepdims=True)
    weighted = gain_ref[0:1] * da
    gx = dr_ref[...] + inv * weighted - x * (inv * inv * inv) * jnp.mean(weighted * x, -1, keepdims=True)
    gx_ref[...] = gx.astype(jnp.bfloat16)


def last(x, gains, dr, dq, dk, dv, w_q, w_kvg, cosine, sine, padded):
    rows, model = x.shape
    return pl.pallas_call(
        last_kernel,
        in_specs=[VMEM] * 10,
        out_specs=[VMEM] * 3,
        out_shape=[
            jax.ShapeDtypeStruct((rows, model), jnp.bfloat16),
            jax.ShapeDtypeStruct((rows, padded), jnp.bfloat16),
            jax.ShapeDtypeStruct((1, model), jnp.float32),
        ],
        compiler_params=ROOM,
        cost_estimate=cost(2 * rows * model * (H + 2 * KVH) * HD, 10 * rows * model + 2 * model * (H + 2 * KVH) * HD),
        name="last",
    )(x, gains, dr, dq, dk, dv, w_q, w_kvg, cosine, sine)


def product_kernel(pos_ref, l0_ref, l1_ref, r0_ref, r1_ref, out_ref):
    total = mm(l0_ref[...], r0_ref[0], NN) + mm(l1_ref[...], r1_ref[0], NN)
    out_ref[0] = total.astype(jnp.bfloat16)


def products(pos, left, right, blocks, width, column):
    rows, tokens = left[0].shape
    spec = pl.BlockSpec((rows, tokens), lambda n, *_: (0, 0))
    act = pl.BlockSpec((1, tokens, width), lambda n, pos_ref: column(n, pos_ref))
    return pl.pallas_call(
        product_kernel,
        grid_spec=pltpu.PrefetchScalarGridSpec(
            num_scalar_prefetch=1,
            grid=(blocks,),
            in_specs=[spec, spec, act, act],
            out_specs=pl.BlockSpec((1, rows, width), lambda n, *_: (n, 0, 0)),
        ),
        out_shape=jax.ShapeDtypeStruct((blocks, rows, width), jnp.bfloat16),
        compiler_params=ROOM,
        cost_estimate=cost(4 * blocks * rows * tokens * width, 4 * rows * tokens + 2 * blocks * (2 * tokens + rows) * width),
        name="products",
    )(pos, left[0], left[1], right[0], right[1])


def whole_product_kernel(pos_ref, left_ref, right_ref, out_ref):
    shards, cut = out_ref.shape[0], out_ref.shape[2]
    total = mm(left_ref[0], right_ref[...], NN).astype(jnp.bfloat16)
    for s in range(shards):
        out_ref[s, 0] = total[s * cut : (s + 1) * cut]


def down_product(pos, left, right, shards):
    parts, rows, tokens = left.shape
    model = right.shape[1]
    out = pl.pallas_call(
        whole_product_kernel,
        grid_spec=pltpu.PrefetchScalarGridSpec(
            num_scalar_prefetch=1,
            grid=(parts,),
            in_specs=[pl.BlockSpec((1, rows, tokens), lambda r, *_: (r, 0, 0)), pl.BlockSpec((tokens, model), lambda r, *_: (0, 0))],
            out_specs=pl.BlockSpec((shards, 1, rows // shards, model), lambda r, pos_ref: (0, pos_ref[0] ^ r, 0, 0)),
        ),
        out_shape=jax.ShapeDtypeStruct((shards, parts, rows // shards, model), jnp.bfloat16),
        compiler_params=ROOM,
        cost_estimate=cost(2 * parts * rows * tokens * model, 2 * (parts * rows * tokens + tokens * model + parts * rows * model)),
        name="down_product",
    )(pos, left, right)
    return out.reshape(parts * rows, model)


ACROSS_X = [(t, t ^ 1) for t in range(4)]
ACROSS_Y = [(t, t ^ 2) for t in range(4)]
ACROSS_CORE = [(f, f ^ 1) for f in range(8)]
ACROSS_PAIR = [(f, f ^ 2) for f in range(8)]
MIDDLE = [(f, 6 - 2 * (f // 2) + f % 2) for f in (2, 3, 4, 5)]
TO_ENDS = [(2, 0), (3, 1), (4, 6), (5, 7)]
TO_MIDDLE = [(b, a) for a, b in TO_ENDS]


def across_x(v):
    return lax.ppermute(v, "ctx", ACROSS_X)


def across_y(v):
    return lax.ppermute(v, "ctx", ACROSS_Y)


def other_core(v):
    return lax.ppermute(v, "fsdp", ACROSS_CORE)


def gather_line(v, z):
    odd = z % 2 == 1
    partner = lax.ppermute(v, "fsdp", ACROSS_PAIR)
    pair = jnp.stack([jnp.where(odd, partner, v), jnp.where(odd, v, partner)])
    far = lax.ppermute(pair, "fsdp", MIDDLE)
    end = lax.ppermute(far, "fsdp", TO_ENDS)
    other = far + end
    high = z >= 2
    return jnp.concatenate([jnp.where(high, other, pair), jnp.where(high, pair, other)])


def gather_square(v):
    from_x, from_y = across_x(v), across_y(v)
    half = v.shape[0] // 2
    far_x = across_x(from_y[:half])
    far_y = across_y(from_x[half:])
    return jnp.stack([v, from_x, from_y, jnp.concatenate([far_x, far_y])])


def scatter_square(x_send, x_keep, y_send, y_keep):
    wide = lambda v: v.astype(jnp.float32)
    got_x, got_y = across_x(x_send), across_y(y_send)
    pass_y = (wide(x_keep[1]) + wide(got_x[1])).astype(jnp.bfloat16)
    pass_x = (wide(y_keep[1]) + wide(got_y[1])).astype(jnp.bfloat16)
    last_y, last_x = across_y(pass_y), across_x(pass_x)
    return (
        wide(x_keep[0]) + wide(got_x[0]) + wide(last_y),
        wide(y_keep[0]) + wide(got_y[0]) + wide(last_x),
    )


def scatter_line(v, z):
    wide = lambda v: v.astype(jnp.float32)
    side = z // 2
    far = lax.dynamic_slice_in_dim(v, 2 * (1 - side), 2, 0)
    near = lax.dynamic_slice_in_dim(v, 2 * side, 2, 0)
    got = lax.ppermute(far, "fsdp", TO_MIDDLE)
    crossed = lax.ppermute((wide(far) + wide(got)).astype(jnp.bfloat16), "fsdp", MIDDLE)
    near = wide(near) + wide(crossed)
    send = lax.dynamic_index_in_dim(near, 1 - z % 2, 0, keepdims=False).astype(jnp.bfloat16)
    keep = lax.dynamic_index_in_dim(near, z % 2, 0, keepdims=False)
    return keep + wide(lax.ppermute(send, "fsdp", ACROSS_PAIR))


def in_order(parts, t):
    return jnp.stack([lax.dynamic_index_in_dim(parts, t ^ q, 0, keepdims=False) for q in range(4)])


def lanes(v, core):
    shaped = v.reshape(4, 2, v.shape[0] // 8, v.shape[1])
    pick = lambda c: lax.dynamic_index_in_dim(shaped, c, 1, keepdims=False).reshape(-1, v.shape[1])
    return pick(core), pick(1 - core)


def square_body(
    tokens,
    table,
    norm1_gain,
    w_query,
    w_key,
    w_value,
    w_out,
    norm2_gain,
    w_gate,
    w_up,
    w_down,
    cotangent,
):
    x, dy = tokens[0], cotangent[0]
    rows, model = x.shape
    t = lax.axis_index("ctx")
    f = lax.axis_index("fsdp")
    z, core = f // 2, f % 2
    pos = t.reshape(1).astype(jnp.int32)
    cut, hidden_width = w_gate.shape
    cut_d = w_down.shape[0]
    quarter = hidden_width // 4
    kv_width = 2 * KVH * HD

    gains_pad = jnp.pad(jnp.stack([norm1_gain, norm2_gain], 1), ((0, 0), (0, WIDE - 2)))
    w_kvg = lax.all_gather(jnp.concatenate([w_key, w_value, gains_pad], 1), "fsdp", axis=0, tiled=True)
    w_q = lax.all_gather(w_query, "fsdp", axis=0, tiled=True)
    w_o = lax.all_gather(w_out, "fsdp", axis=0, tiled=True)

    def own_quarter(w):
        shaped = w.reshape(cut, 8, 4, cut_d // 4)
        return lax.dynamic_index_in_dim(shaped, t, 2, keepdims=False).reshape(cut, quarter)

    gu_own = gather_square(gather_line(jnp.stack([own_quarter(w_gate), own_quarter(w_up)]), z))
    d_part = lax.dynamic_index_in_dim(w_down.reshape(4, cut_d // 4, model), t, 0, keepdims=False)
    d_own = gather_square(gather_line(d_part, z))
    gu = (gu_own, other_core(gu_own))
    d = (d_own, other_core(d_own))

    relative = jnp.arange(4) ^ t
    offsets = jnp.arange(BLK, dtype=jnp.int32)
    ordered = table[relative].reshape(-1)
    own = ordered[:2].astype(jnp.int32)
    slots = jnp.zeros((ordered.shape[0],), jnp.int32).at[ordered].set(jnp.arange(ordered.shape[0], dtype=jnp.int32))
    places = (own[:, None] * BLK + offsets[None, :]).reshape(-1)
    frequency = 10000.0 ** (-(jnp.arange(HD // 2, dtype=jnp.float32) * 2.0 / HD))
    angles = places.astype(jnp.float32)[:, None] * frequency
    cosine = jnp.tile(jnp.cos(angles), (1, 4))
    sine = jnp.sin(angles)
    sine = jnp.concatenate([-sine, sine, -sine, sine], 1)

    a, a_t, kv_own, gains = kv_project(x, w_kvg, cosine, sine)
    q = q_project(a, w_q, cosine, sine)
    kv = gather_square(kv_own).reshape(4 * rows, kv_width)
    mixed, lse = attend(own, slots, q, kv)
    out, mixed_t, b_t, hidden_t, dgate, dup, dr, dr_low, dheads, gg2 = middle(
        core.reshape(1).astype(jnp.int32), mixed, x, dy, w_o, gains, gu, d
    )

    grad_d = lax.psum_scatter(down_product(pos, hidden_t, dy, 8), "fsdp", scatter_dimension=0, tiled=True)
    b_mine, b_other = lanes(b_t, core)
    left = (b_mine, other_core(b_other))
    gates, ups = (dgate, other_core(dgate)), (dup, other_core(dup))
    r_gu = scatter_square(
        products(pos, left, gates, 2, quarter, lambda n, p: (1 + 2 * n, 0, 0)),
        products(pos, left, gates, 2, quarter, lambda n, p: (2 * n, 0, 0)),
        products(pos, left, ups, 2, quarter, lambda n, p: (2 + n, 0, 0)),
        products(pos, left, ups, 2, quarter, lambda n, p: (n, 0, 0)),
    )
    r_gu = jnp.stack([v.astype(jnp.bfloat16).reshape(4, cut, quarter) for v in r_gu], 1)
    s_gu = scatter_line(r_gu, z).astype(jnp.bfloat16)
    all_gu = lax.all_gather(s_gu, "ctx", axis=0, tiled=False)

    def whole_columns(v):
        return v.reshape(4, cut, 8, cut_d // 4).transpose(1, 2, 0, 3).reshape(cut, hidden_width).astype(jnp.float32)

    grad_g, grad_u = whole_columns(all_gu[:, 0]), whole_columns(all_gu[:, 1])

    grad_o = mm(mixed_t, dr_low, NN).astype(jnp.bfloat16)
    grad_o = lax.psum_scatter(grad_o, "fsdp", scatter_dimension=0, tiled=True)
    grad_o = lax.psum(grad_o, "ctx").astype(jnp.float32)
    grad_d = lax.psum(grad_d, "ctx").astype(jnp.float32)
    dq, dk_send, dk_keep, dv_send, dv_keep = attend_back(own, slots, q, kv, dheads, mixed, lse, cosine, sine)
    dk, dv = scatter_square(dk_send, dk_keep, dv_send, dv_keep)
    padded = -(-(H * HD + kv_width) // (8 * WIDE)) * 8 * WIDE
    grad_x, act, gg1 = last(x, gains, dr, dq, dk, dv, w_q, w_kvg, cosine, sine, padded)
    a_mine, a_other = lanes(a_t, core)
    left = (a_mine, other_core(a_other))
    acts = (act[None], other_core(act)[None])
    eighth = padded // 8
    r_qkv = scatter_square(
        products(pos, left, acts, 2, eighth, lambda n, p: (0, 0, 2 * (p[0] ^ (1 + 2 * n)))),
        products(pos, left, acts, 2, eighth, lambda n, p: (0, 0, 2 * (p[0] ^ (2 * n)))),
        products(pos, left, acts, 2, eighth, lambda n, p: (0, 0, 2 * (p[0] ^ (2 + n)) + 1)),
        products(pos, left, acts, 2, eighth, lambda n, p: (0, 0, 2 * (p[0] ^ n) + 1)),
    )
    r_qkv = jnp.concatenate([v.astype(jnp.bfloat16) for v in r_qkv], 1).reshape(4, cut, 2 * eighth)
    s_qkv = scatter_line(r_qkv, z).astype(jnp.bfloat16)
    all_qkv = in_order(gather_square(s_qkv), t)
    grad_qkv = all_qkv.transpose(1, 0, 2).reshape(cut, padded).astype(jnp.float32)
    gain_grads = lax.psum(jnp.concatenate([gg1, gg2]), ("ctx", "fsdp"))
    gain_grads = lax.dynamic_slice_in_dim(gain_grads, f * cut, cut, 1)
    return (
        out[None],
        grad_x[None],
        gain_grads[0],
        grad_qkv[:, : H * HD],
        grad_qkv[:, H * HD : H * HD + kv_width // 2],
        grad_qkv[:, H * HD + kv_width // 2 : H * HD + kv_width],
        grad_o,
        gain_grads[1],
        grad_g,
        grad_u,
        grad_d,
    )


def solution(mesh):
    placed = (
        P("fsdp", "ctx", None),
        P(),
        P("fsdp"),
        P("fsdp", None),
        P("fsdp", None),
        P("fsdp", None),
        P("fsdp", None),
        P("fsdp"),
        P("fsdp", None),
        P("fsdp", None),
        P("fsdp", None),
        P("fsdp", "ctx", None),
    )
    square = mesh.shape["ctx"] == 4 and mesh.shape["fsdp"] == 8
    return jax.shard_map(
        square_body if square else plain_body,
        mesh=mesh,
        in_specs=placed,
        out_specs=(
            P("fsdp", "ctx", None),
            P("fsdp", "ctx", None),
            P("fsdp"),
            P("fsdp", None),
            P("fsdp", None),
            P("fsdp", None),
            P("fsdp", None),
            P("fsdp"),
            P("fsdp", None),
            P("fsdp", None),
            P("fsdp", None),
        ),
        check_vma=False,
    )
```

```python
import functools

import jax
import jax.numpy as jnp
from jax import lax
from jax.experimental import pallas as pl
from jax.experimental.pallas import tpu as pltpu
from jax.sharding import PartitionSpec as P

H = 18
KVH = 6
HD = 64
BLK = 256


EPS = 1e-05


def dot_first(left, right):
    return lax.dot_general(
        left, right, (((0,), (0,)), ((), ())), preferred_element_type=jnp.float32
    )


def dot_last(left, right):
    return lax.dot_general(
        left, right, (((1,), (1,)), ((), ())), preferred_element_type=jnp.float32
    )


def rotate(values, places, count, sign):
    split = HD // 2
    shaped = values.reshape(values.shape[0], count, HD)
    frequency = 10000.0 ** (-(jnp.arange(split, dtype=jnp.float32) * 2.0 / HD))
    angles = places.astype(jnp.float32)[:, None] * frequency
    cosine = jnp.cos(angles)[:, None, :]
    sine = jnp.sin(angles)[:, None, :] * sign
    first_half = shaped[..., :split]
    second_half = shaped[..., split:]
    turned = jnp.concatenate(
        [first_half * cosine - second_half * sine, second_half * cosine + first_half * sine], -1
    )
    return turned.reshape(values.shape[0], count * HD)


def norm_back(values, scale_inv, gain, grad_in):
    weighted = gain.astype(jnp.float32) * grad_in
    gain_grad = jnp.sum(grad_in * values * scale_inv, 0)
    grad_out = scale_inv * weighted - values * scale_inv**3 * jnp.mean(
        weighted * values, -1, keepdims=True
    )
    return (gain_grad, grad_out)


def to_groups(values, rows):
    ratio = H // KVH
    return values.reshape(rows, KVH, ratio, HD).transpose(1, 2, 0, 3).reshape(KVH, ratio * rows, HD)


def from_groups(values, rows):
    ratio = H // KVH
    return values.reshape(KVH, ratio, rows, HD).transpose(2, 0, 1, 3).reshape(rows, H * HD)


def plain_body(
    tokens,
    table,
    norm1_gain,
    w_query,
    w_key,
    w_value,
    w_out,
    norm2_gain,
    w_gate,
    w_up,
    w_down,
    cotangent,
):
    ratio = H // KVH
    scale = HD ** (-0.5)
    x = tokens[0].astype(jnp.float32)
    rows = x.shape[0]
    offsets = jnp.arange(BLK, dtype=jnp.int32)
    own_blocks = lax.dynamic_index_in_dim(table, lax.axis_index("ctx"), 0, keepdims=False)
    own_places = (own_blocks[:, None] * BLK + offsets[None, :]).reshape(-1)
    own_ids = jnp.tile(jnp.repeat(own_blocks, BLK), ratio)
    all_ids = jnp.repeat(table.reshape(-1), BLK)
    visible = all_ids[None, :] <= own_ids[:, None]
    forward_set = (
        lax.all_gather(norm1_gain, "fsdp", axis=0, tiled=True),
        lax.all_gather(w_query, "fsdp", axis=0, tiled=True),
        lax.all_gather(w_key, "fsdp", axis=0, tiled=True),
        lax.all_gather(w_value, "fsdp", axis=0, tiled=True),
        lax.all_gather(w_out, "fsdp", axis=0, tiled=True),
        lax.all_gather(norm2_gain, "fsdp", axis=0, tiled=True),
        lax.all_gather(w_gate, "fsdp", axis=0, tiled=True),
        lax.all_gather(w_up, "fsdp", axis=0, tiled=True),
        lax.all_gather(w_down, "fsdp", axis=0, tiled=True),
    )
    gain_one, w_q, w_k, w_v, w_o, gain_two, w_g, w_u, w_d = forward_set
    scale_one = lax.rsqrt(jnp.mean(x * x, -1, keepdims=True) + EPS)
    a = (x * scale_one * gain_one.astype(jnp.float32)).astype(jnp.bfloat16)
    q = jnp.dot(a, w_q, preferred_element_type=jnp.float32)
    k = jnp.dot(a, w_k, preferred_element_type=jnp.float32)
    v = jnp.dot(a, w_v, preferred_element_type=jnp.float32).astype(jnp.bfloat16)
    query_rot = rotate(q, own_places, H, 1.0).astype(jnp.bfloat16)
    key_rot = rotate(k, own_places, KVH, 1.0).astype(jnp.bfloat16)
    key_all, value_all = (
        lax.all_gather(key_rot, "ctx", axis=0, tiled=True),
        lax.all_gather(v, "ctx", axis=0, tiled=True),
    )
    length = key_all.shape[0]
    query_groups = to_groups(query_rot, rows)
    key_groups = key_all.reshape(length, KVH, HD).transpose(1, 0, 2)
    value_groups = value_all.reshape(length, KVH, HD).transpose(1, 0, 2)

    def group_fwd(inputs):
        query_one, key_one, value_one = inputs
        scores = dot_last(query_one, key_one) * scale
        masked = jnp.where(visible, scores, -1e30)
        top = jnp.max(masked, -1, keepdims=True)
        expo = jnp.exp(masked - top)
        total = jnp.sum(expo, -1, keepdims=True)
        probs = (expo / total).astype(jnp.bfloat16)
        mixed = jnp.dot(probs, value_one, preferred_element_type=jnp.float32)
        return (mixed.astype(jnp.bfloat16), (top + jnp.log(total))[:, 0])

    mixed_groups, log_sums = lax.map(group_fwd, (query_groups, key_groups, value_groups))
    head_out = from_groups(mixed_groups, rows)
    resid = x + jnp.dot(head_out, w_o, preferred_element_type=jnp.float32)
    scale_two = lax.rsqrt(jnp.mean(resid * resid, -1, keepdims=True) + EPS)
    b = (resid * scale_two * gain_two.astype(jnp.float32)).astype(jnp.bfloat16)
    gate_pre = jnp.dot(b, w_g, preferred_element_type=jnp.float32)
    up_pre = jnp.dot(b, w_u, preferred_element_type=jnp.float32)
    sig_gate = jax.nn.sigmoid(gate_pre)
    silu_gate = gate_pre * sig_gate
    hidden = (silu_gate * up_pre).astype(jnp.bfloat16)
    result = (resid + jnp.dot(hidden, w_d, preferred_element_type=jnp.float32)).astype(jnp.bfloat16)
    backward_set = (
        lax.all_gather(norm1_gain, "fsdp", axis=0, tiled=True),
        lax.all_gather(w_query, "fsdp", axis=0, tiled=True),
        lax.all_gather(w_key, "fsdp", axis=0, tiled=True),
        lax.all_gather(w_value, "fsdp", axis=0, tiled=True),
        lax.all_gather(w_out, "fsdp", axis=0, tiled=True),
        lax.all_gather(norm2_gain, "fsdp", axis=0, tiled=True),
        lax.all_gather(w_gate, "fsdp", axis=0, tiled=True),
        lax.all_gather(w_up, "fsdp", axis=0, tiled=True),
        lax.all_gather(w_down, "fsdp", axis=0, tiled=True),
    )
    gain_one_b, w_q_b, w_k_b, w_v_b, w_o_b, gain_two_b, w_g_b, w_u_b, w_d_b = backward_set
    dy = cotangent[0].astype(jnp.float32)
    dy_low = dy.astype(jnp.bfloat16)
    grad_d = dot_first(hidden, dy_low)
    dhidden = dot_last(dy_low, w_d_b)
    dgate = (dhidden * up_pre * sig_gate * (1.0 + gate_pre * (1.0 - sig_gate))).astype(jnp.bfloat16)
    dup_low = (dhidden * silu_gate).astype(jnp.bfloat16)
    grad_g = dot_first(b, dgate)
    grad_u = dot_first(b, dup_low)
    grad_b = dot_last(dgate, w_g_b) + dot_last(dup_low, w_u_b)
    grad_gain_two, norm_part = norm_back(resid, scale_two, gain_two_b, grad_b)
    grad_resid = dy + norm_part
    resid_low = grad_resid.astype(jnp.bfloat16)
    grad_o = dot_first(head_out, resid_low)
    dheads = dot_last(resid_low, w_o_b).astype(jnp.bfloat16)
    dhead_groups = to_groups(dheads, rows)

    def group_bwd(inputs):
        query_one, key_one, value_one, dout_one, lse_one = inputs
        scores = dot_last(query_one, key_one) * scale
        probs = jnp.exp(jnp.where(visible, scores, -1e30) - lse_one[:, None])
        probs_low = probs.astype(jnp.bfloat16)
        dprobs = dot_last(dout_one, value_one)
        inner = jnp.sum(probs * dprobs, -1, keepdims=True)
        dscores = (probs * (dprobs - inner)).astype(jnp.bfloat16)
        dquery = jnp.dot(dscores, key_one, preferred_element_type=jnp.float32) * scale
        dkey = dot_first(dscores, query_one) * scale
        dvalue = dot_first(probs_low, dout_one)
        return (dquery, dkey, dvalue)

    dquery_groups, dkey_groups, dvalue_groups = lax.map(
        group_bwd, (query_groups, key_groups, value_groups, dhead_groups, log_sums)
    )
    dquery_rot = from_groups(dquery_groups, rows)
    dkey_all = dkey_groups.transpose(1, 0, 2).reshape(length, KVH * HD)
    dvalue_all = dvalue_groups.transpose(1, 0, 2).reshape(length, KVH * HD)
    own_kv = lax.psum_scatter(
        jnp.concatenate([dkey_all, dvalue_all], 1).astype(jnp.bfloat16),
        "ctx",
        scatter_dimension=0,
        tiled=True,
    ).astype(jnp.float32)
    dq = rotate(dquery_rot, own_places, H, -1.0).astype(jnp.bfloat16)
    dk = rotate(own_kv[:, : KVH * HD], own_places, KVH, -1.0).astype(jnp.bfloat16)
    dv_low = own_kv[:, KVH * HD :].astype(jnp.bfloat16)
    grad_q = dot_first(a, dq)
    grad_k = dot_first(a, dk)
    grad_v = dot_first(a, dv_low)
    grad_a = dot_last(dq, w_q_b) + dot_last(dk, w_k_b) + dot_last(dv_low, w_v_b)
    grad_gain_one, input_part = norm_back(x, scale_one, gain_one_b, grad_a)
    grad_x = (grad_resid + input_part).astype(jnp.bfloat16)
    grad_terms = (
        grad_gain_one,
        grad_q,
        grad_k,
        grad_v,
        grad_o,
        grad_gain_two,
        grad_g,
        grad_u,
        grad_d,
    )
    shares = (
        lax.psum_scatter(
            grad_terms[0].astype(jnp.bfloat16), "fsdp", scatter_dimension=0, tiled=True
        ).astype(jnp.float32),
        lax.psum_scatter(
            grad_terms[1].astype(jnp.bfloat16), "fsdp", scatter_dimension=0, tiled=True
        ).astype(jnp.float32),
        lax.psum_scatter(
            grad_terms[2].astype(jnp.bfloat16), "fsdp", scatter_dimension=0, tiled=True
        ).astype(jnp.float32),
        lax.psum_scatter(
            grad_terms[3].astype(jnp.bfloat16), "fsdp", scatter_dimension=0, tiled=True
        ).astype(jnp.float32),
        lax.psum_scatter(
            grad_terms[4].astype(jnp.bfloat16), "fsdp", scatter_dimension=0, tiled=True
        ).astype(jnp.float32),
        lax.psum_scatter(
            grad_terms[5].astype(jnp.bfloat16), "fsdp", scatter_dimension=0, tiled=True
        ).astype(jnp.float32),
        lax.psum_scatter(
            grad_terms[6].astype(jnp.bfloat16), "fsdp", scatter_dimension=0, tiled=True
        ).astype(jnp.float32),
        lax.psum_scatter(
            grad_terms[7].astype(jnp.bfloat16), "fsdp", scatter_dimension=0, tiled=True
        ).astype(jnp.float32),
        lax.psum_scatter(
            grad_terms[8].astype(jnp.bfloat16), "fsdp", scatter_dimension=0, tiled=True
        ).astype(jnp.float32),
    )
    summed = (
        lax.psum(shares[0].astype(jnp.bfloat16), "ctx").astype(jnp.float32),
        lax.psum(shares[1].astype(jnp.bfloat16), "ctx").astype(jnp.float32),
        lax.psum(shares[2].astype(jnp.bfloat16), "ctx").astype(jnp.float32),
        lax.psum(shares[3].astype(jnp.bfloat16), "ctx").astype(jnp.float32),
        lax.psum(shares[4].astype(jnp.bfloat16), "ctx").astype(jnp.float32),
        lax.psum(shares[5].astype(jnp.bfloat16), "ctx").astype(jnp.float32),
        lax.psum(shares[6].astype(jnp.bfloat16), "ctx").astype(jnp.float32),
        lax.psum(shares[7].astype(jnp.bfloat16), "ctx").astype(jnp.float32),
        lax.psum(shares[8].astype(jnp.bfloat16), "ctx").astype(jnp.float32),
    )
    return (
        result[None],
        grad_x[None],
        summed[0],
        summed[1],
        summed[2],
        summed[3],
        summed[4],
        summed[5],
        summed[6],
        summed[7],
        summed[8],
    )


RATIO = H // KVH
PAIR = 2 * RATIO * HD
WIDE = 2 * HD
NT = (((1,), (1,)), ((), ()))
TN = (((0,), (0,)), ((), ()))
NN = (((1,), (0,)), ((), ()))
VMEM = pl.BlockSpec(memory_space=pltpu.VMEM)
HBM = pl.BlockSpec(memory_space=pl.ANY)
ROOM = pltpu.CompilerParams(vmem_limit_bytes=60 * 2**20)


def mm(left, right, dims):
    return lax.dot_general(left, right, dims, preferred_element_type=jnp.float32)


def cost(flops, nbytes, exps=0):
    return pl.CostEstimate(flops=int(flops), bytes_accessed=int(nbytes), transcendentals=int(exps))


def turn(values, cosine, sine):
    lane = lax.broadcasted_iota(jnp.int32, values.shape, 1)
    first = lax.rem(lane, HD) < HD // 2
    partner = jnp.where(first, pltpu.roll(values, WIDE - HD // 2, 1), pltpu.roll(values, HD // 2, 1))
    return values * cosine + partner * sine


def far_lines(z):
    return (z ^ 1, z ^ 2, z ^ 3)


def qkv_kernel(
    at_ref, x_ref, cos_ref, sin_ref, w0_ref, w1_ref, own0_ref, own1_ref, a_ref, at_out_ref, q_ref, kv_ref, gain_ref, w_ref, sem
):
    t, core, z = at_ref[0], at_ref[1], at_ref[2]
    parts, lines, cut, width = w0_ref.shape
    copies = []
    for n, (w, own) in enumerate(((w0_ref, own0_ref), (w1_ref, own1_ref))):
        other = core if n == 0 else 1 - core
        row = pl.multiple_of((2 * z + other) * cut, 16)
        copies.append((own, w_ref.at[pl.ds(row, cut), :]))
        for k, far in enumerate(far_lines(z)):
            row = pl.multiple_of((2 * far + other) * cut, 16)
            for r in range(parts):
                column = pl.multiple_of((t ^ r) * width, WIDE)
                copies.append((w.at[r, k], w_ref.at[pl.ds(row, cut), pl.ds(column, width)]))
    copies = [pltpu.make_async_copy(src, dst, sem.at[i]) for i, (src, dst) in enumerate(copies)]
    for c in copies:
        c.start()
    x = x_ref[...].astype(jnp.float32)
    inv = lax.rsqrt(jnp.mean(x * x, -1, keepdims=True) + EPS)
    for c in copies:
        c.wait()
    first, half = H * HD, KVH * HD
    gains = jnp.transpose(w_ref[:, first + 2 * half : first + 2 * half + WIDE].astype(jnp.float32))[0:8]
    gain_ref[...] = gains
    a = (x * inv * gains[0:1]).astype(jnp.bfloat16)
    a_ref[...] = a
    at_out_ref[...] = jnp.transpose(a)
    for at in range(0, first + 2 * half, 2 * WIDE):
        both = mm(a_ref[...], w_ref[:, at : at + 2 * WIDE], NN)
        for n in range(0, 2 * WIDE, WIDE):
            part, column = both[:, n : n + WIDE], at + n
            if column < first + half:
                part = turn(part, cos_ref[...], sin_ref[...])
            if column < first:
                q_ref[:, column : column + WIDE] = part.astype(jnp.bfloat16)
            elif column < first + 2 * half:
                kv_ref[:, column - first : column - first + WIDE] = part.astype(jnp.bfloat16)


def qkv_project(where, x, cosine, sine, w, own):
    rows, model = x.shape
    width = own[0].shape[1]
    low = jnp.bfloat16
    return pl.pallas_call(
        qkv_kernel,
        in_specs=[pl.BlockSpec(memory_space=pltpu.SMEM)] + [VMEM] * 3 + [HBM] * 4,
        out_specs=[VMEM] * 6,
        out_shape=[
            jax.ShapeDtypeStruct((rows, model), low),
            jax.ShapeDtypeStruct((model, rows), low),
            jax.ShapeDtypeStruct((rows, H * HD), low),
            jax.ShapeDtypeStruct((rows, 2 * KVH * HD), low),
            jax.ShapeDtypeStruct((8, model), jnp.float32),
            jax.ShapeDtypeStruct((model, width), low),
        ],
        scratch_shapes=[pltpu.SemaphoreType.DMA((2 + 2 * 3 * w[0].shape[0],))],
        compiler_params=ROOM,
        cost_estimate=cost(2 * rows * model * width, 2 * (4 * rows * model + 2 * model * width)),
        name="qkv_project",
    )(where, x, cosine, sine, w[0], w[1], own[0], own[1])


def pick_heads(ref, row, group, factor):
    own = lax.broadcasted_iota(jnp.int32, (BLK, WIDE), 1) // HD == group
    out = []
    for n in range(group * RATIO, (group + 1) * RATIO):
        piece = ref[pl.ds(row, BLK), pl.ds(n // 2 * WIDE, WIDE)].astype(jnp.float32) * factor
        if n % 2 != group:
            piece = pltpu.roll(piece, HD, 1)
        out.append(jnp.where(own, piece, 0.0).astype(jnp.bfloat16))
    return jnp.concatenate(out, 0)


def join_heads(groups):
    lane = lax.broadcasted_iota(jnp.int32, (BLK, WIDE), 1)
    parts = []
    for n in range(2 * RATIO):
        group, i = divmod(n, RATIO)
        piece = groups[group][i * BLK : (i + 1) * BLK, :]
        parts.append(piece if n % 2 == group else pltpu.roll(piece, HD, 1))
    return [jnp.where(lane < HD, parts[2 * b], parts[2 * b + 1]) for b in range(RATIO)]


def steps_of(pairs, most):
    return max(u for u in range(1, most + 1) if pairs % u == 0)


def attend_kernel(own_ref, slot_ref, q_ref, k_ref, v_ref, o_ref, lse_ref, s_scr, v_scr, q_scr, m_scr, a_scr):
    rows = RATIO * BLK
    length = v_ref.shape[0]
    pairs = length // BLK + 1
    lane = lax.broadcasted_iota(jnp.int32, (length, WIDE), 1)
    first = own_ref[0] + 1

    def place(t):
        j = jnp.where(t >= first, 1, 0)
        return j, pl.multiple_of(slot_ref[t - j * first] * BLK, BLK)

    outs = [[], []]
    for group in range(2):
        v_scr[...] = jnp.where(lane // HD == group, v_ref[...].astype(jnp.float32), 1.0).astype(jnp.bfloat16)
        for j in range(2):
            q_scr[j] = pick_heads(q_ref, j * BLK, group, HD**-0.5)
        m_scr[...] = jnp.full(m_scr.shape, -jnp.inf, jnp.float32)
        a_scr[...] = jnp.zeros(a_scr.shape, jnp.float32)

        def scores(t, carry):
            j, at = place(t)
            s = mm(q_scr[j], k_ref[pl.ds(at, BLK), :], NT)
            s_scr[t] = s
            m_scr[j] = jnp.maximum(m_scr[j], jnp.maximum(s[:, 0:WIDE], s[:, WIDE : 2 * WIDE]))
            return carry

        lax.fori_loop(0, pairs, scores, 0, unroll=steps_of(pairs, 9))
        for j in range(2):
            m_scr[j] = jnp.broadcast_to(jnp.max(m_scr[j], 1, keepdims=True), (rows, WIDE))

        def mix(t, carry):
            j, at = place(t)
            top = m_scr[j]
            p = jnp.exp(s_scr[t] - jnp.concatenate([top, top], 1)).astype(jnp.bfloat16)
            a_scr[j] += mm(p, v_scr[pl.ds(at, BLK), :], NN)
            return carry

        lax.fori_loop(0, pairs, mix, 0, unroll=steps_of(pairs, 9))
        own = lax.broadcasted_iota(jnp.int32, (rows, WIDE), 1) // HD == group
        for j in range(2):
            acc = a_scr[j]
            total = jnp.where(own, pltpu.roll(acc, HD, 1), acc)
            outs[j].append(acc / total)
            lse_ref[group, j] = jnp.transpose(m_scr[j] + jnp.log(total))[0:1]
    for j in range(2):
        for b, part in enumerate(join_heads(outs[j])):
            o_ref[pl.ds(j * BLK, BLK), pl.ds(b * WIDE, WIDE)] = part.astype(jnp.bfloat16)


def attend(own, slots, q, kv, start, count):
    rows, length = q.shape[0], kv.shape[0]
    nblk = length // BLK
    work = rows * length * H * (nblk + 1) // (2 * nblk) * count // (KVH // 2)
    return pl.pallas_call(
        attend_kernel,
        grid_spec=pltpu.PrefetchScalarGridSpec(
            num_scalar_prefetch=2,
            grid=(count,),
            in_specs=[
                pl.BlockSpec((rows, PAIR), lambda p, *_: (0, p + start)),
                pl.BlockSpec((length, WIDE), lambda p, *_: (0, p + start)),
                pl.BlockSpec((length, WIDE), lambda p, *_: (0, p + start + KVH // 2)),
            ],
            out_specs=[
                pl.BlockSpec((rows, PAIR), lambda p, *_: (0, p)),
                pl.BlockSpec((2, 2, 1, RATIO * BLK), lambda p, *_: (p, 0, 0, 0)),
            ],
            scratch_shapes=[
                pltpu.VMEM((nblk + 1, RATIO * BLK, BLK), jnp.float32),
                pltpu.VMEM((length, WIDE), jnp.bfloat16),
                pltpu.VMEM((2, RATIO * BLK, WIDE), jnp.bfloat16),
                pltpu.VMEM((2, RATIO * BLK, WIDE), jnp.float32),
                pltpu.VMEM((2, RATIO * BLK, WIDE), jnp.float32),
            ],
        ),
        out_shape=[
            jax.ShapeDtypeStruct((rows, PAIR * count), jnp.bfloat16),
            jax.ShapeDtypeStruct((2 * count, 2, 1, RATIO * BLK), jnp.float32),
        ],
        compiler_params=ROOM,
        cost_estimate=cost(4 * 8 * work * HD, 4 * rows * PAIR * count + 4 * length * WIDE * count, work),
        name="attend",
    )(own, slots, q, kv, kv)


def attend_back_kernel(
    own_ref, slot_ref, q_ref, k_ref, v_ref, do_ref, o_ref, lse_ref, cos_ref, sin_ref,
    dq_ref, dkv0_ref, dkv1_ref, dkv2_ref, dkv3_ref, dk_scr, dv_scr, q_scr, do_scr, st_scr, a_scr,
):
    rows = RATIO * BLK
    length = v_ref.shape[0]
    pairs = length // BLK + 1
    dk_scr[...] = jnp.zeros_like(dk_scr)
    dv_scr[...] = jnp.zeros_like(dv_scr)
    first = own_ref[0] + 1
    outs = [[], []]
    for group in range(2):
        for j in range(2):
            q_scr[j] = pick_heads(q_ref, j * BLK, group, HD**-0.5)
            grads = pick_heads(do_ref, j * BLK, group, 1.0)
            do_scr[j] = grads
            mixed = pick_heads(o_ref, j * BLK, group, 1.0)
            inner = jnp.sum(grads.astype(jnp.float32) * mixed.astype(jnp.float32), 1, keepdims=True)
            st_scr[j, 0:1] = jnp.transpose(jnp.broadcast_to(inner, (rows, WIDE)))[0:1]
            st_scr[j, 1:2] = lse_ref[group, j]
        a_scr[...] = jnp.zeros_like(a_scr)

        def step(t, carry):
            j = jnp.where(t >= first, 1, 0)
            at = pl.multiple_of(slot_ref[t - j * first] * BLK, BLK)
            keys = k_ref[pl.ds(at, BLK), :]
            qs, grads = q_scr[j], do_scr[j]
            p = jnp.exp(mm(keys, qs, NT) - st_scr[j, 1:2])
            dp = mm(v_ref[pl.ds(at, BLK), :], grads, NT)
            ds = (p * (dp - st_scr[j, 0:1])).astype(jnp.bfloat16)
            dv_scr[pl.ds(at, BLK), :] += mm(p.astype(jnp.bfloat16), grads, NN)
            dk_scr[pl.ds(at, BLK), :] += mm(ds, qs, NN)
            a_scr[j] += mm(ds, keys, TN)
            return carry

        lax.fori_loop(0, pairs, step, 0, unroll=steps_of(pairs, 3))
        for j in range(2):
            outs[j].append(a_scr[j] * HD**-0.5)
    for j in range(2):
        span = pl.ds(j * BLK, BLK)
        for b, part in enumerate(join_heads(outs[j])):
            dq_ref[span, pl.ds(b * WIDE, WIDE)] = turn(part, cos_ref[span, :], -sin_ref[span, :]).astype(jnp.bfloat16)
    own_rows = length // 4
    for r, ref in enumerate((dkv0_ref, dkv1_ref, dkv2_ref, dkv3_ref)):
        for n, scr in enumerate((dk_scr, dv_scr)):
            ref[n] = scr[pl.ds(r * own_rows, own_rows), :].astype(jnp.bfloat16)


def attend_back(own, slots, q, kv, grads, mixed, lse, cosine, sine, start, count):
    rows, length = q.shape[0], kv.shape[0]
    nblk = length // BLK
    work = rows * length * H * (nblk + 1) // (2 * nblk) * count // (KVH // 2)
    wide = pl.BlockSpec((rows, PAIR), lambda p, *_: (0, p))
    shifted = pl.BlockSpec((rows, PAIR), lambda p, *_: (0, p + start))
    whole = pl.BlockSpec((rows, WIDE), lambda p, *_: (0, 0))
    part = pl.BlockSpec((2, length // 4, WIDE), lambda p, *_: (0, 0, p))
    part_shape = jax.ShapeDtypeStruct((2, length // 4, WIDE * count), jnp.bfloat16)
    return pl.pallas_call(
        attend_back_kernel,
        grid_spec=pltpu.PrefetchScalarGridSpec(
            num_scalar_prefetch=2,
            grid=(count,),
            in_specs=[
                shifted,
                pl.BlockSpec((length, WIDE), lambda p, *_: (0, p + start)),
                pl.BlockSpec((length, WIDE), lambda p, *_: (0, p + start + KVH // 2)),
                shifted,
                wide,
                pl.BlockSpec((2, 2, 1, RATIO * BLK), lambda p, *_: (p, 0, 0, 0)),
                whole,
                whole,
            ],
            out_specs=[wide] + [part] * 4,
            scratch_shapes=[
                pltpu.VMEM((length, WIDE), jnp.float32),
                pltpu.VMEM((length, WIDE), jnp.float32),
                pltpu.VMEM((2, RATIO * BLK, WIDE), jnp.bfloat16),
                pltpu.VMEM((2, RATIO * BLK, WIDE), jnp.bfloat16),
                pltpu.VMEM((2, 8, RATIO * BLK), jnp.float32),
                pltpu.VMEM((2, RATIO * BLK, WIDE), jnp.float32),
            ],
        ),
        out_shape=[jax.ShapeDtypeStruct((rows, PAIR * count), jnp.bfloat16)] + [part_shape] * 4,
        compiler_params=ROOM,
        cost_estimate=cost(10 * 8 * work * HD, 8 * rows * PAIR * count + 8 * length * WIDE * count, work),
        name="attend_back",
    )(own, slots, q, kv, kv, grads, mixed, lse, cosine, sine)


def middle_kernel(
    at_ref, ho_ref, x_ref, dy_ref, gain_ref,
    near0_ref, near1_ref, far0_ref, far1_ref, d0_ref, d1_ref,
    g0_ref, g1_ref, u0_ref, u1_ref, o0_ref, o1_ref, down0_ref, down1_ref,
    out_ref, hot_ref, bt_ref, ht_ref, dg_ref, du_ref, dr_ref, low_ref, dh_ref, gg_ref,
    gu_scr, d_scr, wo_ref, r_scr, b_scr, acc_scr, db_scr, h_scr, gu_sem, o_sem, d_sem,
):
    r = pl.program_id(0)
    count = pl.num_programs(0)
    t, core, z = at_ref[0], at_ref[1], at_ref[2]
    lines, cut, cut_d = near0_ref.shape[1], near0_ref.shape[2], d0_ref.shape[2]
    width = dg_ref.shape[2]
    parts = near0_ref.shape[0] + 1
    o_width = near0_ref.shape[3] - 2 * width
    o_parts = wo_ref.shape[1] // o_width
    cores = (core, 1 - core)
    others = far_lines(z)

    def piece(n, part, k):
        near, far = ((near0_ref, far0_ref), (near1_ref, far1_ref))[n]
        return near.at[part, k] if part < parts - 1 else far.at[k]

    def gu_copies(part, slot):
        out = []
        for n, other in enumerate(cores):
            columns = pl.ds(pl.multiple_of((t ^ part) * width, WIDE), width)
            rows = pl.ds(pl.multiple_of((2 * z + other) * cut, 16), cut)
            for m, ref in enumerate(((g0_ref, u0_ref), (g1_ref, u1_ref))[n]):
                out.append((ref.at[:, columns], gu_scr.at[slot, m, rows, :]))
            for k in range(lines):
                rows = pl.ds(pl.multiple_of((2 * others[k] + other) * cut, 16), cut)
                for m in range(2):
                    out.append((piece(n, part, k).at[:, pl.ds(m * width, width)], gu_scr.at[slot, m, rows, :]))
        return [pltpu.make_async_copy(src, dst, gu_sem.at[slot, i]) for i, (src, dst) in enumerate(out)]

    def o_copies(part):
        out = []
        columns = pl.ds(pl.multiple_of((t ^ part) * o_width, WIDE), o_width)
        for n, other in enumerate(cores):
            for k in range(lines):
                rows = pl.ds(pl.multiple_of((2 * others[k] + other) * cut, 16), cut)
                out.append((piece(n, part, k).at[:, pl.ds(2 * width, o_width)], wo_ref.at[rows, columns]))
        return [pltpu.make_async_copy(src, dst, o_sem.at[part, i]) for i, (src, dst) in enumerate(out)]

    def d_copies():
        out = []
        for n, other in enumerate(cores):
            d, down, o = ((d0_ref, down0_ref, o0_ref), (d1_ref, down1_ref, o1_ref))[n]
            shard = 2 * z + other
            out.append((down, d_scr.at[pl.ds(pl.multiple_of(shard * parts * cut_d, 16), parts * cut_d), :]))
            out.append((o, wo_ref.at[pl.ds(pl.multiple_of(shard * cut, 16), cut), :]))
            for k in range(lines):
                for part in range(parts):
                    row = pl.multiple_of(((2 * others[k] + other) * parts + (t ^ part)) * cut_d, 16)
                    out.append((d.at[part, k], d_scr.at[pl.ds(row, cut_d), :]))
        return [pltpu.make_async_copy(src, dst, d_sem.at[i]) for i, (src, dst) in enumerate(out)]

    slot = lax.rem(r, 2)

    @pl.when(r == 0)
    def _():
        for part in range(parts):

            @pl.when(t ^ part < o_parts)
            def _():
                for c in o_copies(part):
                    c.start()

        for c in d_copies() + gu_copies(0, 0):
            c.start()
        for part in range(parts):

            @pl.when(t ^ part < o_parts)
            def _():
                for c in o_copies(part):
                    c.wait()

        for c in d_copies():
            c.wait()
        resid = x_ref[...].astype(jnp.float32) + mm(ho_ref[...], wo_ref[...], NN)
        r_scr[...] = resid
        inv = lax.rsqrt(jnp.mean(resid * resid, -1, keepdims=True) + EPS)
        b = (resid * inv * gain_ref[1:2]).astype(jnp.bfloat16)
        b_scr[...] = b
        bt_ref[...] = jnp.transpose(b)
        hot_ref[...] = jnp.transpose(ho_ref[...])

    for part in range(parts):

        @pl.when(r == part)
        def _():
            for c in gu_copies(part, part % 2):
                c.wait()
            if part + 1 < parts:
                for c in gu_copies(part + 1, (part + 1) % 2):
                    c.start()

    down = pl.multiple_of((t ^ r) * width, 256)
    for at in range(0, width, 256):
        span = slice(at, at + 256)
        gate = mm(b_scr[...], gu_scr[slot, 0, :, span], NN)
        up = mm(b_scr[...], gu_scr[slot, 1, :, span], NN)
        dhid = mm(dy_ref[...], d_scr[pl.ds(down + at, 256), :], NT)
        sig = jax.nn.sigmoid(gate)
        silu = gate * sig
        hidden = (silu * up).astype(jnp.bfloat16)
        h_scr[:, span] = hidden
        ht_ref[0, span, :] = jnp.transpose(hidden)
        dg_ref[0, :, span] = (dhid * up * sig * (1.0 + gate * (1.0 - sig))).astype(jnp.bfloat16)
        du_ref[0, :, span] = (dhid * silu).astype(jnp.bfloat16)
    model = acc_scr.shape[1]
    for at in range(0, model, 384):
        span = slice(at, at + 384)
        acc = mm(h_scr[...], d_scr[pl.ds(down, width), span], NN)
        db = mm(dg_ref[0], gu_scr[slot, 0, span, :], NT) + mm(du_ref[0], gu_scr[slot, 1, span, :], NT)

        @pl.when(r == 0)
        def _():
            acc_scr[:, span] = acc
            db_scr[:, span] = db

        @pl.when(r > 0)
        def _():
            acc_scr[:, span] += acc
            db_scr[:, span] += db

    @pl.when(r == count - 1)
    def _():
        resid = r_scr[...]
        out_ref[...] = (resid + acc_scr[...]).astype(jnp.bfloat16)
        inv = lax.rsqrt(jnp.mean(resid * resid, -1, keepdims=True) + EPS)
        db = db_scr[...]
        gg_ref[...] = jnp.sum(db * resid * inv, 0, keepdims=True)
        weighted = gain_ref[1:2] * db
        dr = (
            dy_ref[...].astype(jnp.float32)
            + inv * weighted
            - resid * (inv * inv * inv) * jnp.mean(weighted * resid, -1, keepdims=True)
        )
        dr_ref[...] = dr
        low = dr.astype(jnp.bfloat16)
        low_ref[...] = low
        dh_ref[...] = mm(low, wo_ref[...], NT).astype(jnp.bfloat16)


def middle(where, ho, x, dy, gains, near, far, d, own_g, own_u, own_o, own_d):
    rows, model = x.shape
    lines, cut = near[0].shape[1:3]
    count = near[0].shape[0] + 1
    width = own_g[0].shape[1] // count
    once = pl.Buffered(1)
    whole = lambda shape: pl.BlockSpec(shape, lambda r, *_: (0,) * len(shape), pipeline_mode=once)
    act = pl.BlockSpec((1, rows, width), lambda r, *_: (r, 0, 0))
    low = jnp.bfloat16
    return pl.pallas_call(
        middle_kernel,
        grid_spec=pltpu.PrefetchScalarGridSpec(
            num_scalar_prefetch=1,
            grid=(count,),
            in_specs=[whole((rows, H * HD)), whole((rows, model)), whole((rows, model)), whole((8, model))] + [HBM] * 14,
            out_specs=[
                whole((rows, model)), whole((H * HD, rows)), whole((model, rows)),
                pl.BlockSpec((1, width, rows), lambda r, at_ref: (at_ref[0] ^ r, 0, 0)), act, act,
                whole((rows, model)), whole((rows, model)), whole((rows, H * HD)), whole((1, model)),
            ],
            scratch_shapes=[
                pltpu.VMEM((2, 2, 2 * (lines + 1) * cut, width), low),
                pltpu.VMEM((count * width, model), low),
                pltpu.VMEM((H * HD, model), low),
                pltpu.VMEM((rows, model), jnp.float32),
                pltpu.VMEM((rows, model), low),
                pltpu.VMEM((rows, model), jnp.float32),
                pltpu.VMEM((rows, model), jnp.float32),
                pltpu.VMEM((rows, width), low),
                pltpu.SemaphoreType.DMA((2, 4 * (lines + 1))),
                pltpu.SemaphoreType.DMA((count, 2 * lines)),
                pltpu.SemaphoreType.DMA((4 + 2 * count * lines,)),
            ],
        ),
        out_shape=[
            jax.ShapeDtypeStruct((rows, model), low),
            jax.ShapeDtypeStruct((H * HD, rows), low),
            jax.ShapeDtypeStruct((model, rows), low),
            jax.ShapeDtypeStruct((count, width, rows), low),
            jax.ShapeDtypeStruct((count, rows, width), low),
            jax.ShapeDtypeStruct((count, rows, width), low),
            jax.ShapeDtypeStruct((rows, model), jnp.float32),
            jax.ShapeDtypeStruct((rows, model), low),
            jax.ShapeDtypeStruct((rows, H * HD), low),
            jax.ShapeDtypeStruct((1, model), jnp.float32),
        ],
        compiler_params=ROOM,
        cost_estimate=cost(12 * rows * model * width * count + 4 * rows * model * model, 2 * 16 * rows * model + 6 * count * width * model, rows * width * count),
        name="middle",
    )(where, ho, x, dy, gains, *near, *far, *d, *own_g, *own_u, *own_o, *own_d)


def last_kernel(counts, x_ref, gain_ref, dr_ref, w_ref, cos_ref, sin_ref, *refs):
    gx_ref, act_ref, gg_ref = refs[-3:]
    half = KVH * HD
    at = 0
    for n, count in enumerate(counts):
        dq_ref, shares = refs[5 * n], refs[5 * n + 1 : 5 * n + 5]
        act_ref[:, at * PAIR : (at + count) * PAIR] = dq_ref[...]
        for p in range(count):
            span = slice(p * WIDE, (p + 1) * WIDE)
            dk = sum(share[0, :, span].astype(jnp.float32) for share in shares)
            dv = sum(share[1, :, span].astype(jnp.float32) for share in shares)
            column = H * HD + (at + p) * WIDE
            act_ref[:, column : column + WIDE] = turn(dk, cos_ref[...], -sin_ref[...]).astype(jnp.bfloat16)
            act_ref[:, column + half : column + half + WIDE] = dv.astype(jnp.bfloat16)
        at += count
    act_ref[:, H * HD + 2 * half :] = jnp.zeros((x_ref.shape[0], act_ref.shape[1] - H * HD - 2 * half), jnp.bfloat16)
    da = mm(act_ref[:, 0 : H * HD + 2 * half], w_ref[:, 0 : H * HD + 2 * half], NT)
    x = x_ref[...].astype(jnp.float32)
    inv = lax.rsqrt(jnp.mean(x * x, -1, keepdims=True) + EPS)
    gg_ref[...] = jnp.sum(da * x * inv, 0, keepdims=True)
    weighted = gain_ref[0:1] * da
    gx = dr_ref[...] + inv * weighted - x * (inv * inv * inv) * jnp.mean(weighted * x, -1, keepdims=True)
    gx_ref[...] = gx.astype(jnp.bfloat16)


def last(x, gains, dr, w_qkv, cosine, sine, parts, counts):
    rows, model = x.shape
    padded = w_qkv.shape[1]
    return pl.pallas_call(
        functools.partial(last_kernel, counts),
        in_specs=[VMEM] * (6 + len(parts)),
        out_specs=[VMEM] * 3,
        out_shape=[
            jax.ShapeDtypeStruct((rows, model), jnp.bfloat16),
            jax.ShapeDtypeStruct((rows, padded), jnp.bfloat16),
            jax.ShapeDtypeStruct((1, model), jnp.float32),
        ],
        compiler_params=ROOM,
        cost_estimate=cost(2 * rows * model * (H + 2 * KVH) * HD, 10 * rows * model + 2 * model * (H + 2 * KVH) * HD),
        name="last",
    )(x, gains, dr, w_qkv, cosine, sine, *parts)


def gu_products_kernel(l0_ref, l1_ref, g0_ref, g1_ref, u0_ref, u1_ref, g_ref, u_ref):
    @pl.when(pl.program_id(0) == 0)
    def _():
        g_ref[0] = (mm(l0_ref[...], g0_ref[0], NN) + mm(l1_ref[...], g1_ref[0], NN)).astype(jnp.bfloat16)

    @pl.when(pl.program_id(0) == 1)
    def _():
        u_ref[0] = (mm(l0_ref[...], u0_ref[0], NN) + mm(l1_ref[...], u1_ref[0], NN)).astype(jnp.bfloat16)


def gu_products(left, gates, ups, gate_parts, up_parts):
    rows, tokens = left[0].shape
    width = gates[0].shape[2]
    cuts = 2
    piece = width // cuts
    spec = pl.BlockSpec((rows, tokens), lambda m, n, h: (0, 0))
    first = lambda m, v, end: v * (1 - m) + end * m
    then = lambda m, v: v * m

    def gate_at(m, n, h):
        return first(m, n, 1), first(m, h, cuts - 1)

    def up_at(m, n, h):
        return then(m, n), then(m, h)

    def gate_in(m, n, h):
        n, h = gate_at(m, n, h)
        return gate_parts[0] + gate_parts[1] * n, 0, h

    def up_in(m, n, h):
        n, h = up_at(m, n, h)
        return up_parts[0] + up_parts[1] * n, 0, h

    def gate_out(m, n, h):
        n, h = gate_at(m, n, h)
        return n, 0, h

    def up_out(m, n, h):
        n, h = up_at(m, n, h)
        return n, 0, h

    act = lambda index: pl.BlockSpec((1, tokens, piece), index)
    return pl.pallas_call(
        gu_products_kernel,
        grid=(2, 2, cuts),
        in_specs=[spec, spec, act(gate_in), act(gate_in), act(up_in), act(up_in)],
        out_specs=[pl.BlockSpec((1, rows, piece), gate_out), pl.BlockSpec((1, rows, piece), up_out)],
        out_shape=[jax.ShapeDtypeStruct((2, rows, width), jnp.bfloat16)] * 2,
        compiler_params=ROOM,
        cost_estimate=cost(16 * rows * tokens * width, 4 * rows * tokens + 8 * (2 * tokens + rows) * width),
        name="gu_products",
    )(left[0], left[1], gates[0], gates[1], ups[0], ups[1])


def qkv_products_kernel(where_ref, l0_ref, l1_ref, r0_ref, r1_ref, extra_ref, s0_ref, s1_ref, s2_ref, s3_ref):
    r = pl.program_id(0)
    total = mm(l0_ref[...], r0_ref[...], NN) + mm(l1_ref[...], r1_ref[...], NN)
    end = where_ref[0] ^ r == pl.num_programs(0) - 1
    wide = extra_ref.shape[1]
    added = total[:, total.shape[1] - wide :] + jnp.where(end, 1.0, 0.0) * extra_ref[...]
    for n, ref in enumerate((s0_ref, s1_ref, s2_ref, s3_ref)):

        @pl.when(r == n)
        def _():
            ref[:, : total.shape[1] - wide] = total[:, : total.shape[1] - wide].astype(jnp.bfloat16)
            ref[:, total.shape[1] - wide :] = added.astype(jnp.bfloat16)


def qkv_products(where, left, acts, extra):
    rows, tokens = left[0].shape
    width = acts[0].shape[1] // 4
    spec = pl.BlockSpec((rows, tokens), lambda r, *_: (0, 0))
    act = pl.BlockSpec((tokens, width), lambda r, w: (0, w[0] ^ r))
    out = pl.BlockSpec((rows, width), lambda r, *_: (0, 0))
    return pl.pallas_call(
        qkv_products_kernel,
        grid_spec=pltpu.PrefetchScalarGridSpec(
            num_scalar_prefetch=1,
            grid=(4,),
            in_specs=[spec, spec, act, act, pl.BlockSpec(extra.shape, lambda r, *_: (0, 0))],
            out_specs=[out] * 4,
        ),
        out_shape=[jax.ShapeDtypeStruct((rows, width), jnp.bfloat16)] * 4,
        compiler_params=ROOM,
        cost_estimate=cost(16 * rows * tokens * width, 4 * rows * tokens + 8 * (2 * tokens + rows) * width),
        name="qkv_products",
    )(where, left[0], left[1], acts[0], acts[1], extra)


def place_gu_kernel(where_ref, in_ref, g_ref, u_ref):
    g_ref[...] = in_ref[0, 0].astype(jnp.float32)
    u_ref[...] = in_ref[0, 1].astype(jnp.float32)


def place_gu(where, parts):
    count, _, rows, width = parts.shape
    out = pl.BlockSpec((rows, width), lambda n, *_: (0, n))
    return pl.pallas_call(
        place_gu_kernel,
        grid_spec=pltpu.PrefetchScalarGridSpec(
            num_scalar_prefetch=1,
            grid=(count,),
            in_specs=[pl.BlockSpec((1, 2, rows, width), lambda n, where_ref: (where_ref[0] ^ n, 0, 0, 0))],
            out_specs=[out, out],
        ),
        out_shape=[jax.ShapeDtypeStruct((rows, count * width), jnp.float32)] * 2,
        cost_estimate=cost(parts.size, 6 * parts.size),
        name="place_gu",
    )(where, parts)


def place_qkv_kernel(where_ref, in_ref, q_ref, k_ref, v_ref, g_ref):
    t = where_ref[0]
    width = in_ref.shape[2]
    spans = ((q_ref, 0, H * HD), (k_ref, H * HD, KVH * HD), (v_ref, (H + KVH) * HD, KVH * HD))
    for n in range(in_ref.shape[0]):
        part = in_ref[t ^ n].astype(jnp.float32)
        for at in range(0, width, WIDE):
            column = n * width + at
            piece = part[:, at : at + WIDE]
            for ref, first, size in spans:
                if first <= column < first + size:
                    ref[:, column - first : column - first + WIDE] = piece
            if column == (H + 2 * KVH) * HD:
                g_ref[...] = jnp.transpose(piece)[0:8]


def place_qkv(where, parts):
    rows = parts.shape[1]
    wide = lambda columns: jax.ShapeDtypeStruct((rows, columns), jnp.float32)
    return pl.pallas_call(
        place_qkv_kernel,
        in_specs=[pl.BlockSpec(memory_space=pltpu.SMEM), VMEM],
        out_specs=[VMEM] * 4,
        out_shape=[wide(H * HD), wide(KVH * HD), wide(KVH * HD), jax.ShapeDtypeStruct((8, rows), jnp.float32)],
        cost_estimate=cost(parts.size, 6 * parts.size),
        name="place_qkv",
    )(where, parts)


def square(v, r):
    return lax.ppermute(v, "ctx", [(t, t ^ r) for t in range(4)])


def line(v, k):
    return lax.ppermute(v, "fsdp", [(f, f ^ (2 * k)) for f in range(8)])


def other_core(v):
    return lax.ppermute(v, "fsdp", [(f, f ^ 1) for f in range(8)])


def after(v, *others):
    return lax.optimization_barrier((v, *others))[0]


def wide(v):
    return v.astype(jnp.float32)


def low(v):
    return v.astype(jnp.bfloat16)


def line_pieces(v):
    return [line(v, k) for k in (1, 2, 3)]


def hold(parts, *events):
    return [after(v, *events) for v in parts]


def square_near(v):
    return [square(v, 1), square(v, 2)]


def square_far(from_x, from_y):
    half = from_x.shape[0] // 2
    return [square(from_y[:half], 1), square(from_x[half:], 2)]


def square_sum(v):
    half = v.shape[0] // 2 // 16 * 16
    upper, lower = v[:half], v[half:]
    upper, lower = wide(upper) + wide(square(low(upper), 1)), wide(lower) + wide(square(low(lower), 2))
    return jnp.concatenate([upper + wide(square(low(upper), 2)), lower + wide(square(low(lower), 1))])


def lanes(v, core):
    shaped = v.reshape(4, 2, v.shape[0] // 8, v.shape[1])
    pick = lambda c: lax.dynamic_index_in_dim(shaped, c, 1, keepdims=False).reshape(-1, v.shape[1])
    return pick(core), pick(1 - core)


def square_body(
    tokens,
    table,
    norm1_gain,
    w_query,
    w_key,
    w_value,
    w_out,
    norm2_gain,
    w_gate,
    w_up,
    w_down,
    cotangent,
):
    x, dy = tokens[0], cotangent[0]
    rows, model = x.shape
    t = lax.axis_index("ctx")
    f = lax.axis_index("fsdp")
    z, core = f // 2, f % 2
    where = jnp.stack([t, core, z]).astype(jnp.int32)
    cut, hidden_width = w_gate.shape
    cut_d = w_down.shape[0] // 4
    kv_width = 2 * KVH * HD

    slice_of = lambda w: lax.dynamic_slice_in_dim(w, t * (w.shape[1] // 4), w.shape[1] // 4, 1)
    filled = -(-(H * HD + kv_width + WIDE) // (8 * WIDE)) * 8 * WIDE
    gains_own = jnp.stack([norm1_gain, norm2_gain], 1)
    qkv_own = jnp.concatenate([w_query, w_key, w_value, gains_own], 1)
    qkv_own = jnp.pad(qkv_own, ((0, 0), (0, filled - qkv_own.shape[1])))
    out_width = -(-model // (4 * WIDE)) * WIDE
    out_own = jnp.pad(w_out, ((0, 0), (0, 4 * out_width - model)))
    guo_part = jnp.concatenate([slice_of(w_gate), slice_of(w_up), slice_of(out_own)], 1)
    d_part = lax.dynamic_slice_in_dim(w_down, t * cut_d, cut_d, 0)
    rows_of = lambda v: v.reshape(-1, v.shape[-1])
    swap = lambda w: (w, other_core(w))
    rows_of = lambda v: v.reshape(-1, v.shape[-1])
    swap = lambda w: (w, other_core(w))
    qkv_line = line_pieces(slice_of(qkv_own))
    own_qkv = swap(qkv_own)
    own_g, own_u, own_o, own_d = swap(w_gate), swap(w_up), swap(w_out), swap(w_down)
    qkv_rows = jnp.concatenate(qkv_line)
    d_line = line_pieces(after(d_part, *qkv_line))
    qkv_parts = [qkv_rows] + [square(qkv_rows, r) for r in (1, 2, 3)]
    qkv_all = after(jnp.stack(qkv_parts).reshape(4, 3, cut, -1), *d_line)
    guo_line = line_pieces(after(guo_part, *qkv_parts, *d_line))
    qkv_both = swap(qkv_all)

    relative = jnp.arange(4) ^ t
    offsets = jnp.arange(BLK, dtype=jnp.int32)
    ordered = table[relative].reshape(-1)
    own = ordered[:2].astype(jnp.int32)
    slots = jnp.zeros((ordered.shape[0],), jnp.int32).at[ordered].set(jnp.arange(ordered.shape[0], dtype=jnp.int32))
    places = (own[:, None] * BLK + offsets[None, :]).reshape(-1)
    frequency = 10000.0 ** (-(jnp.arange(HD // 2, dtype=jnp.float32) * 2.0 / HD))
    angles = places.astype(jnp.float32)[:, None] * frequency
    cosine = jnp.tile(jnp.cos(angles), (1, 4))
    sine = jnp.sin(angles)
    sine = jnp.concatenate([-sine, sine, -sine, sine], 1)

    early = [w[1] for w in (own_g, own_u, own_o, own_d)]
    a, a_t, q, kv_own, gains, w_qkv = qkv_project(where, after(x, *early), cosine, sine, qkv_both, own_qkv)
    d_rows = after(jnp.concatenate(d_line), *qkv_parts)
    d_near = square_near(d_rows)
    kv_near = square_near(after(kv_own, *d_near))
    kv_far = square_far(*kv_near)
    d_far = square_far(*hold(d_near, *kv_far))
    kv = jnp.concatenate([kv_own, *kv_near, *kv_far])
    mixed_0, lse_0 = attend(own, slots, q, kv, 0, 1)
    guo_rows = jnp.concatenate(hold(guo_line, mixed_0))
    d_far = hold(d_far, mixed_0)
    d = swap(jnp.stack([d_rows, *d_near, jnp.concatenate(d_far)]).reshape(4, 3, cut_d, model))
    guo_near = square_near(guo_rows)
    mixed_1, lse_1 = attend(own, slots, after(q, guo_rows), kv, 1, 2)
    guo_near = hold(guo_near, mixed_1)
    guo_far = square_far(*guo_near)
    near = swap(jnp.stack([guo_rows, *guo_near]).reshape(3, 3, cut, -1))
    far = swap(jnp.concatenate(guo_far).reshape(3, cut, -1))
    mixed = jnp.concatenate([mixed_0, mixed_1], 1)
    out, mixed_t, b_t, hidden_t, dgate, dup, dr, dr_low, dheads, gg2 = middle(
        where, mixed, x, dy, gains, near, far, d, own_g, own_u, own_o, own_d
    )

    gates, ups = swap(dgate), swap(dup)
    b_mine, b_other = lanes(b_t, core)
    left = (b_mine, other_core(b_other))
    g_send, u_send = gu_products(left, gates, ups, (1, 2), (2, 1))
    got_x, got_y = square(g_send, 1), square(u_send, 2)
    scatter = lambda v: lax.psum_scatter(v, "fsdp", scatter_dimension=0, tiled=True)
    grad_d = scatter(low(mm(hidden_t.reshape(-1, rows), after(dy, g_send), NN)))
    grad_o = scatter(low(mm(mixed_t, after(dr_low, g_send), NN)))
    g_keep, u_keep = gu_products(left, gates, ups, (0, 2), (0, 1))

    dq_1, *dkv_1 = attend_back(own, slots, after(q, g_keep), kv, dheads, mixed_1, lse_1, cosine, sine, 1, 2)
    got_x, got_y = hold((got_x, got_y), dq_1)
    pass_y = low(wide(g_keep[1]) + wide(got_x[1]))
    pass_x = low(wide(u_keep[1]) + wide(got_y[1]))
    last_y, last_x = square(pass_y, 2), square(pass_x, 1)
    dkv_1_got = [square(v, r) for r, v in zip((1, 2, 3), dkv_1[1:])]
    dq_0, *dkv_0 = attend_back(own, slots, after(q, pass_x, pass_y), kv, dheads, mixed_0, lse_0, cosine, sine, 0, 1)
    last_y, last_x, *dkv_1_got = hold([last_y, last_x, *dkv_1_got], dq_0)
    rows_at = lambda v, at: lax.dynamic_slice_in_dim(v, at * cut, cut, 0)

    def gu_share(at):
        g = sum(wide(rows_at(v, at)) for v in (g_keep[0], got_x[0], last_y))
        u = sum(wide(rows_at(v, at)) for v in (u_keep[0], got_y[0], last_x))
        return jnp.stack([g, u])

    gu_sends = [low(gu_share(z ^ k)) for k in (1, 2, 3)]
    gu_got = [line(v, k) for k, v in zip((1, 2, 3), gu_sends)]
    dkv_0_got = [square(v, r) for r, v in zip((1, 2, 3), dkv_0[1:])]
    parts = [dq_0, dkv_0[0], *dkv_0_got, dq_1, dkv_1[0], *dkv_1_got]
    grad_x, act, gg1 = last(after(x, *gu_sends), gains, dr, w_qkv, cosine, sine, parts, (1, 2))

    a_mine, a_other = lanes(a_t, core)
    left = (a_mine, other_core(a_other))
    gain_rows = jnp.concatenate([gg1, gg2])
    gain_rows = (gain_rows + other_core(gain_rows)).reshape(2, 4, 2, cut)
    gain_rows = lax.dynamic_index_in_dim(gain_rows, core, 2, keepdims=False).reshape(2, 4 * cut)
    extra = jnp.pad(gain_rows.T, ((0, 0), (0, WIDE - 2)))
    qkv_keep, *qkv_sends = qkv_products(where, left, swap(act), extra)
    shares = [qkv_keep] + [square(v, r) for r, v in zip((1, 2, 3), qkv_sends)]
    gu_got = hold(gu_got, qkv_keep)
    s_gu = low(gu_share(z) + sum(wide(v) for v in gu_got))
    all_gu = jnp.stack([s_gu] + [square(s_gu, r) for r in (1, 2, 3)])
    grad_g, grad_u = place_gu(where, all_gu)
    shares = hold(shares, s_gu)
    qkv_share = lambda at: sum(wide(rows_at(v, at)) for v in shares)
    qkv_sends = [low(qkv_share(z ^ k)) for k in (1, 2, 3)]
    qkv_got = [line(v, k) for k, v in zip((1, 2, 3), qkv_sends)]
    grad_do = square_sum(jnp.concatenate([after(grad_d, *qkv_sends), after(grad_o, *qkv_sends)]))
    s_qkv = low(qkv_share(z) + sum(wide(v) for v in qkv_got))
    all_qkv = jnp.stack([s_qkv] + [square(s_qkv, r) for r in (1, 2, 3)])
    grad_q, grad_k, grad_v, grad_gains = place_qkv(where, all_qkv)
    return (
        out[None],
        grad_x[None],
        grad_gains[0],
        grad_q,
        grad_k,
        grad_v,
        grad_do[4 * cut_d :],
        grad_gains[1],
        grad_g,
        grad_u,
        grad_do[: 4 * cut_d],
    )


def solution(mesh):
    placed = (
        P("fsdp", "ctx", None),
        P(),
        P("fsdp"),
        P("fsdp", None),
        P("fsdp", None),
        P("fsdp", None),
        P("fsdp", None),
        P("fsdp"),
        P("fsdp", None),
        P("fsdp", None),
        P("fsdp", None),
        P("fsdp", "ctx", None),
    )
    square = mesh.shape["ctx"] == 4 and mesh.shape["fsdp"] == 8
    return jax.shard_map(
        square_body if square else plain_body,
        mesh=mesh,
        in_specs=placed,
        out_specs=(
            P("fsdp", "ctx", None),
            P("fsdp", "ctx", None),
            P("fsdp"),
            P("fsdp", None),
            P("fsdp", None),
            P("fsdp", None),
            P("fsdp", None),
            P("fsdp"),
            P("fsdp", None),
            P("fsdp", None),
            P("fsdp", None),
        ),
        check_vma=False,
    )
```

```python
import functools

import jax
import jax.numpy as jnp
from jax import lax
from jax.experimental import pallas as pl
from jax.experimental.pallas import tpu as pltpu
from jax.sharding import PartitionSpec as P

H = 18
KVH = 6
HD = 64
BLK = 256


EPS = 1e-05


def dot_first(left, right):
    return lax.dot_general(
        left, right, (((0,), (0,)), ((), ())), preferred_element_type=jnp.float32
    )


def dot_last(left, right):
    return lax.dot_general(
        left, right, (((1,), (1,)), ((), ())), preferred_element_type=jnp.float32
    )


def rotate(values, places, count, sign):
    split = HD // 2
    shaped = values.reshape(values.shape[0], count, HD)
    frequency = 10000.0 ** (-(jnp.arange(split, dtype=jnp.float32) * 2.0 / HD))
    angles = places.astype(jnp.float32)[:, None] * frequency
    cosine = jnp.cos(angles)[:, None, :]
    sine = jnp.sin(angles)[:, None, :] * sign
    first_half = shaped[..., :split]
    second_half = shaped[..., split:]
    turned = jnp.concatenate(
        [first_half * cosine - second_half * sine, second_half * cosine + first_half * sine], -1
    )
    return turned.reshape(values.shape[0], count * HD)


def norm_back(values, scale_inv, gain, grad_in):
    weighted = gain.astype(jnp.float32) * grad_in
    gain_grad = jnp.sum(grad_in * values * scale_inv, 0)
    grad_out = scale_inv * weighted - values * scale_inv**3 * jnp.mean(
        weighted * values, -1, keepdims=True
    )
    return (gain_grad, grad_out)


def to_groups(values, rows):
    ratio = H // KVH
    return values.reshape(rows, KVH, ratio, HD).transpose(1, 2, 0, 3).reshape(KVH, ratio * rows, HD)


def from_groups(values, rows):
    ratio = H // KVH
    return values.reshape(KVH, ratio, rows, HD).transpose(2, 0, 1, 3).reshape(rows, H * HD)


def plain_body(
    tokens,
    table,
    norm1_gain,
    w_query,
    w_key,
    w_value,
    w_out,
    norm2_gain,
    w_gate,
    w_up,
    w_down,
    cotangent,
):
    ratio = H // KVH
    scale = HD ** (-0.5)
    x = tokens[0].astype(jnp.float32)
    rows = x.shape[0]
    offsets = jnp.arange(BLK, dtype=jnp.int32)
    own_blocks = lax.dynamic_index_in_dim(table, lax.axis_index("ctx"), 0, keepdims=False)
    own_places = (own_blocks[:, None] * BLK + offsets[None, :]).reshape(-1)
    own_ids = jnp.tile(jnp.repeat(own_blocks, BLK), ratio)
    all_ids = jnp.repeat(table.reshape(-1), BLK)
    visible = all_ids[None, :] <= own_ids[:, None]
    forward_set = (
        lax.all_gather(norm1_gain, "fsdp", axis=0, tiled=True),
        lax.all_gather(w_query, "fsdp", axis=0, tiled=True),
        lax.all_gather(w_key, "fsdp", axis=0, tiled=True),
        lax.all_gather(w_value, "fsdp", axis=0, tiled=True),
        lax.all_gather(w_out, "fsdp", axis=0, tiled=True),
        lax.all_gather(norm2_gain, "fsdp", axis=0, tiled=True),
        lax.all_gather(w_gate, "fsdp", axis=0, tiled=True),
        lax.all_gather(w_up, "fsdp", axis=0, tiled=True),
        lax.all_gather(w_down, "fsdp", axis=0, tiled=True),
    )
    gain_one, w_q, w_k, w_v, w_o, gain_two, w_g, w_u, w_d = forward_set
    scale_one = lax.rsqrt(jnp.mean(x * x, -1, keepdims=True) + EPS)
    a = (x * scale_one * gain_one.astype(jnp.float32)).astype(jnp.bfloat16)
    q = jnp.dot(a, w_q, preferred_element_type=jnp.float32)
    k = jnp.dot(a, w_k, preferred_element_type=jnp.float32)
    v = jnp.dot(a, w_v, preferred_element_type=jnp.float32).astype(jnp.bfloat16)
    query_rot = rotate(q, own_places, H, 1.0).astype(jnp.bfloat16)
    key_rot = rotate(k, own_places, KVH, 1.0).astype(jnp.bfloat16)
    key_all, value_all = (
        lax.all_gather(key_rot, "ctx", axis=0, tiled=True),
        lax.all_gather(v, "ctx", axis=0, tiled=True),
    )
    length = key_all.shape[0]
    query_groups = to_groups(query_rot, rows)
    key_groups = key_all.reshape(length, KVH, HD).transpose(1, 0, 2)
    value_groups = value_all.reshape(length, KVH, HD).transpose(1, 0, 2)

    def group_fwd(inputs):
        query_one, key_one, value_one = inputs
        scores = dot_last(query_one, key_one) * scale
        masked = jnp.where(visible, scores, -1e30)
        top = jnp.max(masked, -1, keepdims=True)
        expo = jnp.exp(masked - top)
        total = jnp.sum(expo, -1, keepdims=True)
        probs = (expo / total).astype(jnp.bfloat16)
        mixed = jnp.dot(probs, value_one, preferred_element_type=jnp.float32)
        return (mixed.astype(jnp.bfloat16), (top + jnp.log(total))[:, 0])

    mixed_groups, log_sums = lax.map(group_fwd, (query_groups, key_groups, value_groups))
    head_out = from_groups(mixed_groups, rows)
    resid = x + jnp.dot(head_out, w_o, preferred_element_type=jnp.float32)
    scale_two = lax.rsqrt(jnp.mean(resid * resid, -1, keepdims=True) + EPS)
    b = (resid * scale_two * gain_two.astype(jnp.float32)).astype(jnp.bfloat16)
    gate_pre = jnp.dot(b, w_g, preferred_element_type=jnp.float32)
    up_pre = jnp.dot(b, w_u, preferred_element_type=jnp.float32)
    sig_gate = jax.nn.sigmoid(gate_pre)
    silu_gate = gate_pre * sig_gate
    hidden = (silu_gate * up_pre).astype(jnp.bfloat16)
    result = (resid + jnp.dot(hidden, w_d, preferred_element_type=jnp.float32)).astype(jnp.bfloat16)
    backward_set = (
        lax.all_gather(norm1_gain, "fsdp", axis=0, tiled=True),
        lax.all_gather(w_query, "fsdp", axis=0, tiled=True),
        lax.all_gather(w_key, "fsdp", axis=0, tiled=True),
        lax.all_gather(w_value, "fsdp", axis=0, tiled=True),
        lax.all_gather(w_out, "fsdp", axis=0, tiled=True),
        lax.all_gather(norm2_gain, "fsdp", axis=0, tiled=True),
        lax.all_gather(w_gate, "fsdp", axis=0, tiled=True),
        lax.all_gather(w_up, "fsdp", axis=0, tiled=True),
        lax.all_gather(w_down, "fsdp", axis=0, tiled=True),
    )
    gain_one_b, w_q_b, w_k_b, w_v_b, w_o_b, gain_two_b, w_g_b, w_u_b, w_d_b = backward_set
    dy = cotangent[0].astype(jnp.float32)
    dy_low = dy.astype(jnp.bfloat16)
    grad_d = dot_first(hidden, dy_low)
    dhidden = dot_last(dy_low, w_d_b)
    dgate = (dhidden * up_pre * sig_gate * (1.0 + gate_pre * (1.0 - sig_gate))).astype(jnp.bfloat16)
    dup_low = (dhidden * silu_gate).astype(jnp.bfloat16)
    grad_g = dot_first(b, dgate)
    grad_u = dot_first(b, dup_low)
    grad_b = dot_last(dgate, w_g_b) + dot_last(dup_low, w_u_b)
    grad_gain_two, norm_part = norm_back(resid, scale_two, gain_two_b, grad_b)
    grad_resid = dy + norm_part
    resid_low = grad_resid.astype(jnp.bfloat16)
    grad_o = dot_first(head_out, resid_low)
    dheads = dot_last(resid_low, w_o_b).astype(jnp.bfloat16)
    dhead_groups = to_groups(dheads, rows)

    def group_bwd(inputs):
        query_one, key_one, value_one, dout_one, lse_one = inputs
        scores = dot_last(query_one, key_one) * scale
        probs = jnp.exp(jnp.where(visible, scores, -1e30) - lse_one[:, None])
        probs_low = probs.astype(jnp.bfloat16)
        dprobs = dot_last(dout_one, value_one)
        inner = jnp.sum(probs * dprobs, -1, keepdims=True)
        dscores = (probs * (dprobs - inner)).astype(jnp.bfloat16)
        dquery = jnp.dot(dscores, key_one, preferred_element_type=jnp.float32) * scale
        dkey = dot_first(dscores, query_one) * scale
        dvalue = dot_first(probs_low, dout_one)
        return (dquery, dkey, dvalue)

    dquery_groups, dkey_groups, dvalue_groups = lax.map(
        group_bwd, (query_groups, key_groups, value_groups, dhead_groups, log_sums)
    )
    dquery_rot = from_groups(dquery_groups, rows)
    dkey_all = dkey_groups.transpose(1, 0, 2).reshape(length, KVH * HD)
    dvalue_all = dvalue_groups.transpose(1, 0, 2).reshape(length, KVH * HD)
    own_kv = lax.psum_scatter(
        jnp.concatenate([dkey_all, dvalue_all], 1).astype(jnp.bfloat16),
        "ctx",
        scatter_dimension=0,
        tiled=True,
    ).astype(jnp.float32)
    dq = rotate(dquery_rot, own_places, H, -1.0).astype(jnp.bfloat16)
    dk = rotate(own_kv[:, : KVH * HD], own_places, KVH, -1.0).astype(jnp.bfloat16)
    dv_low = own_kv[:, KVH * HD :].astype(jnp.bfloat16)
    grad_q = dot_first(a, dq)
    grad_k = dot_first(a, dk)
    grad_v = dot_first(a, dv_low)
    grad_a = dot_last(dq, w_q_b) + dot_last(dk, w_k_b) + dot_last(dv_low, w_v_b)
    grad_gain_one, input_part = norm_back(x, scale_one, gain_one_b, grad_a)
    grad_x = (grad_resid + input_part).astype(jnp.bfloat16)
    grad_terms = (
        grad_gain_one,
        grad_q,
        grad_k,
        grad_v,
        grad_o,
        grad_gain_two,
        grad_g,
        grad_u,
        grad_d,
    )
    shares = (
        lax.psum_scatter(
            grad_terms[0].astype(jnp.bfloat16), "fsdp", scatter_dimension=0, tiled=True
        ).astype(jnp.float32),
        lax.psum_scatter(
            grad_terms[1].astype(jnp.bfloat16), "fsdp", scatter_dimension=0, tiled=True
        ).astype(jnp.float32),
        lax.psum_scatter(
            grad_terms[2].astype(jnp.bfloat16), "fsdp", scatter_dimension=0, tiled=True
        ).astype(jnp.float32),
        lax.psum_scatter(
            grad_terms[3].astype(jnp.bfloat16), "fsdp", scatter_dimension=0, tiled=True
        ).astype(jnp.float32),
        lax.psum_scatter(
            grad_terms[4].astype(jnp.bfloat16), "fsdp", scatter_dimension=0, tiled=True
        ).astype(jnp.float32),
        lax.psum_scatter(
            grad_terms[5].astype(jnp.bfloat16), "fsdp", scatter_dimension=0, tiled=True
        ).astype(jnp.float32),
        lax.psum_scatter(
            grad_terms[6].astype(jnp.bfloat16), "fsdp", scatter_dimension=0, tiled=True
        ).astype(jnp.float32),
        lax.psum_scatter(
            grad_terms[7].astype(jnp.bfloat16), "fsdp", scatter_dimension=0, tiled=True
        ).astype(jnp.float32),
        lax.psum_scatter(
            grad_terms[8].astype(jnp.bfloat16), "fsdp", scatter_dimension=0, tiled=True
        ).astype(jnp.float32),
    )
    summed = (
        lax.psum(shares[0].astype(jnp.bfloat16), "ctx").astype(jnp.float32),
        lax.psum(shares[1].astype(jnp.bfloat16), "ctx").astype(jnp.float32),
        lax.psum(shares[2].astype(jnp.bfloat16), "ctx").astype(jnp.float32),
        lax.psum(shares[3].astype(jnp.bfloat16), "ctx").astype(jnp.float32),
        lax.psum(shares[4].astype(jnp.bfloat16), "ctx").astype(jnp.float32),
        lax.psum(shares[5].astype(jnp.bfloat16), "ctx").astype(jnp.float32),
        lax.psum(shares[6].astype(jnp.bfloat16), "ctx").astype(jnp.float32),
        lax.psum(shares[7].astype(jnp.bfloat16), "ctx").astype(jnp.float32),
        lax.psum(shares[8].astype(jnp.bfloat16), "ctx").astype(jnp.float32),
    )
    return (
        result[None],
        grad_x[None],
        summed[0],
        summed[1],
        summed[2],
        summed[3],
        summed[4],
        summed[5],
        summed[6],
        summed[7],
        summed[8],
    )


RATIO = H // KVH
PAIR = 2 * RATIO * HD
WIDE = 2 * HD
NT = (((1,), (1,)), ((), ()))
TN = (((0,), (0,)), ((), ()))
NN = (((1,), (0,)), ((), ()))
VMEM = pl.BlockSpec(memory_space=pltpu.VMEM)
HBM = pl.BlockSpec(memory_space=pl.ANY)
ROOM = pltpu.CompilerParams(vmem_limit_bytes=60 * 2**20)


def mm(left, right, dims):
    return lax.dot_general(left, right, dims, preferred_element_type=jnp.float32)


def cost(flops, nbytes, exps=0):
    return pl.CostEstimate(flops=int(flops), bytes_accessed=int(nbytes), transcendentals=int(exps))


def turn(values, cosine, sine):
    lane = lax.broadcasted_iota(jnp.int32, values.shape, 1)
    first = lax.rem(lane, HD) < HD // 2
    partner = jnp.where(first, pltpu.roll(values, WIDE - HD // 2, 1), pltpu.roll(values, HD // 2, 1))
    return values * cosine + partner * sine


def far_lines(z):
    return (z ^ 1, z ^ 2, z ^ 3)


def qkv_kernel(
    at_ref, x_ref, cos_ref, sin_ref, w0_ref, w1_ref, own0_ref, own1_ref, a_ref, at_out_ref, q_ref, kv_ref, gain_ref, w_ref, sem
):
    t, core, z = at_ref[0], at_ref[1], at_ref[2]
    parts, lines, cut, width = w0_ref.shape
    copies = []
    for n, (w, own) in enumerate(((w0_ref, own0_ref), (w1_ref, own1_ref))):
        other = core if n == 0 else 1 - core
        row = pl.multiple_of((2 * z + other) * cut, 16)
        copies.append((own.at[:, pl.ds(0, parts * width)], w_ref.at[pl.ds(row, cut), :]))
        for k, far in enumerate(far_lines(z)):
            row = pl.multiple_of((2 * far + other) * cut, 16)
            for r in range(parts):
                column = pl.multiple_of((t ^ r) * width, WIDE)
                copies.append((w.at[r, k], w_ref.at[pl.ds(row, cut), pl.ds(column, width)]))
    copies = [pltpu.make_async_copy(src, dst, sem.at[i]) for i, (src, dst) in enumerate(copies)]
    for c in copies:
        c.start()
    x = x_ref[...].astype(jnp.float32)
    inv = lax.rsqrt(jnp.mean(x * x, -1, keepdims=True) + EPS)
    for c in copies:
        c.wait()
    first, half = H * HD, KVH * HD
    gains = jnp.transpose(w_ref[:, first + 2 * half : first + 2 * half + WIDE].astype(jnp.float32))[0:8]
    gain_ref[...] = gains
    a = (x * inv * gains[0:1]).astype(jnp.bfloat16)
    a_ref[...] = a
    at_out_ref[...] = jnp.transpose(a)
    for at in range(0, first + 2 * half, 2 * WIDE):
        both = mm(a_ref[...], w_ref[:, at : at + 2 * WIDE], NN)
        for n in range(0, 2 * WIDE, WIDE):
            part, column = both[:, n : n + WIDE], at + n
            if column < first + half:
                part = turn(part, cos_ref[...], sin_ref[...])
            if column < first:
                q_ref[:, column : column + WIDE] = part.astype(jnp.bfloat16)
            elif column < first + 2 * half:
                kv_ref[:, column - first : column - first + WIDE] = part.astype(jnp.bfloat16)


def qkv_project(where, x, cosine, sine, w, own):
    rows, model = x.shape
    width = 4 * w[0].shape[3]
    low = jnp.bfloat16
    return pl.pallas_call(
        qkv_kernel,
        in_specs=[pl.BlockSpec(memory_space=pltpu.SMEM)] + [VMEM] * 3 + [HBM] * 4,
        out_specs=[VMEM] * 6,
        out_shape=[
            jax.ShapeDtypeStruct((rows, model), low),
            jax.ShapeDtypeStruct((model, rows), low),
            jax.ShapeDtypeStruct((rows, H * HD), low),
            jax.ShapeDtypeStruct((rows, 2 * KVH * HD), low),
            jax.ShapeDtypeStruct((8, model), jnp.float32),
            jax.ShapeDtypeStruct((model, width), low),
        ],
        scratch_shapes=[pltpu.SemaphoreType.DMA((2 + 2 * 3 * w[0].shape[0],))],
        compiler_params=ROOM,
        cost_estimate=cost(2 * rows * model * width, 2 * (4 * rows * model + 2 * model * width)),
        name="qkv_project",
    )(where, x, cosine, sine, w[0], w[1], own[0], own[1])


def pick_heads(ref, row, group, factor):
    own = lax.broadcasted_iota(jnp.int32, (BLK, WIDE), 1) // HD == group
    out = []
    for n in range(group * RATIO, (group + 1) * RATIO):
        piece = ref[pl.ds(row, BLK), pl.ds(n // 2 * WIDE, WIDE)].astype(jnp.float32) * factor
        if n % 2 != group:
            piece = pltpu.roll(piece, HD, 1)
        out.append(jnp.where(own, piece, 0.0).astype(jnp.bfloat16))
    return jnp.concatenate(out, 0)


def join_heads(groups):
    lane = lax.broadcasted_iota(jnp.int32, (BLK, WIDE), 1)
    parts = []
    for n in range(2 * RATIO):
        group, i = divmod(n, RATIO)
        piece = groups[group][i * BLK : (i + 1) * BLK, :]
        parts.append(piece if n % 2 == group else pltpu.roll(piece, HD, 1))
    return [jnp.where(lane < HD, parts[2 * b], parts[2 * b + 1]) for b in range(RATIO)]


def steps_of(pairs, most):
    return max(u for u in range(1, most + 1) if pairs % u == 0)


def attend_kernel(own_ref, slot_ref, q_ref, k_ref, v_ref, o_ref, lse_ref, s_scr, v_scr, q_scr, m_scr, a_scr):
    rows = RATIO * BLK
    length = v_ref.shape[0]
    pairs = length // BLK + 1
    lane = lax.broadcasted_iota(jnp.int32, (length, WIDE), 1)
    first = own_ref[0] + 1

    def place(t):
        j = jnp.where(t >= first, 1, 0)
        return j, pl.multiple_of(slot_ref[t - j * first] * BLK, BLK)

    outs = [[], []]
    for group in range(2):
        v_scr[...] = jnp.where(lane // HD == group, v_ref[...].astype(jnp.float32), 1.0).astype(jnp.bfloat16)
        for j in range(2):
            q_scr[j] = pick_heads(q_ref, j * BLK, group, HD**-0.5)
        m_scr[...] = jnp.full(m_scr.shape, -jnp.inf, jnp.float32)
        a_scr[...] = jnp.zeros(a_scr.shape, jnp.float32)

        def scores(t, carry):
            j, at = place(t)
            s = mm(q_scr[j], k_ref[pl.ds(at, BLK), :], NT)
            s_scr[t] = s
            m_scr[j] = jnp.maximum(m_scr[j], jnp.maximum(s[:, 0:WIDE], s[:, WIDE : 2 * WIDE]))
            return carry

        lax.fori_loop(0, pairs, scores, 0, unroll=steps_of(pairs, 9))
        for j in range(2):
            m_scr[j] = jnp.broadcast_to(jnp.max(m_scr[j], 1, keepdims=True), (rows, WIDE))

        def mix(t, carry):
            j, at = place(t)
            top = m_scr[j]
            p = jnp.exp(s_scr[t] - jnp.concatenate([top, top], 1)).astype(jnp.bfloat16)
            a_scr[j] += mm(p, v_scr[pl.ds(at, BLK), :], NN)
            return carry

        lax.fori_loop(0, pairs, mix, 0, unroll=steps_of(pairs, 9))
        own = lax.broadcasted_iota(jnp.int32, (rows, WIDE), 1) // HD == group
        for j in range(2):
            acc = a_scr[j]
            total = jnp.where(own, pltpu.roll(acc, HD, 1), acc)
            outs[j].append(acc / total)
            lse_ref[group, j] = jnp.transpose(m_scr[j] + jnp.log(total))[0:1]
    for j in range(2):
        for b, part in enumerate(join_heads(outs[j])):
            o_ref[pl.ds(j * BLK, BLK), pl.ds(b * WIDE, WIDE)] = part.astype(jnp.bfloat16)


def attend(own, slots, q, kv, start, count):
    rows, length = q.shape[0], kv.shape[0]
    nblk = length // BLK
    work = rows * length * H * (nblk + 1) // (2 * nblk) * count // (KVH // 2)
    return pl.pallas_call(
        attend_kernel,
        grid_spec=pltpu.PrefetchScalarGridSpec(
            num_scalar_prefetch=2,
            grid=(count,),
            in_specs=[
                pl.BlockSpec((rows, PAIR), lambda p, *_: (0, p + start)),
                pl.BlockSpec((length, WIDE), lambda p, *_: (0, p + start)),
                pl.BlockSpec((length, WIDE), lambda p, *_: (0, p + start + KVH // 2)),
            ],
            out_specs=[
                pl.BlockSpec((rows, PAIR), lambda p, *_: (0, p)),
                pl.BlockSpec((2, 2, 1, RATIO * BLK), lambda p, *_: (p, 0, 0, 0)),
            ],
            scratch_shapes=[
                pltpu.VMEM((nblk + 1, RATIO * BLK, BLK), jnp.float32),
                pltpu.VMEM((length, WIDE), jnp.bfloat16),
                pltpu.VMEM((2, RATIO * BLK, WIDE), jnp.bfloat16),
                pltpu.VMEM((2, RATIO * BLK, WIDE), jnp.float32),
                pltpu.VMEM((2, RATIO * BLK, WIDE), jnp.float32),
            ],
        ),
        out_shape=[
            jax.ShapeDtypeStruct((rows, PAIR * count), jnp.bfloat16),
            jax.ShapeDtypeStruct((2 * count, 2, 1, RATIO * BLK), jnp.float32),
        ],
        compiler_params=ROOM,
        cost_estimate=cost(4 * 8 * work * HD, 4 * rows * PAIR * count + 4 * length * WIDE * count, work),
        name="attend",
    )(own, slots, q, kv, kv)


def attend_back_kernel(
    own_ref, slot_ref, where_ref, q_ref, k_ref, v_ref, do_ref, o_ref, lse_ref, cos_ref, sin_ref, *refs
):
    dq_ref, dkv_ref, dk_scr, dv_scr, q_scr, do_scr, st_scr, a_scr = refs[-8:]
    rows = RATIO * BLK
    length = v_ref.shape[0]
    pairs = length // BLK + 1
    dk_scr[...] = jnp.zeros_like(dk_scr)
    dv_scr[...] = jnp.zeros_like(dv_scr)
    first = own_ref[0] + 1
    outs = [[], []]
    for group in range(2):
        for j in range(2):
            q_scr[j] = pick_heads(q_ref, j * BLK, group, HD**-0.5)
            grads = pick_heads(do_ref, j * BLK, group, 1.0)
            do_scr[j] = grads
            mixed = pick_heads(o_ref, j * BLK, group, 1.0)
            inner = jnp.sum(grads.astype(jnp.float32) * mixed.astype(jnp.float32), 1, keepdims=True)
            st_scr[j, 0:1] = jnp.transpose(jnp.broadcast_to(inner, (rows, WIDE)))[0:1]
            st_scr[j, 1:2] = lse_ref[group, j]
        a_scr[...] = jnp.zeros_like(a_scr)

        def step(t, carry):
            j = jnp.where(t >= first, 1, 0)
            at = pl.multiple_of(slot_ref[t - j * first] * BLK, BLK)
            keys = k_ref[pl.ds(at, BLK), :]
            qs, grads = q_scr[j], do_scr[j]
            p = jnp.exp(mm(keys, qs, NT) - st_scr[j, 1:2])
            dp = mm(v_ref[pl.ds(at, BLK), :], grads, NT)
            ds = (p * (dp - st_scr[j, 0:1])).astype(jnp.bfloat16)
            dv_scr[pl.ds(at, BLK), :] += mm(p.astype(jnp.bfloat16), grads, NN)
            dk_scr[pl.ds(at, BLK), :] += mm(ds, qs, NN)
            a_scr[j] += mm(ds, keys, TN)
            return carry

        lax.fori_loop(0, pairs, step, 0, unroll=steps_of(pairs, 3))
        for j in range(2):
            outs[j].append(a_scr[j] * HD**-0.5)
    for j in range(2):
        span = pl.ds(j * BLK, BLK)
        for b, part in enumerate(join_heads(outs[j])):
            dq_ref[span, pl.ds(b * WIDE, WIDE)] = turn(part, cos_ref[span, :], -sin_ref[span, :]).astype(jnp.bfloat16)
    own_rows = length // 4
    for n, (scr, order) in enumerate(((dk_scr, (1, 3, 0, 2)), (dv_scr, (2, 3, 0, 1)))):
        for i, r in enumerate(order):
            dkv_ref[n, i] = scr[pl.ds(r * own_rows, own_rows), :].astype(jnp.bfloat16)


def attend_back(own, slots, where, q, kv, grads, mixed, lse, cosine, sine, start, count, into=None):
    rows, length = q.shape[0], kv.shape[0]
    nblk = length // BLK
    work = rows * length * H * (nblk + 1) // (2 * nblk) * count // (KVH // 2)
    wide = pl.BlockSpec((rows, PAIR), lambda p, *_: (0, p))
    shifted = pl.BlockSpec((rows, PAIR), lambda p, *_: (0, p + start))
    whole = pl.BlockSpec((rows, WIDE), lambda p, *_: (0, 0))
    part = pl.BlockSpec((2, 4, length // 4, WIDE), lambda p, *_: (0, 0, 0, p + start))
    part_shape = jax.ShapeDtypeStruct((2, 4, length // 4, KVH * HD), jnp.bfloat16)
    more = [] if into is None else [into]
    return pl.pallas_call(
        attend_back_kernel,
        grid_spec=pltpu.PrefetchScalarGridSpec(
            num_scalar_prefetch=3,
            grid=(count,),
            in_specs=[
                shifted,
                pl.BlockSpec((length, WIDE), lambda p, *_: (0, p + start)),
                pl.BlockSpec((length, WIDE), lambda p, *_: (0, p + start + KVH // 2)),
                shifted,
                wide,
                pl.BlockSpec((2, 2, 1, RATIO * BLK), lambda p, *_: (p, 0, 0, 0)),
                whole,
                whole,
            ]
            + [HBM] * len(more),
            out_specs=[wide, part],
            scratch_shapes=[
                pltpu.VMEM((length, WIDE), jnp.float32),
                pltpu.VMEM((length, WIDE), jnp.float32),
                pltpu.VMEM((2, RATIO * BLK, WIDE), jnp.bfloat16),
                pltpu.VMEM((2, RATIO * BLK, WIDE), jnp.bfloat16),
                pltpu.VMEM((2, 8, RATIO * BLK), jnp.float32),
                pltpu.VMEM((2, RATIO * BLK, WIDE), jnp.float32),
            ],
        ),
        out_shape=[jax.ShapeDtypeStruct((rows, PAIR * count), jnp.bfloat16), part_shape],
        input_output_aliases={} if into is None else {11: 1},
        compiler_params=ROOM,
        cost_estimate=cost(1000, 1000) if into is None else cost(80 * work * HD, 8 * rows * PAIR * count + 8 * length * WIDE * count, work),
        name="attend_back",
    )(own, slots, where, q, kv, kv, grads, mixed, lse, cosine, sine, *more)


def middle_kernel(
    at_ref, ho_ref, x_ref, dy_ref, gain_ref,
    near0_ref, near1_ref, far0_ref, far1_ref, p0_ref, p1_ref, o0_ref, o1_ref, all0_ref, all1_ref, down0_ref, down1_ref,
    out_ref, go_ref, bt_ref, gd_ref, gs_ref, gk_ref, us_ref, uk_ref, dr_ref, dh_ref, gg_ref,
    gu_scr, d_scr, wo_ref, r_scr, b_scr, acc_scr, db_scr, h_scr, dg_ref, du_ref, gu_sem, o_sem, d_sem,
):
    r = pl.program_id(0)
    count = pl.num_programs(0)
    t, core, z = at_ref[0], at_ref[1], at_ref[2]
    parts, lines, cut = p0_ref.shape[:3]
    width = dg_ref.shape[1]
    model = wo_ref.shape[1]
    third = width // 2
    cut_d = down0_ref.shape[0] // parts
    first_g = all0_ref.shape[1] - model - 2 * parts * width
    alls, ps = (all0_ref, all1_ref), (p0_ref, p1_ref)
    cores = (core, 1 - core)
    others = far_lines(z)

    def piece(n, part, k):
        near, far = ((near0_ref, far0_ref), (near1_ref, far1_ref))[n]
        return near.at[part, k] if part < parts - 1 else far.at[k]

    def gu_copies(part, slot):
        out = []
        for n, other in enumerate(cores):
            rows = pl.ds(pl.multiple_of((2 * z + other) * cut, 16), cut)
            for m in range(2):
                column = pl.multiple_of(first_g + (m * parts + (t ^ part)) * width, WIDE)
                out.append((alls[n].at[:, pl.ds(column, width)], gu_scr.at[slot, m, rows, :]))
            for k in range(lines):
                rows = pl.ds(pl.multiple_of((2 * others[k] + other) * cut, 16), cut)
                for m in range(2):
                    out.append((piece(n, part, k).at[:, pl.ds(m * width, width)], gu_scr.at[slot, m, rows, :]))
        return [pltpu.make_async_copy(src, dst, gu_sem.at[slot, i]) for i, (src, dst) in enumerate(out)]

    def o_copies():
        out = []
        for n, other in enumerate(cores):
            for line in range(lines + 1):
                rows = pl.ds(pl.multiple_of((2 * line + other) * cut, 16), cut)
                out.append(((o0_ref, o1_ref)[n].at[line], wo_ref.at[rows, :]))
        return [pltpu.make_async_copy(src, dst, o_sem.at[i]) for i, (src, dst) in enumerate(out)]

    def d_copies():
        out = []
        for n, other in enumerate(cores):
            row = pl.multiple_of((2 * z + other) * parts * cut_d, 16)
            out.append(((down0_ref, down1_ref)[n], d_scr.at[pl.ds(row, parts * cut_d), :]))
            for k in range(lines):
                for part in range(parts):
                    row = pl.multiple_of(((2 * others[k] + other) * parts + (t ^ part)) * cut_d, 16)
                    p = ps[n].at[part, k]
                    out.append((p.at[pl.ds(0, cut_d), :], d_scr.at[pl.ds(row, cut_d), pl.ds(0, width)]))
                    for m in range(2):
                        src = p.at[pl.ds(cut_d, cut_d // 2), pl.ds(m * third, third)]
                        row_m = pl.multiple_of(row + m * (cut_d // 2), 16)
                        out.append((src, d_scr.at[pl.ds(row_m, cut_d // 2), pl.ds(width, third)]))
        return [pltpu.make_async_copy(src, dst, d_sem.at[i]) for i, (src, dst) in enumerate(out)]

    slot = lax.rem(r, 2)

    @pl.when(r == 0)
    def _():
        for c in o_copies():
            c.start()
        for c in gu_copies(0, 0) + d_copies():
            c.start()
        for c in o_copies():
            c.wait()
        resid = x_ref[...].astype(jnp.float32) + mm(ho_ref[...], wo_ref[...], NN)
        r_scr[...] = resid
        inv = lax.rsqrt(jnp.mean(resid * resid, -1, keepdims=True) + EPS)
        b = (resid * inv * gain_ref[1:2]).astype(jnp.bfloat16)
        b_scr[...] = b
        turned = jnp.transpose(b)
        for shard in range(2 * (lines + 1)):
            rows = slice(shard * cut, (shard + 1) * cut)
            bt_ref[lax.rem(shard + core, 2), shard // 2 * cut : (shard // 2 + 1) * cut] = turned[rows]

    for part in range(parts):

        @pl.when(r == part)
        def _():
            for c in gu_copies(part, part % 2):
                c.wait()
            if part == 0:
                for c in d_copies():
                    c.wait()
            if part + 1 < parts:
                for c in gu_copies(part + 1, (part + 1) % 2):
                    c.start()

    down = pl.multiple_of((t ^ r) * width, 256)
    for at in range(0, width, 256):
        span = slice(at, at + 256)
        gate = mm(b_scr[...], gu_scr[slot, 0, :, span], NN)
        up = mm(b_scr[...], gu_scr[slot, 1, :, span], NN)
        dhid = mm(dy_ref[...], d_scr[pl.ds(down + at, 256), :], NT)
        sig = jax.nn.sigmoid(gate)
        silu = gate * sig
        hidden = (silu * up).astype(jnp.bfloat16)
        h_scr[:, span] = hidden
        dg_ref[:, span] = (dhid * up * sig * (1.0 + gate * (1.0 - sig))).astype(jnp.bfloat16)
        du_ref[:, span] = (dhid * silu).astype(jnp.bfloat16)
    for n, (g_ref, u_ref) in enumerate(((gk_ref, uk_ref), (gs_ref, uk_ref), (gk_ref, us_ref), (gs_ref, us_ref))):

        @pl.when(r == n)
        def _():
            g_ref[0] = dg_ref[...]
            u_ref[0] = du_ref[...]

    gd_ref[0] = mm(h_scr[...], dy_ref[...], TN).astype(jnp.bfloat16)
    for at in range(0, model, 1152):
        span = slice(at, at + 1152)
        acc = mm(h_scr[...], d_scr[pl.ds(down, width), span], NN)
        db = mm(dg_ref[...], gu_scr[slot, 0, span, :], NT) + mm(du_ref[...], gu_scr[slot, 1, span, :], NT)

        @pl.when(r == 0)
        def _():
            acc_scr[:, span] = acc
            db_scr[:, span] = db

        @pl.when(r > 0)
        def _():
            acc_scr[:, span] += acc
            db_scr[:, span] += db

    @pl.when(r == count - 1)
    def _():
        resid = r_scr[...]
        out_ref[...] = (resid + acc_scr[...]).astype(jnp.bfloat16)
        inv = lax.rsqrt(jnp.mean(resid * resid, -1, keepdims=True) + EPS)
        db = db_scr[...]
        gg_ref[...] = jnp.sum(db * resid * inv, 0, keepdims=True)
        weighted = gain_ref[1:2] * db
        dr = (
            dy_ref[...].astype(jnp.float32)
            + inv * weighted
            - resid * (inv * inv * inv) * jnp.mean(weighted * resid, -1, keepdims=True)
        )
        dr_ref[...] = dr
        low = dr.astype(jnp.bfloat16)
        go_ref[...] = mm(ho_ref[...], low, TN).astype(jnp.bfloat16)
        dh_ref[...] = mm(low, wo_ref[...], NT).astype(jnp.bfloat16)


def middle(where, ho, x, dy, gains, near, far, p, o, own_all, own_d):
    rows, model = x.shape
    lines, cut = near[0].shape[1:3]
    count = near[0].shape[0] + 1
    width = near[0].shape[3] // 2
    once = pl.Buffered(1)
    whole = lambda shape: pl.BlockSpec(shape, lambda r, *_: (0,) * len(shape), pipeline_mode=once)
    act = lambda at: pl.BlockSpec((1, rows, width), lambda r, *_: (at(r), 0, 0))
    low = jnp.bfloat16
    return pl.pallas_call(
        middle_kernel,
        grid_spec=pltpu.PrefetchScalarGridSpec(
            num_scalar_prefetch=1,
            grid=(count,),
            in_specs=[whole((rows, H * HD)), whole((rows, model)), whole((rows, model)), whole((8, model))] + [HBM] * 12,
            out_specs=[
                whole((rows, model)), whole((H * HD, model)), whole((2, model // 2, rows)),
                pl.BlockSpec((1, width, model), lambda r, at_ref: (at_ref[0] ^ r, 0, 0)),
                act(lambda r: r // 3), act(lambda r: r // 2), act(lambda r: r // 3), act(lambda r: (r + 2) // 3),
                whole((rows, model)), whole((rows, H * HD)), whole((1, model)),
            ],
            scratch_shapes=[
                pltpu.VMEM((2, 2, 2 * (lines + 1) * cut, width), low),
                pltpu.VMEM((count * width, model), low),
                pltpu.VMEM((H * HD, model), low),
                pltpu.VMEM((rows, model), jnp.float32),
                pltpu.VMEM((rows, model), low),
                pltpu.VMEM((rows, model), jnp.float32),
                pltpu.VMEM((rows, model), jnp.float32),
                pltpu.VMEM((rows, width), low),
                pltpu.VMEM((rows, width), low),
                pltpu.VMEM((rows, width), low),
                pltpu.SemaphoreType.DMA((2, 4 * (lines + 1))),
                pltpu.SemaphoreType.DMA((2 * (lines + 1),)),
                pltpu.SemaphoreType.DMA((2 + 6 * count * lines,)),
            ],
        ),
        out_shape=[
            jax.ShapeDtypeStruct((rows, model), low),
            jax.ShapeDtypeStruct((H * HD, model), low),
            jax.ShapeDtypeStruct((2, model // 2, rows), low),
            jax.ShapeDtypeStruct((count, width, model), low),
            *[jax.ShapeDtypeStruct((2, rows, width), low)] * 4,
            jax.ShapeDtypeStruct((rows, model), jnp.float32),
            jax.ShapeDtypeStruct((rows, H * HD), low),
            jax.ShapeDtypeStruct((1, model), jnp.float32),
        ],
        compiler_params=ROOM,
        cost_estimate=cost(12 * rows * model * width * count + 4 * rows * model * model, 2 * 16 * rows * model + 6 * count * width * model, rows * width * count),
        name="middle",
    )(where, ho, x, dy, gains, *near, *far, *p, *o, *own_all, *own_d)


def act_kernel(counts, cos_ref, sin_ref, dkv_ref, gx_ref, lasty_ref, gy_ref, lastx_ref, *refs):
    act_ref = refs[-1]
    half = KVH * HD
    at = 0
    for dq_ref, count in zip(refs, counts):
        act_ref[:, at * PAIR : (at + count) * PAIR] = dq_ref[...]
        at += count
    for p in range(at):
        span = slice(p * WIDE, (p + 1) * WIDE)
        dk = sum(v.astype(jnp.float32) for v in (dkv_ref[0, 2, :, span], gx_ref[0, :, span], lasty_ref[:, span]))
        dv = sum(v.astype(jnp.float32) for v in (dkv_ref[1, 2, :, span], gy_ref[0, :, span], lastx_ref[:, span]))
        column = H * HD + p * WIDE
        act_ref[:, column : column + WIDE] = turn(dk, cos_ref[...], -sin_ref[...]).astype(jnp.bfloat16)
        act_ref[:, column + half : column + half + WIDE] = dv.astype(jnp.bfloat16)
    act_ref[:, H * HD + 2 * half :] = jnp.zeros((act_ref.shape[0], act_ref.shape[1] - H * HD - 2 * half), jnp.bfloat16)


def make_act(cosine, sine, shares, parts, counts, width):
    rows = cosine.shape[0]
    return pl.pallas_call(
        functools.partial(act_kernel, counts),
        in_specs=[VMEM] * (7 + len(parts)),
        out_specs=VMEM,
        out_shape=jax.ShapeDtypeStruct((rows, width), jnp.bfloat16),
        compiler_params=ROOM,
        cost_estimate=cost(10 * rows * width, 6 * rows * width),
        name="make_act",
    )(cosine, sine, *shares, *parts)


def last_kernel(x_ref, gain_ref, dr_ref, w_ref, act_ref, gx_ref, gg_ref):
    used = (H + 2 * KVH) * HD
    da = mm(act_ref[:, 0:used], w_ref[:, 0:used], NT)
    x = x_ref[...].astype(jnp.float32)
    inv = lax.rsqrt(jnp.mean(x * x, -1, keepdims=True) + EPS)
    gg_ref[...] = jnp.sum(da * x * inv, 0, keepdims=True)
    weighted = gain_ref[0:1] * da
    gx = dr_ref[...] + inv * weighted - x * (inv * inv * inv) * jnp.mean(weighted * x, -1, keepdims=True)
    gx_ref[...] = gx.astype(jnp.bfloat16)


def last(x, gains, dr, w_qkv, act):
    rows, model = x.shape
    return pl.pallas_call(
        last_kernel,
        in_specs=[VMEM] * 5,
        out_specs=[VMEM] * 2,
        out_shape=[jax.ShapeDtypeStruct((rows, model), jnp.bfloat16), jax.ShapeDtypeStruct((1, model), jnp.float32)],
        compiler_params=ROOM,
        cost_estimate=cost(2 * rows * model * (H + 2 * KVH) * HD, 10 * rows * model + 2 * model * (H + 2 * KVH) * HD),
        name="last",
    )(x, gains, dr, w_qkv, act)


def gu_products_kernel(l0_ref, l1_ref, g0_ref, g1_ref, u0_ref, u1_ref, g_ref, u_ref):
    @pl.when(pl.program_id(0) == 0)
    def _():
        g_ref[0] = (mm(l0_ref[...], g0_ref[0], NN) + mm(l1_ref[...], g1_ref[0], NN)).astype(jnp.bfloat16)

    @pl.when(pl.program_id(0) == 1)
    def _():
        u_ref[0] = (mm(l0_ref[...], u0_ref[0], NN) + mm(l1_ref[...], u1_ref[0], NN)).astype(jnp.bfloat16)


def gu_products(left, gates, ups):
    rows, tokens = left[0].shape
    width = gates[0].shape[2]
    cuts = 1
    piece = width // cuts
    spec = pl.BlockSpec((rows, tokens), lambda m, n, h: (0, 0))
    first = lambda m, v, end: v * (1 - m) + end * m
    then = lambda m, v: v * m

    def gate_at(m, n, h):
        return first(m, n, 1), first(m, h, cuts - 1)

    def up_at(m, n, h):
        return then(m, n), then(m, h)

    def gate_in(m, n, h):
        n, h = gate_at(m, n, h)
        return n, 0, h

    def up_in(m, n, h):
        n, h = up_at(m, n, h)
        return n, 0, h

    def gate_out(m, n, h):
        n, h = gate_at(m, n, h)
        return n, 0, h

    def up_out(m, n, h):
        n, h = up_at(m, n, h)
        return n, 0, h

    act = lambda index: pl.BlockSpec((1, tokens, piece), index)
    return pl.pallas_call(
        gu_products_kernel,
        grid=(2, 2, cuts),
        in_specs=[spec, spec, act(gate_in), act(gate_in), act(up_in), act(up_in)],
        out_specs=[pl.BlockSpec((1, rows, piece), gate_out), pl.BlockSpec((1, rows, piece), up_out)],
        out_shape=[jax.ShapeDtypeStruct((2, rows, width), jnp.bfloat16)] * 2,
        compiler_params=ROOM,
        cost_estimate=cost(16 * rows * tokens * width, 4 * rows * tokens + 8 * (2 * tokens + rows) * width),
        name="gu_products",
    )(left[0], left[1], gates[0], gates[1], ups[0], ups[1])


def qkv_products_kernel(where_ref, l0_ref, l1_ref, r0_ref, r1_ref, s0_ref, s1_ref, s2_ref, s3_ref):
    total = mm(l0_ref[...], r0_ref[...], NN) + mm(l1_ref[...], r1_ref[...], NN)
    for n, ref in enumerate((s0_ref, s1_ref, s2_ref, s3_ref)):

        @pl.when(pl.program_id(0) == n)
        def _():
            ref[...] = total.astype(jnp.bfloat16)


def qkv_products(where, left, acts):
    rows, tokens = left[0].shape
    width = acts[0].shape[1] // 4
    spec = pl.BlockSpec((rows, tokens), lambda r, *_: (0, 0))
    act = pl.BlockSpec((tokens, width), lambda r, w: (0, w[0] ^ r))
    out = pl.BlockSpec((rows, width), lambda r, *_: (0, 0))
    return pl.pallas_call(
        qkv_products_kernel,
        grid_spec=pltpu.PrefetchScalarGridSpec(
            num_scalar_prefetch=1,
            grid=(4,),
            in_specs=[spec, spec, act, act],
            out_specs=[out] * 4,
        ),
        out_shape=[jax.ShapeDtypeStruct((rows, width), jnp.bfloat16)] * 4,
        compiler_params=ROOM,
        cost_estimate=cost(16 * rows * tokens * width, 4 * rows * tokens + 8 * (2 * tokens + rows) * width),
        name="qkv_products",
    )(where, left[0], left[1], acts[0], acts[1])


def place_gu_kernel(where_ref, in_ref, g_ref, u_ref):
    g_ref[...] = in_ref[0, 0].astype(jnp.float32)
    u_ref[...] = in_ref[0, 1].astype(jnp.float32)


def place_gu(where, parts):
    count, _, rows, width = parts.shape
    out = pl.BlockSpec((rows, width), lambda n, *_: (0, n))
    return pl.pallas_call(
        place_gu_kernel,
        grid_spec=pltpu.PrefetchScalarGridSpec(
            num_scalar_prefetch=1,
            grid=(count,),
            in_specs=[pl.BlockSpec((1, 2, rows, width), lambda n, where_ref: (where_ref[0] ^ n, 0, 0, 0))],
            out_specs=[out, out],
        ),
        out_shape=[jax.ShapeDtypeStruct((rows, count * width), jnp.float32)] * 2,
        cost_estimate=cost(parts.size, 6 * parts.size),
        name="place_gu",
    )(where, parts)


def place_qkv_kernel(where_ref, in_ref, q_ref, k_ref, v_ref):
    t = where_ref[0]
    width = in_ref.shape[2]
    spans = ((q_ref, 0, H * HD), (k_ref, H * HD, KVH * HD), (v_ref, (H + KVH) * HD, KVH * HD))
    for n in range(in_ref.shape[0]):
        part = in_ref[t ^ n].astype(jnp.float32)
        for at in range(0, width, WIDE):
            column = n * width + at
            piece = part[:, at : at + WIDE]
            for ref, first, size in spans:
                if first <= column < first + size:
                    ref[:, column - first : column - first + WIDE] = piece


def place_qkv(where, parts):
    rows = parts.shape[1]
    wide = lambda columns: jax.ShapeDtypeStruct((rows, columns), jnp.float32)
    return pl.pallas_call(
        place_qkv_kernel,
        in_specs=[pl.BlockSpec(memory_space=pltpu.SMEM), VMEM],
        out_specs=[VMEM] * 3,
        out_shape=[wide(H * HD), wide(KVH * HD), wide(KVH * HD)],
        cost_estimate=cost(parts.size, 6 * parts.size),
        name="place_qkv",
    )(where, parts)


def square(v, r):
    return lax.ppermute(v, "ctx", [(t, t ^ r) for t in range(4)])


def line(v, k):
    return lax.ppermute(v, "fsdp", [(f, f ^ (2 * k)) for f in range(8)])


def other_core(v):
    return lax.ppermute(v, "fsdp", [(f, f ^ 1) for f in range(8)])


def after(v, *others):
    return lax.optimization_barrier((v, *others))[0]


def wide(v):
    return v.astype(jnp.float32)


def low(v):
    return v.astype(jnp.bfloat16)


LINES = [[0, 2, 4, 6], [1, 3, 5, 7]]


def line_all(v):
    return lax.all_to_all(v, "fsdp", 0, 0, axis_index_groups=LINES, tiled=True)


def line_spread(v):
    return line_all(jnp.broadcast_to(v[None], (4, *v.shape)))


def far_pieces(got, z):
    return [lax.dynamic_index_in_dim(got, z ^ k, 0, keepdims=False) for k in (1, 2, 3)]


def hold(parts, *events):
    return [after(v, *events) for v in parts]


def square_near(v):
    return [square(v, 1), square(v, 2)]


def square_far(from_x, from_y):
    half = from_x.shape[0] // 2
    return [square(from_y[:half], 1), square(from_x[half:], 2)]


def lanes(v, core):
    shaped = v.reshape(4, 2, v.shape[0] // 8, v.shape[1])
    pick = lambda c: lax.dynamic_index_in_dim(shaped, c, 1, keepdims=False).reshape(-1, v.shape[1])
    return pick(core), pick(1 - core)


def square_body(
    tokens,
    table,
    norm1_gain,
    w_query,
    w_key,
    w_value,
    w_out,
    norm2_gain,
    w_gate,
    w_up,
    w_down,
    cotangent,
):
    x, dy = tokens[0], cotangent[0]
    rows, model = x.shape
    t = lax.axis_index("ctx")
    f = lax.axis_index("fsdp")
    z, core = f // 2, f % 2
    where = jnp.stack([t, core, z]).astype(jnp.int32)
    cut, hidden_width = w_gate.shape
    cut_d = w_down.shape[0] // 4
    kv_width = 2 * KVH * HD

    relative = jnp.arange(4) ^ t
    offsets = jnp.arange(BLK, dtype=jnp.int32)
    ordered = table[relative].reshape(-1)
    own = ordered[:2].astype(jnp.int32)
    slots = jnp.zeros((ordered.shape[0],), jnp.int32).at[ordered].set(jnp.arange(ordered.shape[0], dtype=jnp.int32))
    places = (own[:, None] * BLK + offsets[None, :]).reshape(-1)
    frequency = 10000.0 ** (-(jnp.arange(HD // 2, dtype=jnp.float32) * 2.0 / HD))
    angles = places.astype(jnp.float32)[:, None] * frequency
    cosine = jnp.tile(jnp.cos(angles), (1, 4))
    sine = jnp.sin(angles)
    sine = jnp.concatenate([-sine, sine, -sine, sine], 1)

    slice_of = lambda w: lax.dynamic_slice_in_dim(w, t * (w.shape[1] // 4), w.shape[1] // 4, 1)
    filled = -(-(H * HD + kv_width + WIDE) // (8 * WIDE)) * 8 * WIDE
    gains_own = jnp.stack([norm1_gain, norm2_gain], 1)
    qkv_own = jnp.concatenate([w_query, w_key, w_value, gains_own], 1)
    qkv_own = jnp.pad(qkv_own, ((0, 0), (0, filled - qkv_own.shape[1])))
    gu_part = jnp.concatenate([slice_of(w_gate), slice_of(w_up)], 1)
    width = hidden_width // 4
    d_part = lax.dynamic_slice_in_dim(w_down, t * cut_d, cut_d, 0)
    d_below = jnp.concatenate([d_part[: cut_d // 2, width:], d_part[cut_d // 2 :, width:]], 1)
    d_part = jnp.concatenate([d_part[:, :width], d_below])
    swap = lambda w: (w, other_core(w))
    qkv_line = line_spread(slice_of(qkv_own))
    own_all = swap(jnp.concatenate([qkv_own, w_gate, w_up, w_out], 1))
    own_d = swap(w_down)
    qkv_line = after(qkv_line, cosine, sine, slots, gu_part, d_part)
    qkv_rows = jnp.concatenate(far_pieces(qkv_line, z))
    d_line = line_spread(after(d_part, qkv_line))
    qkv_parts = [qkv_rows] + [square(qkv_rows, r) for r in (1, 2, 3)]
    qkv_all = after(jnp.stack(qkv_parts).reshape(4, 3, cut, -1), own_all[1], own_d[1], d_line)
    qkv_both = swap(qkv_all)

    a, a_t, q, kv_own, gains, w_qkv = qkv_project(where, x, cosine, sine, qkv_both, own_all)
    kv_near = square_near(kv_own)
    gu_line = line_spread(after(gu_part, d_line))
    kv_far = square_far(*kv_near)
    d_rows = jnp.concatenate(far_pieces(d_line, z))
    d_rest = [square(after(d_rows, *kv_far), r) for r in (1, 2, 3)]
    kv = jnp.concatenate([kv_own, *kv_near, *kv_far])
    mixed_0, lse_0 = attend(own, slots, q, kv, 0, 1)
    gu_line = after(gu_line, mixed_0)
    gu_rows = jnp.concatenate(far_pieces(gu_line, z))
    gu_near = square_near(gu_rows)
    o_line = line_spread(after(w_out, gu_line))
    d_rest = hold(d_rest, mixed_0)
    mixed_1, lse_1 = attend(own, slots, after(q, gu_rows, *d_rest), kv, 1, 2)
    o_line = after(o_line, mixed_1)
    gu_near = hold(gu_near, o_line)
    gu_far = square_far(*gu_near)
    o = swap(o_line)
    near = swap(jnp.stack([gu_rows, *gu_near]).reshape(3, 3, cut, -1))
    d = swap(jnp.stack([d_rows, *d_rest]).reshape(4, 3, cut, -1))
    far = swap(jnp.concatenate(gu_far).reshape(3, cut, -1))
    mixed = jnp.concatenate([mixed_0, mixed_1], 1)
    out, grad_o, b_t, grad_d, g_s, g_k, u_s, u_k, dr, dheads, gg2 = middle(
        where, mixed, x, dy, gains, near, far, d, o, own_all, own_d
    )

    left = (b_t[0], other_core(b_t[1]))
    g_send, u_send = gu_products(left, swap(g_s), swap(u_s))
    got_x, got_y = square(g_send, 1), square(u_send, 2)
    scatter = lambda v: lax.psum_scatter(v, "fsdp", scatter_dimension=0, tiled=True)
    grad_d, grad_o = scatter(grad_d.reshape(-1, model)), scatter(grad_o)
    kept = [(after(v[0], g_send), v[1]) for v in (swap(g_k), swap(u_k))]
    g_keep, u_keep = gu_products(left, *kept)

    dq_1, dkv = attend_back(own, slots, where, after(q, g_keep), kv, dheads, mixed_1, lse_1, cosine, sine, 1, 2)
    got_x, got_y = hold((got_x, got_y), dq_1)
    pass_y = low(wide(g_keep[1]) + wide(got_x[1]))
    pass_x = low(wide(u_keep[1]) + wide(got_y[1]))
    last_y, last_x = square(pass_y, 2), square(pass_x, 1)
    dq_0, dkv = attend_back(
        own, slots, where, after(q, pass_x, pass_y), kv, dheads, mixed_0, lse_0, cosine, sine, 0, 1, dkv
    )
    last_y, last_x = hold([last_y, last_x], dq_0)
    dkv = after(dkv, last_y, last_x)
    kv_x, kv_y = square(dkv[0, :2], 1), square(dkv[1, :2], 2)
    rows_at = lambda v, at: v[at * cut : (at + 1) * cut]

    def gu_share(at):
        g = sum(wide(rows_at(v, at)) for v in (g_keep[0], got_x[0], last_y))
        u = sum(wide(rows_at(v, at)) for v in (u_keep[0], got_y[0], last_x))
        return jnp.stack([g, u])

    gu_sends = jnp.stack([low(gu_share(at)) for at in range(4)])
    gu_got = line_all(gu_sends)
    kv_x, kv_y = hold([kv_x, kv_y], gu_sends)
    kv_last_y = square(low(wide(dkv[0, 3]) + wide(kv_x[1])), 2)
    kv_last_x = square(low(wide(dkv[1, 3]) + wide(kv_y[1])), 1)
    act = make_act(cosine, sine, [dkv, kv_x, kv_last_y, kv_y, kv_last_x], [dq_0, dq_1], (1, 2), filled)
    grad_do = jnp.concatenate([grad_d, grad_o])
    half = grad_do.shape[0] // 32 * 16
    do_upper, do_lower = hold([grad_do[:half], grad_do[half:]], kv_last_x, kv_last_y)
    do_got = [square(do_upper, 1), square(do_lower, 2)]
    acts = swap(act)

    a_mine, a_other = lanes(a_t, core)
    left = (a_mine, other_core(a_other))
    qkv_keep, *qkv_sends = qkv_products(where, left, acts)
    shares = [qkv_keep] + [square(v, r) for r, v in zip((1, 2, 3), qkv_sends)]
    do_got = hold(do_got, qkv_keep)
    do_upper, do_lower = low(wide(do_upper) + wide(do_got[0])), low(wide(do_lower) + wide(do_got[1]))
    do_got = [square(do_upper, 2), square(do_lower, 1)]
    grad_x, gg1 = last(after(x, do_upper, do_lower), gains, dr, w_qkv, act)
    do_got = hold(do_got, gg1)
    shares = hold(shares, gg1, *do_got)
    qkv_share = lambda at: sum(wide(rows_at(v, at)) for v in shares)
    qkv_sends = jnp.stack([low(qkv_share(at)) for at in range(4)])
    gu_got = after(gu_got, gg1)
    qkv_got = line_all(after(qkv_sends, gu_got))
    s_gu = low(sum(wide(gu_got[n]) for n in range(4)))
    all_gu = [s_gu] + [square(after(s_gu, qkv_sends), r) for r in (1, 2, 3)]
    gain_rows = after(jnp.concatenate([gg1, gg2]), qkv_sends)
    gain_rows += other_core(gain_rows)
    gain_rows += square(gain_rows, 1)
    gain_rows += square(gain_rows, 2)
    gain_rows += line(gain_rows, 1)
    gain_rows += line(gain_rows, 2)
    gain_rows = lax.dynamic_slice_in_dim(gain_rows, f * cut, cut, 1)
    all_gu = hold(all_gu, gain_rows)
    qkv_got = after(qkv_got, gain_rows, *all_gu)
    s_qkv = low(sum(wide(qkv_got[n]) for n in range(4)))
    all_qkv = [s_qkv] + [square(s_qkv, r) for r in (1, 2, 3)]
    grad_do = jnp.concatenate([wide(do_upper) + wide(do_got[0]), wide(do_lower) + wide(do_got[1])])
    grad_g, grad_u = place_gu(where, jnp.stack(hold(all_gu, s_qkv)))
    grad_q, grad_k, grad_v = place_qkv(where, jnp.stack(all_qkv))
    return (
        out[None],
        grad_x[None],
        gain_rows[0],
        grad_q,
        grad_k,
        grad_v,
        grad_do[4 * cut_d :],
        gain_rows[1],
        grad_g,
        grad_u,
        grad_do[: 4 * cut_d],
    )


def solution(mesh):
    placed = (
        P("fsdp", "ctx", None),
        P(),
        P("fsdp"),
        P("fsdp", None),
        P("fsdp", None),
        P("fsdp", None),
        P("fsdp", None),
        P("fsdp"),
        P("fsdp", None),
        P("fsdp", None),
        P("fsdp", None),
        P("fsdp", "ctx", None),
    )
    square = mesh.shape["ctx"] == 4 and mesh.shape["fsdp"] == 8
    return jax.shard_map(
        square_body if square else plain_body,
        mesh=mesh,
        in_specs=placed,
        out_specs=(
            P("fsdp", "ctx", None),
            P("fsdp", "ctx", None),
            P("fsdp"),
            P("fsdp", None),
            P("fsdp", None),
            P("fsdp", None),
            P("fsdp", None),
            P("fsdp"),
            P("fsdp", None),
            P("fsdp", None),
            P("fsdp", None),
        ),
        check_vma=False,
    )
```

```python
import functools

import jax
import jax.numpy as jnp
from jax import lax
from jax.experimental import pallas as pl
from jax.experimental.pallas import tpu as pltpu
from jax.sharding import PartitionSpec as P

H = 18
KVH = 6
HD = 64
BLK = 256


EPS = 1e-05


def dot_first(left, right):
    return lax.dot_general(
        left, right, (((0,), (0,)), ((), ())), preferred_element_type=jnp.float32
    )


def dot_last(left, right):
    return lax.dot_general(
        left, right, (((1,), (1,)), ((), ())), preferred_element_type=jnp.float32
    )


def rotate(values, places, count, sign):
    split = HD // 2
    shaped = values.reshape(values.shape[0], count, HD)
    frequency = 10000.0 ** (-(jnp.arange(split, dtype=jnp.float32) * 2.0 / HD))
    angles = places.astype(jnp.float32)[:, None] * frequency
    cosine = jnp.cos(angles)[:, None, :]
    sine = jnp.sin(angles)[:, None, :] * sign
    first_half = shaped[..., :split]
    second_half = shaped[..., split:]
    turned = jnp.concatenate(
        [first_half * cosine - second_half * sine, second_half * cosine + first_half * sine], -1
    )
    return turned.reshape(values.shape[0], count * HD)


def norm_back(values, scale_inv, gain, grad_in):
    weighted = gain.astype(jnp.float32) * grad_in
    gain_grad = jnp.sum(grad_in * values * scale_inv, 0)
    grad_out = scale_inv * weighted - values * scale_inv**3 * jnp.mean(
        weighted * values, -1, keepdims=True
    )
    return (gain_grad, grad_out)


def to_groups(values, rows):
    ratio = H // KVH
    return values.reshape(rows, KVH, ratio, HD).transpose(1, 2, 0, 3).reshape(KVH, ratio * rows, HD)


def from_groups(values, rows):
    ratio = H // KVH
    return values.reshape(KVH, ratio, rows, HD).transpose(2, 0, 1, 3).reshape(rows, H * HD)


def plain_body(
    tokens,
    table,
    norm1_gain,
    w_query,
    w_key,
    w_value,
    w_out,
    norm2_gain,
    w_gate,
    w_up,
    w_down,
    cotangent,
):
    ratio = H // KVH
    scale = HD ** (-0.5)
    x = tokens[0].astype(jnp.float32)
    rows = x.shape[0]
    offsets = jnp.arange(BLK, dtype=jnp.int32)
    own_blocks = lax.dynamic_index_in_dim(table, lax.axis_index("ctx"), 0, keepdims=False)
    own_places = (own_blocks[:, None] * BLK + offsets[None, :]).reshape(-1)
    own_ids = jnp.tile(jnp.repeat(own_blocks, BLK), ratio)
    all_ids = jnp.repeat(table.reshape(-1), BLK)
    visible = all_ids[None, :] <= own_ids[:, None]
    forward_set = (
        lax.all_gather(norm1_gain, "fsdp", axis=0, tiled=True),
        lax.all_gather(w_query, "fsdp", axis=0, tiled=True),
        lax.all_gather(w_key, "fsdp", axis=0, tiled=True),
        lax.all_gather(w_value, "fsdp", axis=0, tiled=True),
        lax.all_gather(w_out, "fsdp", axis=0, tiled=True),
        lax.all_gather(norm2_gain, "fsdp", axis=0, tiled=True),
        lax.all_gather(w_gate, "fsdp", axis=0, tiled=True),
        lax.all_gather(w_up, "fsdp", axis=0, tiled=True),
        lax.all_gather(w_down, "fsdp", axis=0, tiled=True),
    )
    gain_one, w_q, w_k, w_v, w_o, gain_two, w_g, w_u, w_d = forward_set
    scale_one = lax.rsqrt(jnp.mean(x * x, -1, keepdims=True) + EPS)
    a = (x * scale_one * gain_one.astype(jnp.float32)).astype(jnp.bfloat16)
    q = jnp.dot(a, w_q, preferred_element_type=jnp.float32)
    k = jnp.dot(a, w_k, preferred_element_type=jnp.float32)
    v = jnp.dot(a, w_v, preferred_element_type=jnp.float32).astype(jnp.bfloat16)
    query_rot = rotate(q, own_places, H, 1.0).astype(jnp.bfloat16)
    key_rot = rotate(k, own_places, KVH, 1.0).astype(jnp.bfloat16)
    key_all, value_all = (
        lax.all_gather(key_rot, "ctx", axis=0, tiled=True),
        lax.all_gather(v, "ctx", axis=0, tiled=True),
    )
    length = key_all.shape[0]
    query_groups = to_groups(query_rot, rows)
    key_groups = key_all.reshape(length, KVH, HD).transpose(1, 0, 2)
    value_groups = value_all.reshape(length, KVH, HD).transpose(1, 0, 2)

    def group_fwd(inputs):
        query_one, key_one, value_one = inputs
        scores = dot_last(query_one, key_one) * scale
        masked = jnp.where(visible, scores, -1e30)
        top = jnp.max(masked, -1, keepdims=True)
        expo = jnp.exp(masked - top)
        total = jnp.sum(expo, -1, keepdims=True)
        probs = (expo / total).astype(jnp.bfloat16)
        mixed = jnp.dot(probs, value_one, preferred_element_type=jnp.float32)
        return (mixed.astype(jnp.bfloat16), (top + jnp.log(total))[:, 0])

    mixed_groups, log_sums = lax.map(group_fwd, (query_groups, key_groups, value_groups))
    head_out = from_groups(mixed_groups, rows)
    resid = x + jnp.dot(head_out, w_o, preferred_element_type=jnp.float32)
    scale_two = lax.rsqrt(jnp.mean(resid * resid, -1, keepdims=True) + EPS)
    b = (resid * scale_two * gain_two.astype(jnp.float32)).astype(jnp.bfloat16)
    gate_pre = jnp.dot(b, w_g, preferred_element_type=jnp.float32)
    up_pre = jnp.dot(b, w_u, preferred_element_type=jnp.float32)
    sig_gate = jax.nn.sigmoid(gate_pre)
    silu_gate = gate_pre * sig_gate
    hidden = (silu_gate * up_pre).astype(jnp.bfloat16)
    result = (resid + jnp.dot(hidden, w_d, preferred_element_type=jnp.float32)).astype(jnp.bfloat16)
    backward_set = (
        lax.all_gather(norm1_gain, "fsdp", axis=0, tiled=True),
        lax.all_gather(w_query, "fsdp", axis=0, tiled=True),
        lax.all_gather(w_key, "fsdp", axis=0, tiled=True),
        lax.all_gather(w_value, "fsdp", axis=0, tiled=True),
        lax.all_gather(w_out, "fsdp", axis=0, tiled=True),
        lax.all_gather(norm2_gain, "fsdp", axis=0, tiled=True),
        lax.all_gather(w_gate, "fsdp", axis=0, tiled=True),
        lax.all_gather(w_up, "fsdp", axis=0, tiled=True),
        lax.all_gather(w_down, "fsdp", axis=0, tiled=True),
    )
    gain_one_b, w_q_b, w_k_b, w_v_b, w_o_b, gain_two_b, w_g_b, w_u_b, w_d_b = backward_set
    dy = cotangent[0].astype(jnp.float32)
    dy_low = dy.astype(jnp.bfloat16)
    grad_d = dot_first(hidden, dy_low)
    dhidden = dot_last(dy_low, w_d_b)
    dgate = (dhidden * up_pre * sig_gate * (1.0 + gate_pre * (1.0 - sig_gate))).astype(jnp.bfloat16)
    dup_low = (dhidden * silu_gate).astype(jnp.bfloat16)
    grad_g = dot_first(b, dgate)
    grad_u = dot_first(b, dup_low)
    grad_b = dot_last(dgate, w_g_b) + dot_last(dup_low, w_u_b)
    grad_gain_two, norm_part = norm_back(resid, scale_two, gain_two_b, grad_b)
    grad_resid = dy + norm_part
    resid_low = grad_resid.astype(jnp.bfloat16)
    grad_o = dot_first(head_out, resid_low)
    dheads = dot_last(resid_low, w_o_b).astype(jnp.bfloat16)
    dhead_groups = to_groups(dheads, rows)

    def group_bwd(inputs):
        query_one, key_one, value_one, dout_one, lse_one = inputs
        scores = dot_last(query_one, key_one) * scale
        probs = jnp.exp(jnp.where(visible, scores, -1e30) - lse_one[:, None])
        probs_low = probs.astype(jnp.bfloat16)
        dprobs = dot_last(dout_one, value_one)
        inner = jnp.sum(probs * dprobs, -1, keepdims=True)
        dscores = (probs * (dprobs - inner)).astype(jnp.bfloat16)
        dquery = jnp.dot(dscores, key_one, preferred_element_type=jnp.float32) * scale
        dkey = dot_first(dscores, query_one) * scale
        dvalue = dot_first(probs_low, dout_one)
        return (dquery, dkey, dvalue)

    dquery_groups, dkey_groups, dvalue_groups = lax.map(
        group_bwd, (query_groups, key_groups, value_groups, dhead_groups, log_sums)
    )
    dquery_rot = from_groups(dquery_groups, rows)
    dkey_all = dkey_groups.transpose(1, 0, 2).reshape(length, KVH * HD)
    dvalue_all = dvalue_groups.transpose(1, 0, 2).reshape(length, KVH * HD)
    own_kv = lax.psum_scatter(
        jnp.concatenate([dkey_all, dvalue_all], 1).astype(jnp.bfloat16),
        "ctx",
        scatter_dimension=0,
        tiled=True,
    ).astype(jnp.float32)
    dq = rotate(dquery_rot, own_places, H, -1.0).astype(jnp.bfloat16)
    dk = rotate(own_kv[:, : KVH * HD], own_places, KVH, -1.0).astype(jnp.bfloat16)
    dv_low = own_kv[:, KVH * HD :].astype(jnp.bfloat16)
    grad_q = dot_first(a, dq)
    grad_k = dot_first(a, dk)
    grad_v = dot_first(a, dv_low)
    grad_a = dot_last(dq, w_q_b) + dot_last(dk, w_k_b) + dot_last(dv_low, w_v_b)
    grad_gain_one, input_part = norm_back(x, scale_one, gain_one_b, grad_a)
    grad_x = (grad_resid + input_part).astype(jnp.bfloat16)
    grad_terms = (
        grad_gain_one,
        grad_q,
        grad_k,
        grad_v,
        grad_o,
        grad_gain_two,
        grad_g,
        grad_u,
        grad_d,
    )
    shares = (
        lax.psum_scatter(
            grad_terms[0].astype(jnp.bfloat16), "fsdp", scatter_dimension=0, tiled=True
        ).astype(jnp.float32),
        lax.psum_scatter(
            grad_terms[1].astype(jnp.bfloat16), "fsdp", scatter_dimension=0, tiled=True
        ).astype(jnp.float32),
        lax.psum_scatter(
            grad_terms[2].astype(jnp.bfloat16), "fsdp", scatter_dimension=0, tiled=True
        ).astype(jnp.float32),
        lax.psum_scatter(
            grad_terms[3].astype(jnp.bfloat16), "fsdp", scatter_dimension=0, tiled=True
        ).astype(jnp.float32),
        lax.psum_scatter(
            grad_terms[4].astype(jnp.bfloat16), "fsdp", scatter_dimension=0, tiled=True
        ).astype(jnp.float32),
        lax.psum_scatter(
            grad_terms[5].astype(jnp.bfloat16), "fsdp", scatter_dimension=0, tiled=True
        ).astype(jnp.float32),
        lax.psum_scatter(
            grad_terms[6].astype(jnp.bfloat16), "fsdp", scatter_dimension=0, tiled=True
        ).astype(jnp.float32),
        lax.psum_scatter(
            grad_terms[7].astype(jnp.bfloat16), "fsdp", scatter_dimension=0, tiled=True
        ).astype(jnp.float32),
        lax.psum_scatter(
            grad_terms[8].astype(jnp.bfloat16), "fsdp", scatter_dimension=0, tiled=True
        ).astype(jnp.float32),
    )
    summed = (
        lax.psum(shares[0].astype(jnp.bfloat16), "ctx").astype(jnp.float32),
        lax.psum(shares[1].astype(jnp.bfloat16), "ctx").astype(jnp.float32),
        lax.psum(shares[2].astype(jnp.bfloat16), "ctx").astype(jnp.float32),
        lax.psum(shares[3].astype(jnp.bfloat16), "ctx").astype(jnp.float32),
        lax.psum(shares[4].astype(jnp.bfloat16), "ctx").astype(jnp.float32),
        lax.psum(shares[5].astype(jnp.bfloat16), "ctx").astype(jnp.float32),
        lax.psum(shares[6].astype(jnp.bfloat16), "ctx").astype(jnp.float32),
        lax.psum(shares[7].astype(jnp.bfloat16), "ctx").astype(jnp.float32),
        lax.psum(shares[8].astype(jnp.bfloat16), "ctx").astype(jnp.float32),
    )
    return (
        result[None],
        grad_x[None],
        summed[0],
        summed[1],
        summed[2],
        summed[3],
        summed[4],
        summed[5],
        summed[6],
        summed[7],
        summed[8],
    )


RATIO = H // KVH
PAIR = 2 * RATIO * HD
WIDE = 2 * HD
NT = (((1,), (1,)), ((), ()))
TN = (((0,), (0,)), ((), ()))
NN = (((1,), (0,)), ((), ()))
VMEM = pl.BlockSpec(memory_space=pltpu.VMEM)
HBM = pl.BlockSpec(memory_space=pl.ANY)
ROOM = pltpu.CompilerParams(vmem_limit_bytes=60 * 2**20)


def mm(left, right, dims):
    return lax.dot_general(left, right, dims, preferred_element_type=jnp.float32)


def cost(flops, nbytes, exps=0):
    return pl.CostEstimate(flops=int(flops), bytes_accessed=int(nbytes), transcendentals=int(exps))


def turn(values, cosine, sine):
    lane = lax.broadcasted_iota(jnp.int32, values.shape, 1)
    first = lax.rem(lane, HD) < HD // 2
    partner = jnp.where(first, pltpu.roll(values, WIDE - HD // 2, 1), pltpu.roll(values, HD // 2, 1))
    return values * cosine + partner * sine


def far_lines(z):
    return (z ^ 1, z ^ 2, z ^ 3)


def qkv_kernel(
    at_ref, x_ref, cos_ref, sin_ref, w0_ref, w1_ref, own0_ref, own1_ref, a_ref, at_out_ref, q_ref, kv_ref, gain_ref, w_ref, sem
):
    t, core, z = at_ref[0], at_ref[1], at_ref[2]
    parts, lines, cut, width = w0_ref.shape
    copies = []
    for n, (w, own) in enumerate(((w0_ref, own0_ref), (w1_ref, own1_ref))):
        other = core if n == 0 else 1 - core
        row = pl.multiple_of((2 * z + other) * cut, 16)
        copies.append((own.at[:, pl.ds(0, parts * width)], w_ref.at[pl.ds(row, cut), :]))
        for k, far in enumerate(far_lines(z)):
            row = pl.multiple_of((2 * far + other) * cut, 16)
            for r in range(parts):
                column = pl.multiple_of((t ^ r) * width, WIDE)
                copies.append((w.at[r, k], w_ref.at[pl.ds(row, cut), pl.ds(column, width)]))
    copies = [pltpu.make_async_copy(src, dst, sem.at[i]) for i, (src, dst) in enumerate(copies)]
    for c in copies:
        c.start()
    x = x_ref[...].astype(jnp.float32)
    inv = lax.rsqrt(jnp.mean(x * x, -1, keepdims=True) + EPS)
    for c in copies:
        c.wait()
    first, half = H * HD, KVH * HD
    gains = jnp.transpose(w_ref[:, first + 2 * half : first + 2 * half + WIDE].astype(jnp.float32))[0:8]
    gain_ref[...] = gains
    a = (x * inv * gains[0:1]).astype(jnp.bfloat16)
    a_ref[...] = a
    at_out_ref[...] = jnp.transpose(a)
    for at in range(0, first + 2 * half, 2 * WIDE):
        both = mm(a_ref[...], w_ref[:, at : at + 2 * WIDE], NN)
        for n in range(0, 2 * WIDE, WIDE):
            part, column = both[:, n : n + WIDE], at + n
            if column < first + half:
                part = turn(part, cos_ref[...], sin_ref[...])
            if column < first:
                q_ref[:, column : column + WIDE] = part.astype(jnp.bfloat16)
            elif column < first + 2 * half:
                kv_ref[:, column - first : column - first + WIDE] = part.astype(jnp.bfloat16)


def qkv_project(where, x, cosine, sine, w, own):
    rows, model = x.shape
    width = 4 * w[0].shape[3]
    low = jnp.bfloat16
    return pl.pallas_call(
        qkv_kernel,
        in_specs=[pl.BlockSpec(memory_space=pltpu.SMEM)] + [VMEM] * 3 + [HBM] * 4,
        out_specs=[VMEM] * 6,
        out_shape=[
            jax.ShapeDtypeStruct((rows, model), low),
            jax.ShapeDtypeStruct((model, rows), low),
            jax.ShapeDtypeStruct((rows, H * HD), low),
            jax.ShapeDtypeStruct((rows, 2 * KVH * HD), low),
            jax.ShapeDtypeStruct((8, model), jnp.float32),
            jax.ShapeDtypeStruct((model, width), low),
        ],
        scratch_shapes=[pltpu.SemaphoreType.DMA((2 + 2 * 3 * w[0].shape[0],))],
        compiler_params=ROOM,
        cost_estimate=cost(2 * rows * model * width, 2 * (4 * rows * model + 2 * model * width)),
        name="qkv_project",
    )(where, x, cosine, sine, w[0], w[1], own[0], own[1])


def pick_heads(ref, row, group, factor):
    own = lax.broadcasted_iota(jnp.int32, (BLK, WIDE), 1) // HD == group
    out = []
    for n in range(group * RATIO, (group + 1) * RATIO):
        piece = ref[pl.ds(row, BLK), pl.ds(n // 2 * WIDE, WIDE)].astype(jnp.float32) * factor
        if n % 2 != group:
            piece = pltpu.roll(piece, HD, 1)
        out.append(jnp.where(own, piece, 0.0).astype(jnp.bfloat16))
    return jnp.concatenate(out, 0)


def join_heads(groups):
    lane = lax.broadcasted_iota(jnp.int32, (BLK, WIDE), 1)
    parts = []
    for n in range(2 * RATIO):
        group, i = divmod(n, RATIO)
        piece = groups[group][i * BLK : (i + 1) * BLK, :]
        parts.append(piece if n % 2 == group else pltpu.roll(piece, HD, 1))
    return [jnp.where(lane < HD, parts[2 * b], parts[2 * b + 1]) for b in range(RATIO)]


def steps_of(pairs, most):
    return max(u for u in range(1, most + 1) if pairs % u == 0)


def attend_kernel(own_ref, slot_ref, q_ref, k_ref, v_ref, o_ref, lse_ref, s_scr, v_scr, q_scr, m_scr, a_scr):
    rows = RATIO * BLK
    length = v_ref.shape[0]
    pairs = length // BLK + 1
    lane = lax.broadcasted_iota(jnp.int32, (length, WIDE), 1)
    first = own_ref[0] + 1

    def place(t):
        j = jnp.where(t >= first, 1, 0)
        return j, pl.multiple_of(slot_ref[t - j * first] * BLK, BLK)

    outs = [[], []]
    for group in range(2):
        v_scr[...] = jnp.where(lane // HD == group, v_ref[...].astype(jnp.float32), 1.0).astype(jnp.bfloat16)
        for j in range(2):
            q_scr[j] = pick_heads(q_ref, j * BLK, group, HD**-0.5)
        m_scr[...] = jnp.full(m_scr.shape, -jnp.inf, jnp.float32)
        a_scr[...] = jnp.zeros(a_scr.shape, jnp.float32)

        def scores(t, carry):
            j, at = place(t)
            s = mm(q_scr[j], k_ref[pl.ds(at, BLK), :], NT)
            s_scr[t] = s
            m_scr[j] = jnp.maximum(m_scr[j], jnp.maximum(s[:, 0:WIDE], s[:, WIDE : 2 * WIDE]))
            return carry

        lax.fori_loop(0, pairs, scores, 0, unroll=steps_of(pairs, 9))
        for j in range(2):
            m_scr[j] = jnp.broadcast_to(jnp.max(m_scr[j], 1, keepdims=True), (rows, WIDE))

        def mix(t, carry):
            j, at = place(t)
            top = m_scr[j]
            p = jnp.exp(s_scr[t] - jnp.concatenate([top, top], 1)).astype(jnp.bfloat16)
            a_scr[j] += mm(p, v_scr[pl.ds(at, BLK), :], NN)
            return carry

        lax.fori_loop(0, pairs, mix, 0, unroll=steps_of(pairs, 9))
        own = lax.broadcasted_iota(jnp.int32, (rows, WIDE), 1) // HD == group
        for j in range(2):
            acc = a_scr[j]
            total = jnp.where(own, pltpu.roll(acc, HD, 1), acc)
            outs[j].append(acc / total)
            lse_ref[group, j] = jnp.transpose(m_scr[j] + jnp.log(total))[0:1]
    for j in range(2):
        for b, part in enumerate(join_heads(outs[j])):
            o_ref[pl.ds(j * BLK, BLK), pl.ds(b * WIDE, WIDE)] = part.astype(jnp.bfloat16)


def attend(own, slots, q, kv, start, count):
    rows, length = q.shape[0], kv.shape[0]
    nblk = length // BLK
    work = rows * length * H * (nblk + 1) // (2 * nblk) * count // (KVH // 2)
    return pl.pallas_call(
        attend_kernel,
        grid_spec=pltpu.PrefetchScalarGridSpec(
            num_scalar_prefetch=2,
            grid=(count,),
            in_specs=[
                pl.BlockSpec((rows, PAIR), lambda p, *_: (0, p + start)),
                pl.BlockSpec((length, WIDE), lambda p, *_: (0, p + start)),
                pl.BlockSpec((length, WIDE), lambda p, *_: (0, p + start + KVH // 2)),
            ],
            out_specs=[
                pl.BlockSpec((rows, PAIR), lambda p, *_: (0, p)),
                pl.BlockSpec((2, 2, 1, RATIO * BLK), lambda p, *_: (p, 0, 0, 0)),
            ],
            scratch_shapes=[
                pltpu.VMEM((nblk + 1, RATIO * BLK, BLK), jnp.float32),
                pltpu.VMEM((length, WIDE), jnp.bfloat16),
                pltpu.VMEM((2, RATIO * BLK, WIDE), jnp.bfloat16),
                pltpu.VMEM((2, RATIO * BLK, WIDE), jnp.float32),
                pltpu.VMEM((2, RATIO * BLK, WIDE), jnp.float32),
            ],
        ),
        out_shape=[
            jax.ShapeDtypeStruct((rows, PAIR * count), jnp.bfloat16),
            jax.ShapeDtypeStruct((2 * count, 2, 1, RATIO * BLK), jnp.float32),
        ],
        compiler_params=ROOM,
        cost_estimate=cost(4 * 8 * work * HD, 4 * rows * PAIR * count + 4 * length * WIDE * count, work),
        name="attend",
    )(own, slots, q, kv, kv)


def attend_back_kernel(
    own_ref, slot_ref, where_ref, q_ref, k_ref, v_ref, do_ref, o_ref, lse_ref, cos_ref, sin_ref, *refs
):
    dq_ref, dkv_ref, dk_scr, dv_scr, q_scr, do_scr, st_scr, a_scr = refs[-8:]
    rows = RATIO * BLK
    length = v_ref.shape[0]
    pairs = length // BLK + 1
    dk_scr[...] = jnp.zeros_like(dk_scr)
    dv_scr[...] = jnp.zeros_like(dv_scr)
    first = own_ref[0] + 1
    outs = [[], []]
    for group in range(2):
        for j in range(2):
            q_scr[j] = pick_heads(q_ref, j * BLK, group, HD**-0.5)
            grads = pick_heads(do_ref, j * BLK, group, 1.0)
            do_scr[j] = grads
            mixed = pick_heads(o_ref, j * BLK, group, 1.0)
            inner = jnp.sum(grads.astype(jnp.float32) * mixed.astype(jnp.float32), 1, keepdims=True)
            st_scr[j, 0:1] = jnp.transpose(jnp.broadcast_to(inner, (rows, WIDE)))[0:1]
            st_scr[j, 1:2] = lse_ref[group, j]
        a_scr[...] = jnp.zeros_like(a_scr)

        def step(t, carry):
            j = jnp.where(t >= first, 1, 0)
            at = pl.multiple_of(slot_ref[t - j * first] * BLK, BLK)
            keys = k_ref[pl.ds(at, BLK), :]
            qs, grads = q_scr[j], do_scr[j]
            p = jnp.exp(mm(keys, qs, NT) - st_scr[j, 1:2])
            dp = mm(v_ref[pl.ds(at, BLK), :], grads, NT)
            ds = (p * (dp - st_scr[j, 0:1])).astype(jnp.bfloat16)
            dv_scr[pl.ds(at, BLK), :] += mm(p.astype(jnp.bfloat16), grads, NN)
            dk_scr[pl.ds(at, BLK), :] += mm(ds, qs, NN)
            a_scr[j] += mm(ds, keys, TN)
            return carry

        lax.fori_loop(0, pairs, step, 0, unroll=steps_of(pairs, 3))
        for j in range(2):
            outs[j].append(a_scr[j] * HD**-0.5)
    for j in range(2):
        span = pl.ds(j * BLK, BLK)
        for b, part in enumerate(join_heads(outs[j])):
            dq_ref[span, pl.ds(b * WIDE, WIDE)] = turn(part, cos_ref[span, :], -sin_ref[span, :]).astype(jnp.bfloat16)
    own_rows = length // 4
    for n, (scr, order) in enumerate(((dk_scr, (1, 3, 0, 2)), (dv_scr, (2, 3, 0, 1)))):
        for i, r in enumerate(order):
            dkv_ref[n, i] = scr[pl.ds(r * own_rows, own_rows), :].astype(jnp.bfloat16)


def attend_back(own, slots, where, q, kv, grads, mixed, lse, cosine, sine, start, count, into=None):
    rows, length = q.shape[0], kv.shape[0]
    nblk = length // BLK
    work = rows * length * H * (nblk + 1) // (2 * nblk) * count // (KVH // 2)
    wide = pl.BlockSpec((rows, PAIR), lambda p, *_: (0, p))
    shifted = pl.BlockSpec((rows, PAIR), lambda p, *_: (0, p + start))
    whole = pl.BlockSpec((rows, WIDE), lambda p, *_: (0, 0))
    part = pl.BlockSpec((2, 4, length // 4, WIDE), lambda p, *_: (0, 0, 0, p + start))
    part_shape = jax.ShapeDtypeStruct((2, 4, length // 4, KVH * HD), jnp.bfloat16)
    more = [] if into is None else [into]
    return pl.pallas_call(
        attend_back_kernel,
        grid_spec=pltpu.PrefetchScalarGridSpec(
            num_scalar_prefetch=3,
            grid=(count,),
            in_specs=[
                shifted,
                pl.BlockSpec((length, WIDE), lambda p, *_: (0, p + start)),
                pl.BlockSpec((length, WIDE), lambda p, *_: (0, p + start + KVH // 2)),
                shifted,
                shifted,
                pl.BlockSpec((2, 2, 1, RATIO * BLK), lambda p, *_: (p + start, 0, 0, 0)),
                whole,
                whole,
            ]
            + [HBM] * len(more),
            out_specs=[wide, part],
            scratch_shapes=[
                pltpu.VMEM((length, WIDE), jnp.float32),
                pltpu.VMEM((length, WIDE), jnp.float32),
                pltpu.VMEM((2, RATIO * BLK, WIDE), jnp.bfloat16),
                pltpu.VMEM((2, RATIO * BLK, WIDE), jnp.bfloat16),
                pltpu.VMEM((2, 8, RATIO * BLK), jnp.float32),
                pltpu.VMEM((2, RATIO * BLK, WIDE), jnp.float32),
            ],
        ),
        out_shape=[jax.ShapeDtypeStruct((rows, PAIR * count), jnp.bfloat16), part_shape],
        input_output_aliases={} if into is None else {11: 1},
        compiler_params=ROOM,
        cost_estimate=cost(1000, 1000) if into is None else cost(80 * work * HD, 8 * rows * PAIR * count + 8 * length * WIDE * count, work),
        name="attend_back",
    )(own, slots, where, q, kv, kv, grads, mixed, lse, cosine, sine, *more)


def middle_kernel(
    at_ref, ho_ref, x_ref, dy_ref, gain_ref,
    *refs,
):
    r = pl.program_id(0)
    count = pl.num_programs(0)
    t, core, z = at_ref[0], at_ref[1], at_ref[2]
    parts = 4
    sent, (d0_ref, d1_ref, all0_ref, all1_ref) = refs[: 2 * parts], refs[2 * parts : 2 * parts + 4]
    out_ref, low_ref, bt_ref, gd_ref, gs_ref, gk_ref, us_ref, uk_ref, dr_ref, dh_ref, gg_ref = refs[-24:-13]
    gu_scr, d_scr, wo_ref, r_scr, b_scr, acc_scr, db_scr, h_scr, dg_ref, du_ref, gu_sem, o_sem, d_sem = refs[-13:]
    lines, cut, columns_sent = sent[0].shape
    width = dg_ref.shape[1]
    model = wo_ref.shape[1]
    o_width = columns_sent - 2 * width
    o_parts = model // o_width
    first_g = all0_ref.shape[1] - model - 2 * parts * width
    alls = (all0_ref, all1_ref)
    cores = (core, 1 - core)
    others = far_lines(z)

    def piece(n, part, k):
        return sent[2 * part + n].at[k]

    def gu_copies(part, slot):
        out = []
        for n, other in enumerate(cores):
            rows = pl.ds(pl.multiple_of((2 * z + other) * cut, 16), cut)
            for m in range(2):
                column = pl.multiple_of(first_g + (m * parts + (t ^ part)) * width, WIDE)
                out.append((alls[n].at[:, pl.ds(column, width)], gu_scr.at[slot, m, rows, :]))
            for k in range(lines):
                rows = pl.ds(pl.multiple_of((2 * others[k] + other) * cut, 16), cut)
                for m in range(2):
                    out.append((piece(n, part, k).at[:, pl.ds(m * width, width)], gu_scr.at[slot, m, rows, :]))
        return [pltpu.make_async_copy(src, dst, gu_sem.at[slot, i]) for i, (src, dst) in enumerate(out)]

    def o_copies(part):
        out = []
        columns = pl.ds(pl.multiple_of((t ^ part) * o_width, WIDE), o_width)
        for n, other in enumerate(cores):
            for k in range(lines):
                rows = pl.ds(pl.multiple_of((2 * others[k] + other) * cut, 16), cut)
                out.append((piece(n, part, k).at[:, pl.ds(2 * width, o_width)], wo_ref.at[rows, columns]))
        return [pltpu.make_async_copy(src, dst, o_sem.at[part, i]) for i, (src, dst) in enumerate(out)]

    def own_copies():
        out = []
        for n, other in enumerate(cores):
            rows = pl.ds(pl.multiple_of((2 * z + other) * cut, 16), cut)
            out.append((alls[n].at[:, pl.ds(first_g + 2 * parts * width, model)], wo_ref.at[rows, :]))
        return [pltpu.make_async_copy(src, dst, o_sem.at[parts, i]) for i, (src, dst) in enumerate(out)]

    def d_copies():
        out = []
        cut_d = d0_ref.shape[1]
        for n, other in enumerate(cores):
            for line in range(lines + 1):
                row = pl.multiple_of((2 * line + other) * cut_d, 16)
                out.append(((d0_ref, d1_ref)[n].at[line], d_scr.at[pl.ds(row, cut_d), :]))
        return [pltpu.make_async_copy(src, dst, d_sem.at[i]) for i, (src, dst) in enumerate(out)]

    slot = lax.rem(r, 2)

    @pl.when(r == 0)
    def _():
        for part in range(parts):

            @pl.when((t ^ part) < o_parts)
            def _():
                for c in o_copies(part):
                    c.start()

        for c in own_copies():
            c.start()
        for c in gu_copies(0, 0) + d_copies():
            c.start()
        for part in range(parts):

            @pl.when((t ^ part) < o_parts)
            def _():
                for c in o_copies(part):
                    c.wait()

        for c in own_copies():
            c.wait()
        resid = x_ref[...].astype(jnp.float32) + mm(ho_ref[...], wo_ref[...], NN)
        r_scr[...] = resid
        inv = lax.rsqrt(jnp.mean(resid * resid, -1, keepdims=True) + EPS)
        b = (resid * inv * gain_ref[1:2]).astype(jnp.bfloat16)
        b_scr[...] = b
        turned = jnp.transpose(b)
        for shard in range(2 * (lines + 1)):
            rows = slice(shard * cut, (shard + 1) * cut)
            bt_ref[lax.rem(shard + core, 2), shard // 2 * cut : (shard // 2 + 1) * cut] = turned[rows]

    for part in range(parts):

        @pl.when(r == part)
        def _():
            for c in gu_copies(part, part % 2):
                c.wait()
            if part == 0:
                for c in d_copies():
                    c.wait()
            if part + 1 < parts:
                for c in gu_copies(part + 1, (part + 1) % 2):
                    c.start()

    down = pl.multiple_of((t ^ r) * width, 256)
    for at in range(0, width, 256):
        span = slice(at, at + 256)
        gate = mm(b_scr[...], gu_scr[slot, 0, :, span], NN)
        up = mm(b_scr[...], gu_scr[slot, 1, :, span], NN)
        dhid = mm(dy_ref[...], d_scr[pl.ds(down + at, 256), :], NT)
        sig = jax.nn.sigmoid(gate)
        silu = gate * sig
        hidden = (silu * up).astype(jnp.bfloat16)
        h_scr[:, span] = hidden
        dg_ref[:, span] = (dhid * up * sig * (1.0 + gate * (1.0 - sig))).astype(jnp.bfloat16)
        du_ref[:, span] = (dhid * silu).astype(jnp.bfloat16)
    for n, (g_ref, u_ref) in enumerate(((gk_ref, uk_ref), (gs_ref, uk_ref), (gk_ref, us_ref), (gs_ref, us_ref))):

        @pl.when(r == n)
        def _():
            g_ref[0] = dg_ref[...]
            u_ref[0] = du_ref[...]

    gd_ref[0] = mm(h_scr[...], dy_ref[...], TN).astype(jnp.bfloat16)
    for at in range(0, model, 1152):
        span = slice(at, at + 1152)
        acc = mm(h_scr[...], d_scr[pl.ds(down, width), span], NN)
        db = mm(dg_ref[...], gu_scr[slot, 0, span, :], NT) + mm(du_ref[...], gu_scr[slot, 1, span, :], NT)

        @pl.when(r == 0)
        def _():
            acc_scr[:, span] = acc
            db_scr[:, span] = db

        @pl.when(r > 0)
        def _():
            acc_scr[:, span] += acc
            db_scr[:, span] += db

    @pl.when(r == count - 1)
    def _():
        resid = r_scr[...]
        out_ref[...] = (resid + acc_scr[...]).astype(jnp.bfloat16)
        inv = lax.rsqrt(jnp.mean(resid * resid, -1, keepdims=True) + EPS)
        db = db_scr[...]
        gg_ref[...] = jnp.sum(db * resid * inv, 0, keepdims=True)
        weighted = gain_ref[1:2] * db
        dr = (
            dy_ref[...].astype(jnp.float32)
            + inv * weighted
            - resid * (inv * inv * inv) * jnp.mean(weighted * resid, -1, keepdims=True)
        )
        dr_ref[...] = dr
        low = dr.astype(jnp.bfloat16)
        low_ref[...] = low
        dh_ref[...] = mm(low, wo_ref[...], NT).astype(jnp.bfloat16)


def middle(where, ho, x, dy, gains, sent, d, own_all):
    rows, model = x.shape
    lines, cut = sent[0][0].shape[:2]
    count = len(sent)
    width = d[0].shape[0] * d[0].shape[1] * 2 // count
    once = pl.Buffered(1)
    whole = lambda shape: pl.BlockSpec(shape, lambda r, *_: (0,) * len(shape), pipeline_mode=once)
    act = lambda at: pl.BlockSpec((1, rows, width), lambda r, *_: (at(r), 0, 0))
    low = jnp.bfloat16
    return pl.pallas_call(
        middle_kernel,
        grid_spec=pltpu.PrefetchScalarGridSpec(
            num_scalar_prefetch=1,
            grid=(count,),
            in_specs=[whole((rows, H * HD)), whole((rows, model)), whole((rows, model)), whole((8, model))] + [HBM] * 12,
            out_specs=[
                whole((rows, model)), whole((rows, model)), whole((2, model // 2, rows)),
                pl.BlockSpec((1, width, model), lambda r, at_ref: (at_ref[0] ^ r, 0, 0)),
                act(lambda r: r // 3), act(lambda r: r // 2), act(lambda r: r // 3), act(lambda r: (r + 2) // 3),
                whole((rows, model)), whole((rows, H * HD)), whole((1, model)),
            ],
            scratch_shapes=[
                pltpu.VMEM((2, 2, 2 * (lines + 1) * cut, width), low),
                pltpu.VMEM((count * width, model), low),
                pltpu.VMEM((H * HD, model), low),
                pltpu.VMEM((rows, model), jnp.float32),
                pltpu.VMEM((rows, model), low),
                pltpu.VMEM((rows, model), jnp.float32),
                pltpu.VMEM((rows, model), jnp.float32),
                pltpu.VMEM((rows, width), low),
                pltpu.VMEM((rows, width), low),
                pltpu.VMEM((rows, width), low),
                pltpu.SemaphoreType.DMA((2, 4 * (lines + 1))),
                pltpu.SemaphoreType.DMA((count + 1, 2 * lines)),
                pltpu.SemaphoreType.DMA((2 * (lines + 1),)),
            ],
        ),
        out_shape=[
            jax.ShapeDtypeStruct((rows, model), low),
            jax.ShapeDtypeStruct((rows, model), low),
            jax.ShapeDtypeStruct((2, model // 2, rows), low),
            jax.ShapeDtypeStruct((count, width, model), low),
            *[jax.ShapeDtypeStruct((2, rows, width), low)] * 4,
            jax.ShapeDtypeStruct((rows, model), jnp.float32),
            jax.ShapeDtypeStruct((rows, H * HD), low),
            jax.ShapeDtypeStruct((1, model), jnp.float32),
        ],
        compiler_params=ROOM,
        cost_estimate=cost(12 * rows * model * width * count + 4 * rows * model * model, 2 * 16 * rows * model + 6 * count * width * model, rows * width * count),
        name="middle",
    )(where, ho, x, dy, gains, *[v for pair in sent for v in pair], *d, *own_all)


def act_kernel(counts, cos_ref, sin_ref, dkv_ref, gx_ref, lasty_ref, gy_ref, lastx_ref, *refs):
    act_ref = refs[-1]
    half = KVH * HD
    at = 0
    for dq_ref, count in zip(refs, counts):
        act_ref[:, at * PAIR : (at + count) * PAIR] = dq_ref[...]
        at += count
    for p in range(at):
        span = slice(p * WIDE, (p + 1) * WIDE)
        dk = sum(v.astype(jnp.float32) for v in (dkv_ref[0, 2, :, span], gx_ref[0, :, span], lasty_ref[:, span]))
        dv = sum(v.astype(jnp.float32) for v in (dkv_ref[1, 2, :, span], gy_ref[0, :, span], lastx_ref[:, span]))
        column = H * HD + p * WIDE
        act_ref[:, column : column + WIDE] = turn(dk, cos_ref[...], -sin_ref[...]).astype(jnp.bfloat16)
        act_ref[:, column + half : column + half + WIDE] = dv.astype(jnp.bfloat16)
    act_ref[:, H * HD + 2 * half :] = jnp.zeros((act_ref.shape[0], act_ref.shape[1] - H * HD - 2 * half), jnp.bfloat16)


def make_act(cosine, sine, shares, parts, counts, width):
    rows = cosine.shape[0]
    return pl.pallas_call(
        functools.partial(act_kernel, counts),
        in_specs=[VMEM] * (7 + len(parts)),
        out_specs=VMEM,
        out_shape=jax.ShapeDtypeStruct((rows, width), jnp.bfloat16),
        compiler_params=ROOM,
        cost_estimate=cost(10 * rows * width, 6 * rows * width),
        name="make_act",
    )(cosine, sine, *shares, *parts)


def last_kernel(x_ref, gain_ref, dr_ref, w_ref, act_ref, gx_ref, gg_ref):
    used = (H + 2 * KVH) * HD
    da = mm(act_ref[:, 0:used], w_ref[:, 0:used], NT)
    x = x_ref[...].astype(jnp.float32)
    inv = lax.rsqrt(jnp.mean(x * x, -1, keepdims=True) + EPS)
    gg_ref[...] = jnp.sum(da * x * inv, 0, keepdims=True)
    weighted = gain_ref[0:1] * da
    gx = dr_ref[...] + inv * weighted - x * (inv * inv * inv) * jnp.mean(weighted * x, -1, keepdims=True)
    gx_ref[...] = gx.astype(jnp.bfloat16)


def last(x, gains, dr, w_qkv, act):
    rows, model = x.shape
    return pl.pallas_call(
        last_kernel,
        in_specs=[VMEM] * 5,
        out_specs=[VMEM] * 2,
        out_shape=[jax.ShapeDtypeStruct((rows, model), jnp.bfloat16), jax.ShapeDtypeStruct((1, model), jnp.float32)],
        compiler_params=ROOM,
        cost_estimate=cost(2 * rows * model * (H + 2 * KVH) * HD, 10 * rows * model + 2 * model * (H + 2 * KVH) * HD),
        name="last",
    )(x, gains, dr, w_qkv, act)


def gu_products_kernel(l0_ref, l1_ref, g0_ref, g1_ref, u0_ref, u1_ref, g_ref, u_ref):
    @pl.when(pl.program_id(0) == 0)
    def _():
        g_ref[0] = (mm(l0_ref[...], g0_ref[0], NN) + mm(l1_ref[...], g1_ref[0], NN)).astype(jnp.bfloat16)

    @pl.when(pl.program_id(0) == 1)
    def _():
        u_ref[0] = (mm(l0_ref[...], u0_ref[0], NN) + mm(l1_ref[...], u1_ref[0], NN)).astype(jnp.bfloat16)


def gu_products(left, gates, ups):
    rows, tokens = left[0].shape
    width = gates[0].shape[2]
    cuts = 1
    piece = width // cuts
    spec = pl.BlockSpec((rows, tokens), lambda m, n, h: (0, 0))
    first = lambda m, v, end: v * (1 - m) + end * m
    then = lambda m, v: v * m

    def gate_at(m, n, h):
        return first(m, n, 1), first(m, h, cuts - 1)

    def up_at(m, n, h):
        return then(m, n), then(m, h)

    def gate_in(m, n, h):
        n, h = gate_at(m, n, h)
        return n, 0, h

    def up_in(m, n, h):
        n, h = up_at(m, n, h)
        return n, 0, h

    def gate_out(m, n, h):
        n, h = gate_at(m, n, h)
        return n, 0, h

    def up_out(m, n, h):
        n, h = up_at(m, n, h)
        return n, 0, h

    act = lambda index: pl.BlockSpec((1, tokens, piece), index)
    return pl.pallas_call(
        gu_products_kernel,
        grid=(2, 2, cuts),
        in_specs=[spec, spec, act(gate_in), act(gate_in), act(up_in), act(up_in)],
        out_specs=[pl.BlockSpec((1, rows, piece), gate_out), pl.BlockSpec((1, rows, piece), up_out)],
        out_shape=[jax.ShapeDtypeStruct((2, rows, width), jnp.bfloat16)] * 2,
        compiler_params=ROOM,
        cost_estimate=cost(16 * rows * tokens * width, 4 * rows * tokens + 8 * (2 * tokens + rows) * width),
        name="gu_products",
    )(left[0], left[1], gates[0], gates[1], ups[0], ups[1])


def qkv_products_kernel(where_ref, l0_ref, l1_ref, r0_ref, r1_ref, s0_ref, s1_ref, s2_ref, s3_ref):
    total = mm(l0_ref[...], r0_ref[...], NN) + mm(l1_ref[...], r1_ref[...], NN)
    for n, ref in enumerate((s0_ref, s1_ref, s2_ref, s3_ref)):

        @pl.when(pl.program_id(0) == n)
        def _():
            ref[...] = total.astype(jnp.bfloat16)


def qkv_products(where, left, acts):
    rows, tokens = left[0].shape
    width = acts[0].shape[1] // 4
    spec = pl.BlockSpec((rows, tokens), lambda r, *_: (0, 0))
    act = pl.BlockSpec((tokens, width), lambda r, w: (0, w[0] ^ r))
    out = pl.BlockSpec((rows, width), lambda r, *_: (0, 0))
    return pl.pallas_call(
        qkv_products_kernel,
        grid_spec=pltpu.PrefetchScalarGridSpec(
            num_scalar_prefetch=1,
            grid=(4,),
            in_specs=[spec, spec, act, act],
            out_specs=[out] * 4,
        ),
        out_shape=[jax.ShapeDtypeStruct((rows, width), jnp.bfloat16)] * 4,
        compiler_params=ROOM,
        cost_estimate=cost(16 * rows * tokens * width, 4 * rows * tokens + 8 * (2 * tokens + rows) * width),
        name="qkv_products",
    )(where, left[0], left[1], acts[0], acts[1])


def place_gu_kernel(where_ref, p0_ref, p1_ref, p2_ref, p3_ref, g_ref, u_ref):
    for r, ref in enumerate((p0_ref, p1_ref, p2_ref, p3_ref)):

        @pl.when(pl.program_id(0) == r)
        def _():
            g_ref[...] = ref[0].astype(jnp.float32)
            u_ref[...] = ref[1].astype(jnp.float32)


def place_gu(where, parts):
    _, rows, width = parts[0].shape
    out = pl.BlockSpec((rows, width), lambda r, w: (0, w[0] ^ r))
    return pl.pallas_call(
        place_gu_kernel,
        grid_spec=pltpu.PrefetchScalarGridSpec(
            num_scalar_prefetch=1,
            grid=(4,),
            in_specs=[pl.BlockSpec((2, rows, width), lambda r, *_: (0, 0, 0))] * 4,
            out_specs=[out, out],
        ),
        out_shape=[jax.ShapeDtypeStruct((rows, 4 * width), jnp.float32)] * 2,
        compiler_params=ROOM,
        cost_estimate=cost(1000, 1000),
        name="place_gu",
    )(where, *parts)


def place_qkv_kernel(in_ref, q_ref, k_ref, v_ref, g_ref):
    width = in_ref.shape[2] - WIDE
    spans = ((q_ref, 0, H * HD), (k_ref, H * HD, KVH * HD), (v_ref, (H + KVH) * HD, KVH * HD))
    gains = 0.0
    for n in range(in_ref.shape[0]):
        part = in_ref[n].astype(jnp.float32)
        gains += part[:, width:]
        for at in range(0, width, WIDE):
            column = n * width + at
            for ref, first, size in spans:
                if first <= column < first + size:
                    ref[:, column - first : column - first + WIDE] = part[:, at : at + WIDE]
    g_ref[...] = jnp.transpose(gains)[0:8]


def place_qkv(parts):
    rows = parts.shape[1]
    shape = lambda columns: jax.ShapeDtypeStruct((rows, columns), jnp.float32)
    return pl.pallas_call(
        place_qkv_kernel,
        in_specs=[VMEM],
        out_specs=[VMEM] * 4,
        out_shape=[shape(H * HD), shape(KVH * HD), shape(KVH * HD), jax.ShapeDtypeStruct((8, rows), jnp.float32)],
        cost_estimate=cost(parts.size, 6 * parts.size),
        name="place_qkv",
    )(parts)


def square(v, r):
    return lax.ppermute(v, "ctx", [(t, t ^ r) for t in range(4)])


def line(v, k):
    return lax.ppermute(v, "fsdp", [(f, f ^ (2 * k)) for f in range(8)])


def other_core(v):
    return lax.ppermute(v, "fsdp", [(f, f ^ 1) for f in range(8)])


def after(v, *others):
    return lax.optimization_barrier((v, *others))[0]


def wide(v):
    return v.astype(jnp.float32)


def low(v):
    return v.astype(jnp.bfloat16)


LINES = [[0, 2, 4, 6], [1, 3, 5, 7]]


def line_all(v):
    return lax.all_to_all(v, "fsdp", 0, 0, axis_index_groups=LINES, tiled=True)


def line_spread(v):
    return line_all(jnp.broadcast_to(v[None], (4, *v.shape)))


def far_pieces(got, z):
    return [lax.dynamic_index_in_dim(got, z ^ k, 0, keepdims=False) for k in (1, 2, 3)]


def hold(parts, *events):
    return [after(v, *events) for v in parts]


def square_near(v):
    return [square(v, 1), square(v, 2)]


def square_far(from_x, from_y):
    half = from_x.shape[0] // 2
    return [square(from_y[:half], 1), square(from_x[half:], 2)]


def lanes(v, core):
    shaped = v.reshape(4, 2, v.shape[0] // 8, v.shape[1])
    pick = lambda c: lax.dynamic_index_in_dim(shaped, c, 1, keepdims=False).reshape(-1, v.shape[1])
    return pick(core), pick(1 - core)


def square_body(
    tokens,
    table,
    norm1_gain,
    w_query,
    w_key,
    w_value,
    w_out,
    norm2_gain,
    w_gate,
    w_up,
    w_down,
    cotangent,
):
    x, dy = tokens[0], cotangent[0]
    rows, model = x.shape
    t = lax.axis_index("ctx")
    f = lax.axis_index("fsdp")
    z, core = f // 2, f % 2
    where = jnp.stack([t, core, z]).astype(jnp.int32)
    cut, hidden_width = w_gate.shape
    cut_d = w_down.shape[0] // 4
    kv_width = 2 * KVH * HD

    relative = jnp.arange(4) ^ t
    offsets = jnp.arange(BLK, dtype=jnp.int32)
    ordered = table[relative].reshape(-1)
    own = ordered[:2].astype(jnp.int32)
    slots = jnp.zeros((ordered.shape[0],), jnp.int32).at[ordered].set(jnp.arange(ordered.shape[0], dtype=jnp.int32))
    places = (own[:, None] * BLK + offsets[None, :]).reshape(-1)
    frequency = 10000.0 ** (-(jnp.arange(HD // 2, dtype=jnp.float32) * 2.0 / HD))
    angles = places.astype(jnp.float32)[:, None] * frequency
    cosine = jnp.tile(jnp.cos(angles), (1, 4))
    sine = jnp.sin(angles)
    sine = jnp.concatenate([-sine, sine, -sine, sine], 1)

    slice_of = lambda w: lax.dynamic_slice_in_dim(w, t * (w.shape[1] // 4), w.shape[1] // 4, 1)
    filled = -(-(H * HD + kv_width + WIDE) // (8 * WIDE)) * 8 * WIDE
    gains_own = jnp.stack([norm1_gain, norm2_gain], 1)
    qkv_own = jnp.concatenate([w_query, w_key, w_value, gains_own], 1)
    qkv_own = jnp.pad(qkv_own, ((0, 0), (0, filled - qkv_own.shape[1])))
    o_whole = jnp.pad(w_out, ((0, 0), (0, 2 * (hidden_width // 4) - model)))
    guo_part = jnp.concatenate([slice_of(w_gate), slice_of(w_up), slice_of(o_whole)], 1)
    swap = lambda w: (w, other_core(w))
    qkv_slice = slice_of(qkv_own)
    qkv_line = [line(qkv_slice, k) for k in (1, 2, 3)]
    own_all = swap(jnp.concatenate([qkv_own, w_gate, w_up, w_out], 1))
    qkv_rows = jnp.concatenate(hold(qkv_line, cosine, sine, slots, guo_part))
    guo_line = line_spread(after(guo_part, *qkv_line))
    qkv_parts = [qkv_rows] + [square(qkv_rows, r) for r in (1, 2, 3)]
    qkv_all = after(jnp.stack(qkv_parts).reshape(4, 3, cut, -1), own_all[1])
    qkv_both = swap(qkv_all)

    a, a_t, q, kv_own, gains, w_qkv = qkv_project(where, x, cosine, sine, qkv_both, own_all)
    kv_near = square_near(kv_own)
    guo_line = after(guo_line, kv_own)
    d_line = line_all(after(jnp.broadcast_to(w_down[None], (4, *w_down.shape)), guo_line))
    kv_far = square_far(*kv_near)
    guo_rows = after(jnp.concatenate(far_pieces(after(guo_line, *kv_near), z)), *kv_far)
    guo_near = square_near(guo_rows)
    guo_own = other_core(guo_rows.reshape(3, cut, -1))
    kv = jnp.concatenate([kv_own, *kv_near, *kv_far])
    mixed, lse = attend(own, slots, after(q, guo_rows), kv, 0, KVH // 2)
    guo_near = hold(guo_near, mixed)
    half = guo_rows.shape[0] // 2
    guo_far = [square(guo_near[1][:half], 1), square(guo_near[0][half:], 2)]
    d = swap(after(d_line, *guo_far))
    shaped = lambda v: v.reshape(3, cut, -1)
    guo = [(shaped(guo_rows), after(guo_own, mixed))] + [swap(shaped(v)) for v in guo_near]
    guo.append(swap(shaped(after(jnp.concatenate(guo_far), *[v[1] for v in guo]))))
    out, dr_low, b_t, grad_d, g_s, g_k, u_s, u_k, dr, dheads, gg2 = middle(
        where, mixed, x, dy, gains, guo, d, own_all
    )

    left = (b_t[0], other_core(b_t[1]))
    g_s, u_s = swap(g_s), swap(u_s)
    grad_o = low(mm(mixed, dr_low, TN))
    g_send, u_send = gu_products(left, (after(g_s[0], grad_o), g_s[1]), u_s)
    got_x, got_y = square(g_send, 1), square(u_send, 2)
    scatter = lambda v: lax.psum_scatter(v, "fsdp", scatter_dimension=0, tiled=True)
    grad_d, grad_o = scatter(grad_d.reshape(-1, model)), scatter(grad_o)
    kept = [(after(v[0], g_send), v[1]) for v in (swap(g_k), swap(u_k))]
    g_keep, u_keep = gu_products(left, *kept)

    dq_1, dkv = attend_back(own, slots, where, after(q, g_keep), kv, dheads, mixed, lse, cosine, sine, 1, 2)
    got_x, got_y = hold((got_x, got_y), dq_1)
    pass_y = low(wide(g_keep[1]) + wide(got_x[1]))
    pass_x = low(wide(u_keep[1]) + wide(got_y[1]))
    last_y, last_x = square(pass_y, 2), square(pass_x, 1)
    dq_0, dkv = attend_back(
        own, slots, where, after(q, pass_x, pass_y), kv, dheads, mixed, lse, cosine, sine, 0, 1, dkv
    )
    last_y, last_x = hold([last_y, last_x], dq_0)
    dkv = after(dkv, last_y, last_x)
    kv_x, kv_y = square(dkv[0, :2], 1), square(dkv[1, :2], 2)
    rows_at = lambda v, at: v[at * cut : (at + 1) * cut]

    def gu_share(at):
        g = sum(wide(rows_at(v, at)) for v in (g_keep[0], got_x[0], last_y))
        u = sum(wide(rows_at(v, at)) for v in (u_keep[0], got_y[0], last_x))
        return jnp.stack([g, u])

    gu_sends = jnp.stack([low(gu_share(at)) for at in range(4)])
    gu_got = line_all(gu_sends)
    kv_x, kv_y = hold([kv_x, kv_y], gu_sends)
    kv_last_y = square(low(wide(dkv[0, 3]) + wide(kv_x[1])), 2)
    kv_last_x = square(low(wide(dkv[1, 3]) + wide(kv_y[1])), 1)
    grad_do = jnp.concatenate([grad_d, grad_o])
    half = grad_do.shape[0] // 32 * 16
    do_upper, do_lower = hold([grad_do[:half], grad_do[half:]], kv_x, kv_y)
    do_got = [square(do_upper, 1), square(do_lower, 2)]
    act = make_act(after(cosine, do_upper, do_lower), sine, [dkv, kv_x, kv_last_y, kv_y, kv_last_x], [dq_0, dq_1], (1, 2), filled)
    acts = swap(act)

    a_mine, a_other = lanes(a_t, core)
    left = (a_mine, other_core(a_other))
    qkv_keep, *qkv_sends = qkv_products(where, left, acts)
    shares = [qkv_keep] + [square(v, r) for r, v in zip((1, 2, 3), qkv_sends)]
    grad_x, gg1 = last(after(x, qkv_keep), gains, dr, w_qkv, act)
    shares = hold(shares, gg1)
    gain_rows = jnp.concatenate([gg1, gg2])
    gain_rows += other_core(gain_rows)
    gain_rows = lax.dynamic_index_in_dim(gain_rows.reshape(2, 4, 2, cut), core, 2, keepdims=False)
    gain_columns = jnp.pad(low(gain_rows.transpose(1, 2, 0)), ((0, 0), (0, 0), (0, WIDE - 2)))
    qkv_share = lambda at: sum(wide(rows_at(v, at)) for v in shares)
    qkv_sends = jnp.stack([low(qkv_share(at)) for at in range(4)])
    qkv_sends = jnp.concatenate([qkv_sends, gain_columns], 2)
    gu_got = after(gu_got, gg1)
    qkv_got = line_all(after(qkv_sends, gu_got))
    do_got = hold(do_got, gg1)
    do_upper, do_lower = low(wide(do_upper) + wide(do_got[0])), low(wide(do_lower) + wide(do_got[1]))
    do_got = [square(after(do_upper, qkv_sends), 2), square(after(do_lower, qkv_sends), 1)]
    s_gu = low(sum(wide(gu_got[n]) for n in range(4)))
    all_gu = [s_gu] + [square(after(s_gu, qkv_sends), r) for r in (1, 2, 3)]
    s_qkv = low(sum(wide(qkv_got[n]) for n in range(4)))
    all_qkv = lax.all_to_all(jnp.broadcast_to(s_qkv[None], (4, *s_qkv.shape)), "ctx", 0, 0, tiled=True)
    do_got, all_gu = hold(do_got, s_qkv), hold(all_gu, s_qkv)
    do_upper, do_lower = wide(do_upper) + wide(do_got[0]), wide(do_lower) + wide(do_got[1])
    below = 4 * cut_d - half
    grad_g, grad_u = place_gu(where, all_gu)
    grad_q, grad_k, grad_v, gain_rows = place_qkv(all_qkv)
    return (
        out[None],
        grad_x[None],
        gain_rows[0],
        grad_q,
        grad_k,
        grad_v,
        do_lower[below:],
        gain_rows[1],
        grad_g,
        grad_u,
        jnp.concatenate([do_upper, do_lower[:below]]),
    )


def solution(mesh):
    placed = (
        P("fsdp", "ctx", None),
        P(),
        P("fsdp"),
        P("fsdp", None),
        P("fsdp", None),
        P("fsdp", None),
        P("fsdp", None),
        P("fsdp"),
        P("fsdp", None),
        P("fsdp", None),
        P("fsdp", None),
        P("fsdp", "ctx", None),
    )
    square = mesh.shape["ctx"] == 4 and mesh.shape["fsdp"] == 8
    return jax.shard_map(
        square_body if square else plain_body,
        mesh=mesh,
        in_specs=placed,
        out_specs=(
            P("fsdp", "ctx", None),
            P("fsdp", "ctx", None),
            P("fsdp"),
            P("fsdp", None),
            P("fsdp", None),
            P("fsdp", None),
            P("fsdp", None),
            P("fsdp"),
            P("fsdp", None),
            P("fsdp", None),
            P("fsdp", None),
        ),
        check_vma=False,
    )
```

```python
import functools

import jax
import jax.numpy as jnp
from jax import lax
from jax.experimental import pallas as pl
from jax.experimental.pallas import tpu as pltpu
from jax.sharding import PartitionSpec as P

H = 18
KVH = 6
HD = 64
BLK = 256


EPS = 1e-05


def dot_first(left, right):
    return lax.dot_general(
        left, right, (((0,), (0,)), ((), ())), preferred_element_type=jnp.float32
    )


def dot_last(left, right):
    return lax.dot_general(
        left, right, (((1,), (1,)), ((), ())), preferred_element_type=jnp.float32
    )


def rotate(values, places, count, sign):
    split = HD // 2
    shaped = values.reshape(values.shape[0], count, HD)
    frequency = 10000.0 ** (-(jnp.arange(split, dtype=jnp.float32) * 2.0 / HD))
    angles = places.astype(jnp.float32)[:, None] * frequency
    cosine = jnp.cos(angles)[:, None, :]
    sine = jnp.sin(angles)[:, None, :] * sign
    first_half = shaped[..., :split]
    second_half = shaped[..., split:]
    turned = jnp.concatenate(
        [first_half * cosine - second_half * sine, second_half * cosine + first_half * sine], -1
    )
    return turned.reshape(values.shape[0], count * HD)


def norm_back(values, scale_inv, gain, grad_in):
    weighted = gain.astype(jnp.float32) * grad_in
    gain_grad = jnp.sum(grad_in * values * scale_inv, 0)
    grad_out = scale_inv * weighted - values * scale_inv**3 * jnp.mean(
        weighted * values, -1, keepdims=True
    )
    return (gain_grad, grad_out)


def to_groups(values, rows):
    ratio = H // KVH
    return values.reshape(rows, KVH, ratio, HD).transpose(1, 2, 0, 3).reshape(KVH, ratio * rows, HD)


def from_groups(values, rows):
    ratio = H // KVH
    return values.reshape(KVH, ratio, rows, HD).transpose(2, 0, 1, 3).reshape(rows, H * HD)


def plain_body(
    tokens,
    table,
    norm1_gain,
    w_query,
    w_key,
    w_value,
    w_out,
    norm2_gain,
    w_gate,
    w_up,
    w_down,
    cotangent,
):
    ratio = H // KVH
    scale = HD ** (-0.5)
    x = tokens[0].astype(jnp.float32)
    rows = x.shape[0]
    offsets = jnp.arange(BLK, dtype=jnp.int32)
    own_blocks = lax.dynamic_index_in_dim(table, lax.axis_index("ctx"), 0, keepdims=False)
    own_places = (own_blocks[:, None] * BLK + offsets[None, :]).reshape(-1)
    own_ids = jnp.tile(jnp.repeat(own_blocks, BLK), ratio)
    all_ids = jnp.repeat(table.reshape(-1), BLK)
    visible = all_ids[None, :] <= own_ids[:, None]
    forward_set = (
        lax.all_gather(norm1_gain, "fsdp", axis=0, tiled=True),
        lax.all_gather(w_query, "fsdp", axis=0, tiled=True),
        lax.all_gather(w_key, "fsdp", axis=0, tiled=True),
        lax.all_gather(w_value, "fsdp", axis=0, tiled=True),
        lax.all_gather(w_out, "fsdp", axis=0, tiled=True),
        lax.all_gather(norm2_gain, "fsdp", axis=0, tiled=True),
        lax.all_gather(w_gate, "fsdp", axis=0, tiled=True),
        lax.all_gather(w_up, "fsdp", axis=0, tiled=True),
        lax.all_gather(w_down, "fsdp", axis=0, tiled=True),
    )
    gain_one, w_q, w_k, w_v, w_o, gain_two, w_g, w_u, w_d = forward_set
    scale_one = lax.rsqrt(jnp.mean(x * x, -1, keepdims=True) + EPS)
    a = (x * scale_one * gain_one.astype(jnp.float32)).astype(jnp.bfloat16)
    q = jnp.dot(a, w_q, preferred_element_type=jnp.float32)
    k = jnp.dot(a, w_k, preferred_element_type=jnp.float32)
    v = jnp.dot(a, w_v, preferred_element_type=jnp.float32).astype(jnp.bfloat16)
    query_rot = rotate(q, own_places, H, 1.0).astype(jnp.bfloat16)
    key_rot = rotate(k, own_places, KVH, 1.0).astype(jnp.bfloat16)
    key_all, value_all = (
        lax.all_gather(key_rot, "ctx", axis=0, tiled=True),
        lax.all_gather(v, "ctx", axis=0, tiled=True),
    )
    length = key_all.shape[0]
    query_groups = to_groups(query_rot, rows)
    key_groups = key_all.reshape(length, KVH, HD).transpose(1, 0, 2)
    value_groups = value_all.reshape(length, KVH, HD).transpose(1, 0, 2)

    def group_fwd(inputs):
        query_one, key_one, value_one = inputs
        scores = dot_last(query_one, key_one) * scale
        masked = jnp.where(visible, scores, -1e30)
        top = jnp.max(masked, -1, keepdims=True)
        expo = jnp.exp(masked - top)
        total = jnp.sum(expo, -1, keepdims=True)
        probs = (expo / total).astype(jnp.bfloat16)
        mixed = jnp.dot(probs, value_one, preferred_element_type=jnp.float32)
        return (mixed.astype(jnp.bfloat16), (top + jnp.log(total))[:, 0])

    mixed_groups, log_sums = lax.map(group_fwd, (query_groups, key_groups, value_groups))
    head_out = from_groups(mixed_groups, rows)
    resid = x + jnp.dot(head_out, w_o, preferred_element_type=jnp.float32)
    scale_two = lax.rsqrt(jnp.mean(resid * resid, -1, keepdims=True) + EPS)
    b = (resid * scale_two * gain_two.astype(jnp.float32)).astype(jnp.bfloat16)
    gate_pre = jnp.dot(b, w_g, preferred_element_type=jnp.float32)
    up_pre = jnp.dot(b, w_u, preferred_element_type=jnp.float32)
    sig_gate = jax.nn.sigmoid(gate_pre)
    silu_gate = gate_pre * sig_gate
    hidden = (silu_gate * up_pre).astype(jnp.bfloat16)
    result = (resid + jnp.dot(hidden, w_d, preferred_element_type=jnp.float32)).astype(jnp.bfloat16)
    backward_set = (
        lax.all_gather(norm1_gain, "fsdp", axis=0, tiled=True),
        lax.all_gather(w_query, "fsdp", axis=0, tiled=True),
        lax.all_gather(w_key, "fsdp", axis=0, tiled=True),
        lax.all_gather(w_value, "fsdp", axis=0, tiled=True),
        lax.all_gather(w_out, "fsdp", axis=0, tiled=True),
        lax.all_gather(norm2_gain, "fsdp", axis=0, tiled=True),
        lax.all_gather(w_gate, "fsdp", axis=0, tiled=True),
        lax.all_gather(w_up, "fsdp", axis=0, tiled=True),
        lax.all_gather(w_down, "fsdp", axis=0, tiled=True),
    )
    gain_one_b, w_q_b, w_k_b, w_v_b, w_o_b, gain_two_b, w_g_b, w_u_b, w_d_b = backward_set
    dy = cotangent[0].astype(jnp.float32)
    dy_low = dy.astype(jnp.bfloat16)
    grad_d = dot_first(hidden, dy_low)
    dhidden = dot_last(dy_low, w_d_b)
    dgate = (dhidden * up_pre * sig_gate * (1.0 + gate_pre * (1.0 - sig_gate))).astype(jnp.bfloat16)
    dup_low = (dhidden * silu_gate).astype(jnp.bfloat16)
    grad_g = dot_first(b, dgate)
    grad_u = dot_first(b, dup_low)
    grad_b = dot_last(dgate, w_g_b) + dot_last(dup_low, w_u_b)
    grad_gain_two, norm_part = norm_back(resid, scale_two, gain_two_b, grad_b)
    grad_resid = dy + norm_part
    resid_low = grad_resid.astype(jnp.bfloat16)
    grad_o = dot_first(head_out, resid_low)
    dheads = dot_last(resid_low, w_o_b).astype(jnp.bfloat16)
    dhead_groups = to_groups(dheads, rows)

    def group_bwd(inputs):
        query_one, key_one, value_one, dout_one, lse_one = inputs
        scores = dot_last(query_one, key_one) * scale
        probs = jnp.exp(jnp.where(visible, scores, -1e30) - lse_one[:, None])
        probs_low = probs.astype(jnp.bfloat16)
        dprobs = dot_last(dout_one, value_one)
        inner = jnp.sum(probs * dprobs, -1, keepdims=True)
        dscores = (probs * (dprobs - inner)).astype(jnp.bfloat16)
        dquery = jnp.dot(dscores, key_one, preferred_element_type=jnp.float32) * scale
        dkey = dot_first(dscores, query_one) * scale
        dvalue = dot_first(probs_low, dout_one)
        return (dquery, dkey, dvalue)

    dquery_groups, dkey_groups, dvalue_groups = lax.map(
        group_bwd, (query_groups, key_groups, value_groups, dhead_groups, log_sums)
    )
    dquery_rot = from_groups(dquery_groups, rows)
    dkey_all = dkey_groups.transpose(1, 0, 2).reshape(length, KVH * HD)
    dvalue_all = dvalue_groups.transpose(1, 0, 2).reshape(length, KVH * HD)
    own_kv = lax.psum_scatter(
        jnp.concatenate([dkey_all, dvalue_all], 1).astype(jnp.bfloat16),
        "ctx",
        scatter_dimension=0,
        tiled=True,
    ).astype(jnp.float32)
    dq = rotate(dquery_rot, own_places, H, -1.0).astype(jnp.bfloat16)
    dk = rotate(own_kv[:, : KVH * HD], own_places, KVH, -1.0).astype(jnp.bfloat16)
    dv_low = own_kv[:, KVH * HD :].astype(jnp.bfloat16)
    grad_q = dot_first(a, dq)
    grad_k = dot_first(a, dk)
    grad_v = dot_first(a, dv_low)
    grad_a = dot_last(dq, w_q_b) + dot_last(dk, w_k_b) + dot_last(dv_low, w_v_b)
    grad_gain_one, input_part = norm_back(x, scale_one, gain_one_b, grad_a)
    grad_x = (grad_resid + input_part).astype(jnp.bfloat16)
    grad_terms = (
        grad_gain_one,
        grad_q,
        grad_k,
        grad_v,
        grad_o,
        grad_gain_two,
        grad_g,
        grad_u,
        grad_d,
    )
    shares = (
        lax.psum_scatter(
            grad_terms[0].astype(jnp.bfloat16), "fsdp", scatter_dimension=0, tiled=True
        ).astype(jnp.float32),
        lax.psum_scatter(
            grad_terms[1].astype(jnp.bfloat16), "fsdp", scatter_dimension=0, tiled=True
        ).astype(jnp.float32),
        lax.psum_scatter(
            grad_terms[2].astype(jnp.bfloat16), "fsdp", scatter_dimension=0, tiled=True
        ).astype(jnp.float32),
        lax.psum_scatter(
            grad_terms[3].astype(jnp.bfloat16), "fsdp", scatter_dimension=0, tiled=True
        ).astype(jnp.float32),
        lax.psum_scatter(
            grad_terms[4].astype(jnp.bfloat16), "fsdp", scatter_dimension=0, tiled=True
        ).astype(jnp.float32),
        lax.psum_scatter(
            grad_terms[5].astype(jnp.bfloat16), "fsdp", scatter_dimension=0, tiled=True
        ).astype(jnp.float32),
        lax.psum_scatter(
            grad_terms[6].astype(jnp.bfloat16), "fsdp", scatter_dimension=0, tiled=True
        ).astype(jnp.float32),
        lax.psum_scatter(
            grad_terms[7].astype(jnp.bfloat16), "fsdp", scatter_dimension=0, tiled=True
        ).astype(jnp.float32),
        lax.psum_scatter(
            grad_terms[8].astype(jnp.bfloat16), "fsdp", scatter_dimension=0, tiled=True
        ).astype(jnp.float32),
    )
    summed = (
        lax.psum(shares[0].astype(jnp.bfloat16), "ctx").astype(jnp.float32),
        lax.psum(shares[1].astype(jnp.bfloat16), "ctx").astype(jnp.float32),
        lax.psum(shares[2].astype(jnp.bfloat16), "ctx").astype(jnp.float32),
        lax.psum(shares[3].astype(jnp.bfloat16), "ctx").astype(jnp.float32),
        lax.psum(shares[4].astype(jnp.bfloat16), "ctx").astype(jnp.float32),
        lax.psum(shares[5].astype(jnp.bfloat16), "ctx").astype(jnp.float32),
        lax.psum(shares[6].astype(jnp.bfloat16), "ctx").astype(jnp.float32),
        lax.psum(shares[7].astype(jnp.bfloat16), "ctx").astype(jnp.float32),
        lax.psum(shares[8].astype(jnp.bfloat16), "ctx").astype(jnp.float32),
    )
    return (
        result[None],
        grad_x[None],
        summed[0],
        summed[1],
        summed[2],
        summed[3],
        summed[4],
        summed[5],
        summed[6],
        summed[7],
        summed[8],
    )


RATIO = H // KVH
PAIR = 2 * RATIO * HD
WIDE = 2 * HD
NT = (((1,), (1,)), ((), ()))
TN = (((0,), (0,)), ((), ()))
NN = (((1,), (0,)), ((), ()))
VMEM = pl.BlockSpec(memory_space=pltpu.VMEM)
HBM = pl.BlockSpec(memory_space=pl.ANY)
ROOM = pltpu.CompilerParams(vmem_limit_bytes=60 * 2**20)


def mm(left, right, dims):
    return lax.dot_general(left, right, dims, preferred_element_type=jnp.float32)


def cost(flops, nbytes, exps=0):
    return pl.CostEstimate(flops=int(flops), bytes_accessed=int(nbytes), transcendentals=int(exps))


def turn(values, cosine, sine):
    lane = lax.broadcasted_iota(jnp.int32, values.shape, 1)
    first = lax.rem(lane, HD) < HD // 2
    partner = jnp.where(first, pltpu.roll(values, WIDE - HD // 2, 1), pltpu.roll(values, HD // 2, 1))
    return values * cosine + partner * sine


def far_lines(z):
    return (z ^ 1, z ^ 2, z ^ 3)


def qkv_kernel(
    at_ref, x_ref, cos_ref, sin_ref, w0_ref, w1_ref, own0_ref, own1_ref, a_ref, at_out_ref, q_ref, kv_ref, gain_ref, w_ref, sem
):
    t, core, z = at_ref[0], at_ref[1], at_ref[2]
    parts, lines, cut, width = w0_ref.shape
    copies = []
    for n, (w, own) in enumerate(((w0_ref, own0_ref), (w1_ref, own1_ref))):
        other = core if n == 0 else 1 - core
        row = pl.multiple_of((2 * z + other) * cut, 16)
        copies.append((own.at[:, pl.ds(0, parts * width)], w_ref.at[pl.ds(row, cut), :]))
        for k, far in enumerate(far_lines(z)):
            row = pl.multiple_of((2 * far + other) * cut, 16)
            for r in range(parts):
                column = pl.multiple_of((t ^ r) * width, WIDE)
                copies.append((w.at[r, k], w_ref.at[pl.ds(row, cut), pl.ds(column, width)]))
    copies = [pltpu.make_async_copy(src, dst, sem.at[i]) for i, (src, dst) in enumerate(copies)]
    for c in copies:
        c.start()
    x = x_ref[...].astype(jnp.float32)
    inv = lax.rsqrt(jnp.mean(x * x, -1, keepdims=True) + EPS)
    for c in copies:
        c.wait()
    first, half = H * HD, KVH * HD
    gains = jnp.transpose(w_ref[:, first + 2 * half : first + 2 * half + WIDE].astype(jnp.float32))[0:8]
    gain_ref[...] = gains
    a = (x * inv * gains[0:1]).astype(jnp.bfloat16)
    a_ref[...] = a
    at_out_ref[...] = jnp.transpose(a)
    for at in range(0, first + 2 * half, 2 * WIDE):
        both = mm(a_ref[...], w_ref[:, at : at + 2 * WIDE], NN)
        for n in range(0, 2 * WIDE, WIDE):
            part, column = both[:, n : n + WIDE], at + n
            if column < first + half:
                part = turn(part, cos_ref[...], sin_ref[...])
            if column < first:
                q_ref[:, column : column + WIDE] = part.astype(jnp.bfloat16)
            elif column < first + 2 * half:
                kv_ref[:, column - first : column - first + WIDE] = part.astype(jnp.bfloat16)


def qkv_project(where, x, cosine, sine, w, own):
    rows, model = x.shape
    width = 4 * w[0].shape[3]
    low = jnp.bfloat16
    return pl.pallas_call(
        qkv_kernel,
        in_specs=[pl.BlockSpec(memory_space=pltpu.SMEM)] + [VMEM] * 3 + [HBM] * 4,
        out_specs=[VMEM] * 6,
        out_shape=[
            jax.ShapeDtypeStruct((rows, model), low),
            jax.ShapeDtypeStruct((model, rows), low),
            jax.ShapeDtypeStruct((rows, H * HD), low),
            jax.ShapeDtypeStruct((rows, 2 * KVH * HD), low),
            jax.ShapeDtypeStruct((8, model), jnp.float32),
            jax.ShapeDtypeStruct((model, width), low),
        ],
        scratch_shapes=[pltpu.SemaphoreType.DMA((2 + 2 * 3 * w[0].shape[0],))],
        compiler_params=ROOM,
        cost_estimate=cost(2 * rows * model * width, 2 * (4 * rows * model + 2 * model * width)),
        name="qkv_project",
    )(where, x, cosine, sine, w[0], w[1], own[0], own[1])


def pick_heads(ref, row, group, factor):
    own = lax.broadcasted_iota(jnp.int32, (BLK, WIDE), 1) // HD == group
    out = []
    for n in range(group * RATIO, (group + 1) * RATIO):
        piece = ref[pl.ds(row, BLK), pl.ds(n // 2 * WIDE, WIDE)].astype(jnp.float32) * factor
        if n % 2 != group:
            piece = pltpu.roll(piece, HD, 1)
        out.append(jnp.where(own, piece, 0.0).astype(jnp.bfloat16))
    return jnp.concatenate(out, 0)


def join_heads(groups):
    lane = lax.broadcasted_iota(jnp.int32, (BLK, WIDE), 1)
    parts = []
    for n in range(2 * RATIO):
        group, i = divmod(n, RATIO)
        piece = groups[group][i * BLK : (i + 1) * BLK, :]
        parts.append(piece if n % 2 == group else pltpu.roll(piece, HD, 1))
    return [jnp.where(lane < HD, parts[2 * b], parts[2 * b + 1]) for b in range(RATIO)]


def steps_of(pairs, most):
    return max(u for u in range(1, most + 1) if pairs % u == 0)


def attend_kernel(own_ref, slot_ref, q_ref, k_ref, v_ref, o_ref, lse_ref, s_scr, v_scr, q_scr, m_scr, a_scr):
    rows = RATIO * BLK
    length = v_ref.shape[0]
    pairs = length // BLK + 1
    lane = lax.broadcasted_iota(jnp.int32, (length, WIDE), 1)
    first = own_ref[0] + 1

    def place(t):
        j = jnp.where(t >= first, 1, 0)
        return j, pl.multiple_of(slot_ref[t - j * first] * BLK, BLK)

    outs = [[], []]
    for group in range(2):
        v_scr[...] = jnp.where(lane // HD == group, v_ref[...].astype(jnp.float32), 1.0).astype(jnp.bfloat16)
        for j in range(2):
            q_scr[j] = pick_heads(q_ref, j * BLK, group, HD**-0.5)
        m_scr[...] = jnp.full(m_scr.shape, -jnp.inf, jnp.float32)
        a_scr[...] = jnp.zeros(a_scr.shape, jnp.float32)

        def scores(t, carry):
            j, at = place(t)
            s = mm(q_scr[j], k_ref[pl.ds(at, BLK), :], NT)
            s_scr[t] = s
            m_scr[j] = jnp.maximum(m_scr[j], jnp.maximum(s[:, 0:WIDE], s[:, WIDE : 2 * WIDE]))
            return carry

        lax.fori_loop(0, pairs, scores, 0, unroll=steps_of(pairs, 9))
        for j in range(2):
            m_scr[j] = jnp.broadcast_to(jnp.max(m_scr[j], 1, keepdims=True), (rows, WIDE))

        def mix(t, carry):
            j, at = place(t)
            top = m_scr[j]
            p = jnp.exp(s_scr[t] - jnp.concatenate([top, top], 1)).astype(jnp.bfloat16)
            a_scr[j] += mm(p, v_scr[pl.ds(at, BLK), :], NN)
            return carry

        lax.fori_loop(0, pairs, mix, 0, unroll=steps_of(pairs, 9))
        own = lax.broadcasted_iota(jnp.int32, (rows, WIDE), 1) // HD == group
        for j in range(2):
            acc = a_scr[j]
            total = jnp.where(own, pltpu.roll(acc, HD, 1), acc)
            outs[j].append(acc / total)
            lse_ref[group, j] = jnp.transpose(m_scr[j] + jnp.log(total))[0:1]
    for j in range(2):
        for b, part in enumerate(join_heads(outs[j])):
            o_ref[pl.ds(j * BLK, BLK), pl.ds(b * WIDE, WIDE)] = part.astype(jnp.bfloat16)


def attend(own, slots, q, kv, start, count):
    rows, length = q.shape[0], kv.shape[0]
    nblk = length // BLK
    work = rows * length * H * (nblk + 1) // (2 * nblk) * count // (KVH // 2)
    return pl.pallas_call(
        attend_kernel,
        grid_spec=pltpu.PrefetchScalarGridSpec(
            num_scalar_prefetch=2,
            grid=(count,),
            in_specs=[
                pl.BlockSpec((rows, PAIR), lambda p, *_: (0, p + start)),
                pl.BlockSpec((length, WIDE), lambda p, *_: (0, p + start)),
                pl.BlockSpec((length, WIDE), lambda p, *_: (0, p + start + KVH // 2)),
            ],
            out_specs=[
                pl.BlockSpec((rows, PAIR), lambda p, *_: (0, p)),
                pl.BlockSpec((2, 2, 1, RATIO * BLK), lambda p, *_: (p, 0, 0, 0)),
            ],
            scratch_shapes=[
                pltpu.VMEM((nblk + 1, RATIO * BLK, BLK), jnp.float32),
                pltpu.VMEM((length, WIDE), jnp.bfloat16),
                pltpu.VMEM((2, RATIO * BLK, WIDE), jnp.bfloat16),
                pltpu.VMEM((2, RATIO * BLK, WIDE), jnp.float32),
                pltpu.VMEM((2, RATIO * BLK, WIDE), jnp.float32),
            ],
        ),
        out_shape=[
            jax.ShapeDtypeStruct((rows, PAIR * count), jnp.bfloat16),
            jax.ShapeDtypeStruct((2 * count, 2, 1, RATIO * BLK), jnp.float32),
        ],
        compiler_params=ROOM,
        cost_estimate=cost(4 * 8 * work * HD, 4 * rows * PAIR * count + 4 * length * WIDE * count, work),
        name="attend",
    )(own, slots, q, kv, kv)


def attend_back_kernel(
    own_ref, slot_ref, where_ref, q_ref, k_ref, v_ref, do_ref, o_ref, lse_ref, cos_ref, sin_ref, *refs
):
    dq_ref, dkv_ref, dk_scr, dv_scr, q_scr, do_scr, st_scr, a_scr = refs[-8:]
    rows = RATIO * BLK
    length = v_ref.shape[0]
    pairs = length // BLK + 1
    dk_scr[...] = jnp.zeros_like(dk_scr)
    dv_scr[...] = jnp.zeros_like(dv_scr)
    first = own_ref[0] + 1
    outs = [[], []]
    for group in range(2):
        for j in range(2):
            q_scr[j] = pick_heads(q_ref, j * BLK, group, HD**-0.5)
            grads = pick_heads(do_ref, j * BLK, group, 1.0)
            do_scr[j] = grads
            mixed = pick_heads(o_ref, j * BLK, group, 1.0)
            inner = jnp.sum(grads.astype(jnp.float32) * mixed.astype(jnp.float32), 1, keepdims=True)
            st_scr[j, 0:1] = jnp.transpose(jnp.broadcast_to(inner, (rows, WIDE)))[0:1]
            st_scr[j, 1:2] = lse_ref[group, j]
        a_scr[...] = jnp.zeros_like(a_scr)

        def step(t, carry):
            j = jnp.where(t >= first, 1, 0)
            at = pl.multiple_of(slot_ref[t - j * first] * BLK, BLK)
            keys = k_ref[pl.ds(at, BLK), :]
            qs, grads = q_scr[j], do_scr[j]
            p = jnp.exp(mm(keys, qs, NT) - st_scr[j, 1:2])
            dp = mm(v_ref[pl.ds(at, BLK), :], grads, NT)
            ds = (p * (dp - st_scr[j, 0:1])).astype(jnp.bfloat16)
            dv_scr[pl.ds(at, BLK), :] += mm(p.astype(jnp.bfloat16), grads, NN)
            dk_scr[pl.ds(at, BLK), :] += mm(ds, qs, NN)
            a_scr[j] += mm(ds, keys, TN)
            return carry

        lax.fori_loop(0, pairs, step, 0, unroll=steps_of(pairs, 3))
        for j in range(2):
            outs[j].append(a_scr[j] * HD**-0.5)
    for j in range(2):
        span = pl.ds(j * BLK, BLK)
        for b, part in enumerate(join_heads(outs[j])):
            dq_ref[span, pl.ds(b * WIDE, WIDE)] = turn(part, cos_ref[span, :], -sin_ref[span, :]).astype(jnp.bfloat16)
    own_rows = length // 4
    for n, (scr, order) in enumerate(((dk_scr, (1, 3, 0, 2)), (dv_scr, (2, 3, 0, 1)))):
        for i, r in enumerate(order):
            dkv_ref[n, i] = scr[pl.ds(r * own_rows, own_rows), :].astype(jnp.bfloat16)


def attend_back(own, slots, where, q, kv, grads, mixed, lse, cosine, sine, start, count, into=None):
    rows, length = q.shape[0], kv.shape[0]
    nblk = length // BLK
    work = rows * length * H * (nblk + 1) // (2 * nblk) * count // (KVH // 2)
    wide = pl.BlockSpec((rows, PAIR), lambda p, *_: (0, p))
    shifted = pl.BlockSpec((rows, PAIR), lambda p, *_: (0, p + start))
    whole = pl.BlockSpec((rows, WIDE), lambda p, *_: (0, 0))
    part = pl.BlockSpec((2, 4, length // 4, WIDE), lambda p, *_: (0, 0, 0, p + start))
    part_shape = jax.ShapeDtypeStruct((2, 4, length // 4, KVH * HD), jnp.bfloat16)
    more = [] if into is None else [into]
    return pl.pallas_call(
        attend_back_kernel,
        grid_spec=pltpu.PrefetchScalarGridSpec(
            num_scalar_prefetch=3,
            grid=(count,),
            in_specs=[
                shifted,
                pl.BlockSpec((length, WIDE), lambda p, *_: (0, p + start)),
                pl.BlockSpec((length, WIDE), lambda p, *_: (0, p + start + KVH // 2)),
                shifted,
                shifted,
                pl.BlockSpec((2, 2, 1, RATIO * BLK), lambda p, *_: (p + start, 0, 0, 0)),
                whole,
                whole,
            ]
            + [HBM] * len(more),
            out_specs=[wide, part],
            scratch_shapes=[
                pltpu.VMEM((length, WIDE), jnp.float32),
                pltpu.VMEM((length, WIDE), jnp.float32),
                pltpu.VMEM((2, RATIO * BLK, WIDE), jnp.bfloat16),
                pltpu.VMEM((2, RATIO * BLK, WIDE), jnp.bfloat16),
                pltpu.VMEM((2, 8, RATIO * BLK), jnp.float32),
                pltpu.VMEM((2, RATIO * BLK, WIDE), jnp.float32),
            ],
        ),
        out_shape=[jax.ShapeDtypeStruct((rows, PAIR * count), jnp.bfloat16), part_shape],
        input_output_aliases={} if into is None else {11: 1},
        compiler_params=ROOM,
        cost_estimate=cost(1000, 1000) if into is None else cost(80 * work * HD, 8 * rows * PAIR * count + 8 * length * WIDE * count, work),
        name="attend_back",
    )(own, slots, where, q, kv, kv, grads, mixed, lse, cosine, sine, *more)


def middle_kernel(
    at_ref, ho_ref, x_ref, dy_ref, gain_ref,
    *refs,
):
    r = pl.program_id(0)
    count = pl.num_programs(0)
    t, core, z = at_ref[0], at_ref[1], at_ref[2]
    parts = 4
    sent, (d0_ref, d1_ref, all0_ref, all1_ref) = refs[: 2 * parts], refs[2 * parts : 2 * parts + 4]
    out_ref, low_ref, bt_ref, gd_ref, gs_ref, gk_ref, us_ref, uk_ref, dr_ref, dh_ref, gg_ref = refs[-24:-13]
    gu_scr, d_scr, wo_ref, r_scr, b_scr, acc_scr, db_scr, h_scr, dg_ref, du_ref, gu_sem, o_sem, d_sem = refs[-13:]
    lines, cut, columns_sent = sent[0].shape
    width = dg_ref.shape[1]
    model = wo_ref.shape[1]
    o_width = columns_sent - 2 * width
    o_parts = model // o_width
    first_g = all0_ref.shape[1] - model - 2 * parts * width
    alls = (all0_ref, all1_ref)
    cores = (core, 1 - core)
    others = far_lines(z)

    def piece(n, part, k):
        return sent[2 * part + n].at[k]

    def gu_copies(part, slot):
        out = []
        for n, other in enumerate(cores):
            rows = pl.ds(pl.multiple_of((2 * z + other) * cut, 16), cut)
            for m in range(2):
                column = pl.multiple_of(first_g + (m * parts + (t ^ part)) * width, WIDE)
                out.append((alls[n].at[:, pl.ds(column, width)], gu_scr.at[slot, m, rows, :]))
            for k in range(lines):
                rows = pl.ds(pl.multiple_of((2 * others[k] + other) * cut, 16), cut)
                for m in range(2):
                    out.append((piece(n, part, k).at[:, pl.ds(m * width, width)], gu_scr.at[slot, m, rows, :]))
        return [pltpu.make_async_copy(src, dst, gu_sem.at[slot, i]) for i, (src, dst) in enumerate(out)]

    def o_copies(part):
        out = []
        columns = pl.ds(pl.multiple_of((t ^ part) * o_width, WIDE), o_width)
        for n, other in enumerate(cores):
            for k in range(lines):
                rows = pl.ds(pl.multiple_of((2 * others[k] + other) * cut, 16), cut)
                out.append((piece(n, part, k).at[:, pl.ds(2 * width, o_width)], wo_ref.at[rows, columns]))
        return [pltpu.make_async_copy(src, dst, o_sem.at[part, i]) for i, (src, dst) in enumerate(out)]

    def own_copies():
        out = []
        for n, other in enumerate(cores):
            rows = pl.ds(pl.multiple_of((2 * z + other) * cut, 16), cut)
            out.append((alls[n].at[:, pl.ds(first_g + 2 * parts * width, model)], wo_ref.at[rows, :]))
        return [pltpu.make_async_copy(src, dst, o_sem.at[parts, i]) for i, (src, dst) in enumerate(out)]

    def d_copies():
        out = []
        cut_d = d0_ref.shape[1]
        for n, other in enumerate(cores):
            for line in range(lines + 1):
                row = pl.multiple_of((2 * line + other) * cut_d, 16)
                out.append(((d0_ref, d1_ref)[n].at[line], d_scr.at[pl.ds(row, cut_d), :]))
        return [pltpu.make_async_copy(src, dst, d_sem.at[i]) for i, (src, dst) in enumerate(out)]

    slot = lax.rem(r, 2)

    @pl.when(r == 0)
    def _():
        for part in range(parts):

            @pl.when((t ^ part) < o_parts)
            def _():
                for c in o_copies(part):
                    c.start()

        for c in own_copies():
            c.start()
        for c in gu_copies(0, 0) + d_copies():
            c.start()
        for part in range(parts):

            @pl.when((t ^ part) < o_parts)
            def _():
                for c in o_copies(part):
                    c.wait()

        for c in own_copies():
            c.wait()
        resid = x_ref[...].astype(jnp.float32) + mm(ho_ref[...], wo_ref[...], NN)
        r_scr[...] = resid
        inv = lax.rsqrt(jnp.mean(resid * resid, -1, keepdims=True) + EPS)
        b = (resid * inv * gain_ref[1:2]).astype(jnp.bfloat16)
        b_scr[...] = b
        turned = jnp.transpose(b)
        for shard in range(2 * (lines + 1)):
            rows = slice(shard * cut, (shard + 1) * cut)
            bt_ref[lax.rem(shard + core, 2), shard // 2 * cut : (shard // 2 + 1) * cut] = turned[rows]

    for part in range(parts):

        @pl.when(r == part)
        def _():
            for c in gu_copies(part, part % 2):
                c.wait()
            if part == 0:
                for c in d_copies():
                    c.wait()
            if part + 1 < parts:
                for c in gu_copies(part + 1, (part + 1) % 2):
                    c.start()

    down = pl.multiple_of((t ^ r) * width, 256)
    for at in range(0, width, 256):
        span = slice(at, at + 256)
        gate = mm(b_scr[...], gu_scr[slot, 0, :, span], NN)
        up = mm(b_scr[...], gu_scr[slot, 1, :, span], NN)
        dhid = mm(dy_ref[...], d_scr[pl.ds(down + at, 256), :], NT)
        sig = jax.nn.sigmoid(gate)
        silu = gate * sig
        hidden = (silu * up).astype(jnp.bfloat16)
        h_scr[:, span] = hidden
        dg_ref[:, span] = (dhid * up * sig * (1.0 + gate * (1.0 - sig))).astype(jnp.bfloat16)
        du_ref[:, span] = (dhid * silu).astype(jnp.bfloat16)
    for n, (g_ref, u_ref) in enumerate(((gk_ref, uk_ref), (gs_ref, uk_ref), (gk_ref, us_ref), (gs_ref, us_ref))):

        @pl.when(r == n)
        def _():
            g_ref[0] = dg_ref[...]
            u_ref[0] = du_ref[...]

    gd_ref[0] = mm(h_scr[...], dy_ref[...], TN).astype(jnp.bfloat16)
    for at in range(0, model, 1152):
        span = slice(at, at + 1152)
        acc = mm(h_scr[...], d_scr[pl.ds(down, width), span], NN)
        db = mm(dg_ref[...], gu_scr[slot, 0, span, :], NT) + mm(du_ref[...], gu_scr[slot, 1, span, :], NT)

        @pl.when(r == 0)
        def _():
            acc_scr[:, span] = acc
            db_scr[:, span] = db

        @pl.when(r > 0)
        def _():
            acc_scr[:, span] += acc
            db_scr[:, span] += db

    @pl.when(r == count - 1)
    def _():
        resid = r_scr[...]
        out_ref[...] = (resid + acc_scr[...]).astype(jnp.bfloat16)
        inv = lax.rsqrt(jnp.mean(resid * resid, -1, keepdims=True) + EPS)
        db = db_scr[...]
        gg_ref[...] = jnp.sum(db * resid * inv, 0, keepdims=True)
        weighted = gain_ref[1:2] * db
        dr = (
            dy_ref[...].astype(jnp.float32)
            + inv * weighted
            - resid * (inv * inv * inv) * jnp.mean(weighted * resid, -1, keepdims=True)
        )
        dr_ref[...] = dr
        low = dr.astype(jnp.bfloat16)
        low_ref[...] = low
        dh_ref[...] = mm(low, wo_ref[...], NT).astype(jnp.bfloat16)


def middle(where, ho, x, dy, gains, sent, d, own_all):
    rows, model = x.shape
    lines, cut = sent[0][0].shape[:2]
    count = len(sent)
    width = d[0].shape[0] * d[0].shape[1] * 2 // count
    once = pl.Buffered(1)
    whole = lambda shape: pl.BlockSpec(shape, lambda r, *_: (0,) * len(shape), pipeline_mode=once)
    act = lambda at: pl.BlockSpec((1, rows, width), lambda r, *_: (at(r), 0, 0))
    low = jnp.bfloat16
    return pl.pallas_call(
        middle_kernel,
        grid_spec=pltpu.PrefetchScalarGridSpec(
            num_scalar_prefetch=1,
            grid=(count,),
            in_specs=[whole((rows, H * HD)), whole((rows, model)), whole((rows, model)), whole((8, model))] + [HBM] * 12,
            out_specs=[
                whole((rows, model)), whole((rows, model)), whole((2, model // 2, rows)),
                pl.BlockSpec((1, width, model), lambda r, at_ref: (at_ref[0] ^ r, 0, 0)),
                act(lambda r: r // 3), act(lambda r: r // 2), act(lambda r: r // 3), act(lambda r: (r + 2) // 3),
                whole((rows, model)), whole((rows, H * HD)), whole((1, model)),
            ],
            scratch_shapes=[
                pltpu.VMEM((2, 2, 2 * (lines + 1) * cut, width), low),
                pltpu.VMEM((count * width, model), low),
                pltpu.VMEM((H * HD, model), low),
                pltpu.VMEM((rows, model), jnp.float32),
                pltpu.VMEM((rows, model), low),
                pltpu.VMEM((rows, model), jnp.float32),
                pltpu.VMEM((rows, model), jnp.float32),
                pltpu.VMEM((rows, width), low),
                pltpu.VMEM((rows, width), low),
                pltpu.VMEM((rows, width), low),
                pltpu.SemaphoreType.DMA((2, 4 * (lines + 1))),
                pltpu.SemaphoreType.DMA((count + 1, 2 * lines)),
                pltpu.SemaphoreType.DMA((2 * (lines + 1),)),
            ],
        ),
        out_shape=[
            jax.ShapeDtypeStruct((rows, model), low),
            jax.ShapeDtypeStruct((rows, model), low),
            jax.ShapeDtypeStruct((2, model // 2, rows), low),
            jax.ShapeDtypeStruct((count, width, model), low),
            *[jax.ShapeDtypeStruct((2, rows, width), low)] * 4,
            jax.ShapeDtypeStruct((rows, model), jnp.float32),
            jax.ShapeDtypeStruct((rows, H * HD), low),
            jax.ShapeDtypeStruct((1, model), jnp.float32),
        ],
        compiler_params=ROOM,
        cost_estimate=cost(12 * rows * model * width * count + 4 * rows * model * model, 2 * 16 * rows * model + 6 * count * width * model, rows * width * count),
        name="middle",
    )(where, ho, x, dy, gains, *[v for pair in sent for v in pair], *d, *own_all)


def act_kernel(counts, cos_ref, sin_ref, dkv_ref, gx_ref, lasty_ref, gy_ref, lastx_ref, *refs):
    act_ref = refs[-1]
    half = KVH * HD
    at = 0
    for dq_ref, count in zip(refs, counts):
        act_ref[:, at * PAIR : (at + count) * PAIR] = dq_ref[...]
        at += count
    for p in range(at):
        span = slice(p * WIDE, (p + 1) * WIDE)
        dk = sum(v.astype(jnp.float32) for v in (dkv_ref[0, 2, :, span], gx_ref[0, :, span], lasty_ref[:, span]))
        dv = sum(v.astype(jnp.float32) for v in (dkv_ref[1, 2, :, span], gy_ref[0, :, span], lastx_ref[:, span]))
        column = H * HD + p * WIDE
        act_ref[:, column : column + WIDE] = turn(dk, cos_ref[...], -sin_ref[...]).astype(jnp.bfloat16)
        act_ref[:, column + half : column + half + WIDE] = dv.astype(jnp.bfloat16)
    act_ref[:, H * HD + 2 * half :] = jnp.zeros((act_ref.shape[0], act_ref.shape[1] - H * HD - 2 * half), jnp.bfloat16)


def make_act(cosine, sine, shares, parts, counts, width):
    rows = cosine.shape[0]
    return pl.pallas_call(
        functools.partial(act_kernel, counts),
        in_specs=[VMEM] * (7 + len(parts)),
        out_specs=VMEM,
        out_shape=jax.ShapeDtypeStruct((rows, width), jnp.bfloat16),
        compiler_params=ROOM,
        cost_estimate=cost(10 * rows * width, 6 * rows * width),
        name="make_act",
    )(cosine, sine, *shares, *parts)


def last_kernel(x_ref, gain_ref, dr_ref, w_ref, act_ref, gx_ref, gg_ref):
    used = (H + 2 * KVH) * HD
    da = mm(act_ref[:, 0:used], w_ref[:, 0:used], NT)
    x = x_ref[...].astype(jnp.float32)
    inv = lax.rsqrt(jnp.mean(x * x, -1, keepdims=True) + EPS)
    gg_ref[...] = jnp.sum(da * x * inv, 0, keepdims=True)
    weighted = gain_ref[0:1] * da
    gx = dr_ref[...] + inv * weighted - x * (inv * inv * inv) * jnp.mean(weighted * x, -1, keepdims=True)
    gx_ref[...] = gx.astype(jnp.bfloat16)


def last(x, gains, dr, w_qkv, act):
    rows, model = x.shape
    return pl.pallas_call(
        last_kernel,
        in_specs=[VMEM] * 5,
        out_specs=[VMEM] * 2,
        out_shape=[jax.ShapeDtypeStruct((rows, model), jnp.bfloat16), jax.ShapeDtypeStruct((1, model), jnp.float32)],
        compiler_params=ROOM,
        cost_estimate=cost(2 * rows * model * (H + 2 * KVH) * HD, 10 * rows * model + 2 * model * (H + 2 * KVH) * HD),
        name="last",
    )(x, gains, dr, w_qkv, act)


def gu_products_kernel(l0_ref, l1_ref, g0_ref, g1_ref, u0_ref, u1_ref, g_ref, u_ref):
    @pl.when(pl.program_id(0) == 0)
    def _():
        g_ref[0] = (mm(l0_ref[...], g0_ref[0], NN) + mm(l1_ref[...], g1_ref[0], NN)).astype(jnp.bfloat16)

    @pl.when(pl.program_id(0) == 1)
    def _():
        u_ref[0] = (mm(l0_ref[...], u0_ref[0], NN) + mm(l1_ref[...], u1_ref[0], NN)).astype(jnp.bfloat16)


def gu_products(left, gates, ups):
    rows, tokens = left[0].shape
    width = gates[0].shape[2]
    cuts = 1
    piece = width // cuts
    spec = pl.BlockSpec((rows, tokens), lambda m, n, h: (0, 0))
    first = lambda m, v, end: v * (1 - m) + end * m
    then = lambda m, v: v * m

    def gate_at(m, n, h):
        return first(m, n, 1), first(m, h, cuts - 1)

    def up_at(m, n, h):
        return then(m, n), then(m, h)

    def gate_in(m, n, h):
        n, h = gate_at(m, n, h)
        return n, 0, h

    def up_in(m, n, h):
        n, h = up_at(m, n, h)
        return n, 0, h

    def gate_out(m, n, h):
        n, h = gate_at(m, n, h)
        return n, 0, h

    def up_out(m, n, h):
        n, h = up_at(m, n, h)
        return n, 0, h

    act = lambda index: pl.BlockSpec((1, tokens, piece), index)
    return pl.pallas_call(
        gu_products_kernel,
        grid=(2, 2, cuts),
        in_specs=[spec, spec, act(gate_in), act(gate_in), act(up_in), act(up_in)],
        out_specs=[pl.BlockSpec((1, rows, piece), gate_out), pl.BlockSpec((1, rows, piece), up_out)],
        out_shape=[jax.ShapeDtypeStruct((2, rows, width), jnp.bfloat16)] * 2,
        compiler_params=ROOM,
        cost_estimate=cost(16 * rows * tokens * width, 4 * rows * tokens + 8 * (2 * tokens + rows) * width),
        name="gu_products",
    )(left[0], left[1], gates[0], gates[1], ups[0], ups[1])


def qkv_products_kernel(where_ref, l0_ref, l1_ref, r0_ref, r1_ref, s0_ref, s1_ref, s2_ref, s3_ref):
    total = mm(l0_ref[...], r0_ref[...], NN) + mm(l1_ref[...], r1_ref[...], NN)
    for n, ref in enumerate((s0_ref, s1_ref, s2_ref, s3_ref)):

        @pl.when(pl.program_id(0) == n)
        def _():
            ref[...] = total.astype(jnp.bfloat16)


def qkv_products(where, left, acts):
    rows, tokens = left[0].shape
    width = acts[0].shape[1] // 4
    spec = pl.BlockSpec((rows, tokens), lambda r, *_: (0, 0))
    act = pl.BlockSpec((tokens, width), lambda r, w: (0, w[0] ^ r))
    out = pl.BlockSpec((rows, width), lambda r, *_: (0, 0))
    return pl.pallas_call(
        qkv_products_kernel,
        grid_spec=pltpu.PrefetchScalarGridSpec(
            num_scalar_prefetch=1,
            grid=(4,),
            in_specs=[spec, spec, act, act],
            out_specs=[out] * 4,
        ),
        out_shape=[jax.ShapeDtypeStruct((rows, width), jnp.bfloat16)] * 4,
        compiler_params=ROOM,
        cost_estimate=cost(16 * rows * tokens * width, 4 * rows * tokens + 8 * (2 * tokens + rows) * width),
        name="qkv_products",
    )(where, left[0], left[1], acts[0], acts[1])


def place_gu_kernel(where_ref, p0_ref, p1_ref, p2_ref, p3_ref, g_ref, u_ref):
    for r, ref in enumerate((p0_ref, p1_ref, p2_ref, p3_ref)):

        @pl.when(pl.program_id(0) == r)
        def _():
            g_ref[...] = ref[0].astype(jnp.float32)
            u_ref[...] = ref[1].astype(jnp.float32)


def place_gu(where, parts):
    _, rows, width = parts[0].shape
    out = pl.BlockSpec((rows, width), lambda r, w: (0, w[0] ^ r))
    return pl.pallas_call(
        place_gu_kernel,
        grid_spec=pltpu.PrefetchScalarGridSpec(
            num_scalar_prefetch=1,
            grid=(4,),
            in_specs=[pl.BlockSpec((2, rows, width), lambda r, *_: (0, 0, 0))] * 4,
            out_specs=[out, out],
        ),
        out_shape=[jax.ShapeDtypeStruct((rows, 4 * width), jnp.float32)] * 2,
        compiler_params=ROOM,
        cost_estimate=cost(1000, 1000),
        name="place_gu",
    )(where, *parts)


def place_qkv_kernel(in_ref, q_ref, k_ref, v_ref, g_ref):
    width = in_ref.shape[2] - WIDE
    spans = ((q_ref, 0, H * HD), (k_ref, H * HD, KVH * HD), (v_ref, (H + KVH) * HD, KVH * HD))
    gains = 0.0
    for n in range(in_ref.shape[0]):
        part = in_ref[n].astype(jnp.float32)
        gains += part[:, width:]
        for at in range(0, width, WIDE):
            column = n * width + at
            for ref, first, size in spans:
                if first <= column < first + size:
                    ref[:, column - first : column - first + WIDE] = part[:, at : at + WIDE]
    g_ref[...] = jnp.transpose(gains)[0:8]


def place_qkv(parts):
    rows = parts.shape[1]
    shape = lambda columns: jax.ShapeDtypeStruct((rows, columns), jnp.float32)
    return pl.pallas_call(
        place_qkv_kernel,
        in_specs=[VMEM],
        out_specs=[VMEM] * 4,
        out_shape=[shape(H * HD), shape(KVH * HD), shape(KVH * HD), jax.ShapeDtypeStruct((8, rows), jnp.float32)],
        cost_estimate=cost(parts.size, 6 * parts.size),
        name="place_qkv",
    )(parts)


def square(v, r):
    return lax.ppermute(v, "ctx", [(t, t ^ r) for t in range(4)])


def line(v, k):
    return lax.ppermute(v, "fsdp", [(f, f ^ (2 * k)) for f in range(8)])


def other_core(v):
    return lax.ppermute(v, "fsdp", [(f, f ^ 1) for f in range(8)])


def after(v, *others):
    return lax.optimization_barrier((v, *others))[0]


def wide(v):
    return v.astype(jnp.float32)


def low(v):
    return v.astype(jnp.bfloat16)


LINES = [[0, 2, 4, 6], [1, 3, 5, 7]]


def line_all(v):
    return lax.all_to_all(v, "fsdp", 0, 0, axis_index_groups=LINES, tiled=True)


def far_pieces(got, z):
    return [lax.dynamic_index_in_dim(got, z ^ k, 0, keepdims=False) for k in (1, 2, 3)]


def hold(parts, *events):
    return [after(v, *events) for v in parts]


def square_near(v):
    return [square(v, 1), square(v, 2)]


def square_far(from_x, from_y):
    half = from_x.shape[0] // 2
    return [square(from_y[:half], 1), square(from_x[half:], 2)]


def lanes(v, core):
    shaped = v.reshape(4, 2, v.shape[0] // 8, v.shape[1])
    pick = lambda c: lax.dynamic_index_in_dim(shaped, c, 1, keepdims=False).reshape(-1, v.shape[1])
    return pick(core), pick(1 - core)


def square_body(
    tokens,
    table,
    norm1_gain,
    w_query,
    w_key,
    w_value,
    w_out,
    norm2_gain,
    w_gate,
    w_up,
    w_down,
    cotangent,
):
    x, dy = tokens[0], cotangent[0]
    rows, model = x.shape
    t = lax.axis_index("ctx")
    f = lax.axis_index("fsdp")
    z, core = f // 2, f % 2
    where = jnp.stack([t, core, z]).astype(jnp.int32)
    cut, hidden_width = w_gate.shape
    cut_d = w_down.shape[0] // 4
    kv_width = 2 * KVH * HD

    relative = jnp.arange(4) ^ t
    offsets = jnp.arange(BLK, dtype=jnp.int32)
    ordered = table[relative].reshape(-1)
    own = ordered[:2].astype(jnp.int32)
    slots = jnp.zeros((ordered.shape[0],), jnp.int32).at[ordered].set(jnp.arange(ordered.shape[0], dtype=jnp.int32))
    places = (own[:, None] * BLK + offsets[None, :]).reshape(-1)
    frequency = 10000.0 ** (-(jnp.arange(HD // 2, dtype=jnp.float32) * 2.0 / HD))
    angles = places.astype(jnp.float32)[:, None] * frequency
    cosine = jnp.tile(jnp.cos(angles), (1, 4))
    sine = jnp.sin(angles)
    sine = jnp.concatenate([-sine, sine, -sine, sine], 1)

    slice_of = lambda w: lax.dynamic_slice_in_dim(w, t * (w.shape[1] // 4), w.shape[1] // 4, 1)
    filled = -(-(H * HD + kv_width + WIDE) // (8 * WIDE)) * 8 * WIDE
    gains_own = jnp.stack([norm1_gain, norm2_gain], 1)
    qkv_own = jnp.concatenate([w_query, w_key, w_value, gains_own], 1)
    qkv_own = jnp.pad(qkv_own, ((0, 0), (0, filled - qkv_own.shape[1])))
    o_whole = jnp.pad(w_out, ((0, 0), (0, 2 * (hidden_width // 4) - model)))
    guo_part = jnp.concatenate([slice_of(w_gate), slice_of(w_up), slice_of(o_whole)], 1)
    swap = lambda w: (w, other_core(w))
    qkv_slice = slice_of(qkv_own)
    qkv_line = [line(qkv_slice, k) for k in (1, 2, 3)]
    own_all = swap(jnp.concatenate([qkv_own, w_gate, w_up, w_out], 1))
    spread = lambda v: jnp.broadcast_to(v[None], (4, *v.shape))
    d_spread, guo_spread = hold([spread(w_down), spread(guo_part)])
    qkv_line = hold(qkv_line, cosine, sine, slots, d_spread, guo_spread)
    qkv_rows = jnp.concatenate(qkv_line)
    guo_line = line_all(after(guo_spread, *qkv_line))
    qkv_parts = [qkv_rows] + [square(qkv_rows, r) for r in (1, 2, 3)]
    qkv_all = after(jnp.stack(qkv_parts).reshape(4, 3, cut, -1), own_all[1])
    qkv_both = swap(qkv_all)

    a, a_t, q, kv_own, gains, w_qkv = qkv_project(where, x, cosine, sine, qkv_both, own_all)
    kv_near = square_near(kv_own)
    guo_line = after(guo_line, kv_own)
    d_line = line_all(after(d_spread, guo_line))
    kv_far = square_far(*kv_near)
    guo_rows = after(jnp.concatenate(far_pieces(after(guo_line, *kv_near), z)), *kv_far)
    guo_near = square_near(guo_rows)
    guo_own = other_core(guo_rows.reshape(3, cut, -1))
    kv = jnp.concatenate([kv_own, *kv_near, *kv_far])
    mixed, lse = attend(own, slots, after(q, guo_rows), kv, 0, KVH // 2)
    guo_near = hold(guo_near, mixed)
    half = guo_rows.shape[0] // 2
    guo_far = [square(guo_near[1][:half], 1), square(guo_near[0][half:], 2)]
    d = swap(after(d_line, *guo_far))
    shaped = lambda v: v.reshape(3, cut, -1)
    guo = [(shaped(guo_rows), after(guo_own, mixed))] + [swap(shaped(v)) for v in guo_near]
    guo.append(swap(shaped(after(jnp.concatenate(guo_far), *[v[1] for v in guo]))))
    out, dr_low, b_t, grad_d, g_s, g_k, u_s, u_k, dr, dheads, gg2 = middle(
        where, mixed, x, dy, gains, guo, d, own_all
    )

    left = (b_t[0], other_core(b_t[1]))
    g_s, u_s = swap(g_s), swap(u_s)
    grad_o = low(mm(mixed, dr_low, TN))
    g_send, u_send = gu_products(left, (after(g_s[0], grad_o), g_s[1]), u_s)
    got_x, got_y = square(g_send, 1), square(u_send, 2)
    scatter = lambda v: lax.psum_scatter(v, "fsdp", scatter_dimension=0, tiled=True)
    grad_d, grad_o = scatter(grad_d.reshape(-1, model)), scatter(grad_o)
    kept = [(after(v[0], g_send), v[1]) for v in (swap(g_k), swap(u_k))]
    g_keep, u_keep = gu_products(left, *kept)

    dq_1, dkv = attend_back(own, slots, where, after(q, g_keep), kv, dheads, mixed, lse, cosine, sine, 1, 2)
    got_x, got_y = hold((got_x, got_y), dq_1)
    pass_y = low(wide(g_keep[1]) + wide(got_x[1]))
    pass_x = low(wide(u_keep[1]) + wide(got_y[1]))
    last_y, last_x = square(pass_y, 2), square(pass_x, 1)
    dq_0, dkv = attend_back(
        own, slots, where, after(q, pass_x, pass_y), kv, dheads, mixed, lse, cosine, sine, 0, 1, dkv
    )
    last_y, last_x = hold([last_y, last_x], dq_0)
    dkv = after(dkv, last_y, last_x)
    kv_x, kv_y = square(dkv[0, :2], 1), square(dkv[1, :2], 2)
    rows_at = lambda v, at: v[at * cut : (at + 1) * cut]

    def gu_share(at):
        g = sum(wide(rows_at(v, at)) for v in (g_keep[0], got_x[0], last_y))
        u = sum(wide(rows_at(v, at)) for v in (u_keep[0], got_y[0], last_x))
        return jnp.stack([g, u])

    gu_sends = jnp.stack([low(gu_share(at)) for at in range(4)])
    gu_got = line_all(gu_sends)
    kv_x, kv_y = hold([kv_x, kv_y], gu_sends)
    kv_last_y = square(low(wide(dkv[0, 3]) + wide(kv_x[1])), 2)
    kv_last_x = square(low(wide(dkv[1, 3]) + wide(kv_y[1])), 1)
    grad_do = jnp.concatenate([grad_d, grad_o])
    half = grad_do.shape[0] // 32 * 16
    do_upper, do_lower = hold([grad_do[:half], grad_do[half:]], kv_x, kv_y)
    do_got = [square(do_upper, 1), square(do_lower, 2)]
    a_mine, a_other = lanes(a_t, core)
    a_both = (a_mine, other_core(a_other))
    act = make_act(after(cosine, do_upper, do_lower, *a_both), sine, [dkv, kv_x, kv_last_y, kv_y, kv_last_x], [dq_0, dq_1], (1, 2), filled)
    acts = swap(act)

    qkv_keep, *qkv_sends = qkv_products(where, a_both, acts)
    shares = [qkv_keep] + [square(v, r) for r, v in zip((1, 2, 3), qkv_sends)]
    grad_x, gg1 = last(after(x, qkv_keep), gains, dr, w_qkv, act)
    shares = hold(shares, gg1)
    gain_rows = jnp.concatenate([gg1, gg2])
    gain_rows += other_core(gain_rows)
    gain_rows = lax.dynamic_index_in_dim(gain_rows.reshape(2, 4, 2, cut), core, 2, keepdims=False)
    gain_columns = jnp.pad(low(gain_rows.transpose(1, 2, 0)), ((0, 0), (0, 0), (0, WIDE - 2)))
    qkv_share = lambda at: sum(wide(rows_at(v, at)) for v in shares)
    qkv_sends = jnp.stack([low(qkv_share(at)) for at in range(4)])
    qkv_sends = jnp.concatenate([qkv_sends, gain_columns], 2)
    gu_got = after(gu_got, gg1)
    qkv_got = line_all(after(qkv_sends, gu_got))
    do_got = hold(do_got, gg1)
    do_upper, do_lower = low(wide(do_upper) + wide(do_got[0])), low(wide(do_lower) + wide(do_got[1]))
    do_got = [square(after(do_upper, qkv_sends), 2), square(after(do_lower, qkv_sends), 1)]
    s_gu = low(sum(wide(gu_got[n]) for n in range(4)))
    all_gu = [s_gu] + [square(after(s_gu, qkv_sends), r) for r in (1, 2, 3)]
    s_qkv = low(sum(wide(qkv_got[n]) for n in range(4)))
    all_qkv = lax.all_to_all(jnp.broadcast_to(s_qkv[None], (4, *s_qkv.shape)), "ctx", 0, 0, tiled=True)
    do_got, all_gu = hold(do_got, s_qkv), hold(all_gu, s_qkv)
    do_upper, do_lower = wide(do_upper) + wide(do_got[0]), wide(do_lower) + wide(do_got[1])
    below = 4 * cut_d - half
    grad_g, grad_u = place_gu(where, all_gu)
    grad_q, grad_k, grad_v, gain_rows = place_qkv(all_qkv)
    return (
        out[None],
        grad_x[None],
        gain_rows[0],
        grad_q,
        grad_k,
        grad_v,
        do_lower[below:],
        gain_rows[1],
        grad_g,
        grad_u,
        jnp.concatenate([do_upper, do_lower[:below]]),
    )


def solution(mesh):
    placed = (
        P("fsdp", "ctx", None),
        P(),
        P("fsdp"),
        P("fsdp", None),
        P("fsdp", None),
        P("fsdp", None),
        P("fsdp", None),
        P("fsdp"),
        P("fsdp", None),
        P("fsdp", None),
        P("fsdp", None),
        P("fsdp", "ctx", None),
    )
    square = mesh.shape["ctx"] == 4 and mesh.shape["fsdp"] == 8
    return jax.shard_map(
        square_body if square else plain_body,
        mesh=mesh,
        in_specs=placed,
        out_specs=(
            P("fsdp", "ctx", None),
            P("fsdp", "ctx", None),
            P("fsdp"),
            P("fsdp", None),
            P("fsdp", None),
            P("fsdp", None),
            P("fsdp", None),
            P("fsdp"),
            P("fsdp", None),
            P("fsdp", None),
            P("fsdp", None),
        ),
        check_vma=False,
    )
```
